128 devices in a mesh: phase: 8 (over x, core), tp: 16 (over z, y).
Axes of the slice: x: 4, y: 4, z: 4, core: 2. Of those that a mesh axis runs over, the one named last changes fastest.
Arguments:
- teacher_rows: bfloat16 [512, 16384], P(None, ('phase', 'tp')), may hold values from -128 to 128
- teacher_gain: bfloat16 [16384], P(('phase', 'tp')), may hold values from 0.25 to 1.75
- teacher_head: bfloat16 [16384, 65536], P(None, ('phase', 'tp')), may hold values from -1 to 1
- student_rows: bfloat16 [512, 4096], P('phase', 'tp'), may hold values from -128 to 128
- student_gain: bfloat16 [4096], P('tp'), may hold values from 0.25 to 1.75
- student_head: bfloat16 [4096, 65536], P(None, ('phase', 'tp')), may hold values from -1 to 1
- labels: int32 [512], replicated, may hold values from 0 to 65535
Outputs:
- token_loss: float32 [512], P('phase')
- student_head_grad: bfloat16 [4096, 65536], P(None, ('phase', 'tp'))
- student_rows_grad: bfloat16 [512, 4096], P('phase', 'tp')
- student_gain_grad: float32 [4096], P('tp')
The draws below stay inside these ranges and needn't reach their ends.
All inputs are finite; a program needn't handle non-finite values.
Results may differ from the reference program's by a relative error of at most 0.011.
Values may be sent and summed in bfloat16 or wider, within the bound.
A program may use at most 128 MiB of HBM per device.

```python
import math
import jax
import jax.numpy as jnp
import numpy as np
from jax import lax

DT = 16384
DS = 4096
VOCAB = 65536
TOKENS = 512


def shared_field(key, salt, height, breadth):
    folded = jax.random.fold_in(key, salt)
    normal_key = jax.random.fold_in(folded, 0)
    gauss = jnp.clip(jax.random.normal(normal_key, (height, breadth), jnp.float32), -6.0, 6.0)
    return gauss


def shaped_rows(shared, key, height, breadth, ramp, spread):
    column = jnp.arange(breadth, dtype=jnp.float32) / breadth
    ramped = jnp.exp(0.5 * ramp * column)
    scales = jnp.exp(jax.random.uniform(key, (height, 1), jnp.float32, 0.0, spread))
    return shared * ramped[None, :] * scales


def spread_head(key, breadth, vocab):
    scale_key, value_key = jax.random.split(key)
    column_scale = jnp.exp(jax.random.uniform(scale_key, (1, vocab), jnp.float32, 0.0, math.log(10.0)))
    values = jnp.clip(jax.random.normal(value_key, (breadth, vocab), jnp.float32), -6.0, 6.0)
    return values * column_scale / math.sqrt(breadth)


def draw_teacher_rows(key, part):
    shared = shared_field(key, 11, TOKENS, DT)
    ramp = math.log(3.0)
    spread = math.log(10.0)
    key = jax.random.fold_in(key, 1)
    return shaped_rows(shared, key, TOKENS, DT, ramp, spread).astype(jnp.bfloat16)


def draw_teacher_head(key, part):
    key = jax.random.fold_in(key, 2)
    head_key = jax.random.fold_in(key, 0)
    head = spread_head(head_key, DT, VOCAB)
    return head.astype(jnp.bfloat16)


def draw_student_rows(key, part):
    shared = shared_field(key, 12, TOKENS, DS)
    ramp = math.log(3.0)
    spread = math.log(10.0)
    key = jax.random.fold_in(key, 3)
    return shaped_rows(shared, key, TOKENS, DS, ramp, spread).astype(jnp.bfloat16)


def draw_student_head(key, part):
    key = jax.random.fold_in(key, 4)
    head_key = jax.random.fold_in(key, 0)
    head = spread_head(head_key, DS, VOCAB)
    return head.astype(jnp.bfloat16)


def with_ends(array, key, least, top_value):
    index_at = [jax.random.randint(jax.random.fold_in(key, axis), (), 0, length) for axis, length in enumerate(array.shape)]
    main_axis = array.shape.index(max(array.shape))
    neighbour = index_at[:main_axis] + [(index_at[main_axis] + 1) % array.shape[main_axis]] + index_at[main_axis + 1:]
    return array.at[tuple(index_at)].set(least).at[tuple(neighbour)].set(top_value)


def rank_bounds(count, slope):
    portions = [(1 << 20) // math.isqrt(standing ** slope) + 1 for standing in range(1, count + 1)]
    width = 1 + sum(portions) // (1 << 30)
    return np.cumsum(np.array([max(1, weight // width) for weight in portions]))


def ranked(rng, extent, number_of, slope):
    grid = rank_bounds(number_of, slope)
    lot = jax.random.randint(jax.random.fold_in(rng, 1), extent, 0, int(grid[number_of - 1]))
    grade = jnp.searchsorted(jnp.asarray(grid, jnp.int32), lot, side="right")
    return jax.random.permutation(jax.random.fold_in(rng, 2), number_of)[grade].astype(jnp.int32)


def setup_inputs(seed: int = 0) -> dict:
    splits = jax.random.split(jax.random.key(seed), 8)
    teacher_rows = draw_teacher_rows(jax.random.fold_in(splits[7], 71), 0)
    teacher_gain = jnp.clip(1.0 + 0.15 * jax.random.normal(splits[1], (DT,), jnp.float32), 0.25, 1.75).astype(jnp.bfloat16)
    teacher_head = draw_teacher_head(jax.random.fold_in(splits[7], 71), 0)
    student_rows = draw_student_rows(jax.random.fold_in(splits[7], 71), 0)
    student_gain = jnp.clip(1.0 + 0.15 * jax.random.normal(splits[4], (DS,), jnp.float32), 0.25, 1.75).astype(jnp.bfloat16)
    student_head = draw_student_head(jax.random.fold_in(splits[7], 71), 0)
    labels = with_ends(ranked(splits[6], (TOKENS,), VOCAB, 2), jax.random.fold_in(splits[6], 3), 0, VOCAB - 1).astype(jnp.int32)
    return dict(teacher_rows=teacher_rows, teacher_gain=teacher_gain, teacher_head=teacher_head, student_rows=student_rows, student_gain=student_gain, student_head=student_head, labels=labels)


NORM_EPSILON = 1e-05
LABEL_WEIGHT = 0.5

def reference(teacher_rows, teacher_gain, teacher_head, student_rows, student_gain, student_head, labels):
    teacher_wide = teacher_rows.astype(jnp.float32)
    teacher_scale = lax.rsqrt(lax.optimization_barrier(jnp.mean(teacher_wide * teacher_wide, axis=1)) + NORM_EPSILON)
    teacher_scaled = (teacher_wide * teacher_gain.astype(jnp.float32)).astype(jnp.bfloat16)
    teacher_logits = teacher_scale[:, None] * jnp.dot(teacher_scaled, teacher_head, preferred_element_type=jnp.float32)
    student_wide = student_rows.astype(jnp.float32)
    gain_wide = student_gain.astype(jnp.float32)
    student_scale = lax.rsqrt(lax.optimization_barrier(jnp.mean(student_wide * student_wide, axis=1)) + NORM_EPSILON)
    student_normed = (student_wide * student_scale[:, None] * gain_wide).astype(jnp.bfloat16)
    student_logits = jnp.dot(student_normed, student_head, preferred_element_type=jnp.float32)
    teacher_top = lax.optimization_barrier(jnp.max(teacher_logits, axis=1))
    teacher_exp = jnp.exp(teacher_logits - teacher_top[:, None])
    teacher_total = lax.optimization_barrier(jnp.sum(teacher_exp, axis=1))
    teacher_cross = lax.optimization_barrier(jnp.sum(teacher_exp * (teacher_logits - student_logits), axis=1))
    student_top = lax.optimization_barrier(jnp.max(student_logits, axis=1))
    student_total = lax.optimization_barrier(jnp.sum(jnp.exp(student_logits - student_top[:, None]), axis=1))
    teacher_lse = teacher_top + jnp.log(teacher_total)
    student_lse = student_top + jnp.log(student_total)
    vocab_ids = jnp.arange(VOCAB, dtype=jnp.int32)
    label_hit = labels[:, None] == vocab_ids[None, :]
    picked = lax.optimization_barrier(jnp.sum(jnp.where(label_hit, student_logits, 0.0), axis=1))
    token_loss = teacher_cross / teacher_total - teacher_lse + student_lse + LABEL_WEIGHT * (student_lse - picked)
    teacher_prob = teacher_exp / teacher_total[:, None]
    student_prob = jnp.exp(student_logits - student_lse[:, None])
    logit_grad = ((1.0 + LABEL_WEIGHT) * student_prob - teacher_prob - LABEL_WEIGHT * label_hit.astype(jnp.float32)).astype(jnp.bfloat16)
    head_grad = lax.dot_general(student_normed, logit_grad, (((0,), (0,)), ((), ())), preferred_element_type=jnp.float32).astype(jnp.bfloat16)
    normed_grad = lax.dot_general(logit_grad, student_head, (((1,), (1,)), ((), ())), preferred_element_type=jnp.float32)
    norm_inner = lax.optimization_barrier(jnp.sum(gain_wide * normed_grad * student_wide, axis=1))
    cubed = student_scale * student_scale * student_scale
    rows_grad = (student_scale[:, None] * gain_wide * normed_grad - student_wide * cubed[:, None] * norm_inner[:, None] / DS).astype(jnp.bfloat16)
    gain_grad = lax.optimization_barrier(jnp.sum(normed_grad * student_wide * student_scale[:, None], axis=0))
    return (token_loss, head_grad, rows_grad, gain_grad)
```

```python
import jax
import jax.numpy as jnp
from jax import lax
from jax.experimental import pallas as pl
from jax.experimental.pallas import tpu as pltpu
from jax.sharding import PartitionSpec as P

NORM_EPSILON = 1e-05
LABEL_WEIGHT = 0.5
F32 = jnp.float32
BF16 = jnp.bfloat16
MESH = pl.DeviceIdType.MESH

DT, DS, TOKENS, LOCAL_V = 16384, 4096, 512, 512
SLAB = 64
PART = ((0, 208), (208, 208), (416, 224))
PART_S = ((0, 48), (208, 48), (416, 32))
PART_T = ((48, 160), (256, 160), (448, 192))
TOKEN_T = (0, 160, 320)
ORDER = (("x", "y", "z"), ("y", "z", "x"), ("z", "x", "y"))
RS_PART = ((0, 48), (48, 48), (96, 32))
ALL = slice(None)
LOW, HIGH = pl.ds(0, 2), pl.ds(2, 2)


def comm_kernel(
    t_rows, t_gain, wt_hbm, s_rows, s_gain, ws_hbm, labels,
    loss_out, rows_out, gain_out, xs_out, g_out,
    G, wt, ws, xs, acc_t, sl, base, st, col, scale_s, gains, g_ref, gp, own,
    sib_in, rs_a0, rs_a1, rs_a2, rs_b, rs_c, rs_d, fin, ex_tp0, ex_ph0, ex_tp1, ex_ph1, ex_gain,
    w_sem, out_sem, gain_s, gain_r, s1, r1, s2, r2, s3s, r3s, s3t, r3t, sibs_s, sibs_r, sibt_s, sibt_r,
    ex_s, ex_r, rs_sib_s, rs_sib_r, rs_s, rs_r,
):
    ph = lax.axis_index("phase")
    tp = lax.axis_index("tp")
    c = ph % 2
    me = {"x": ph // 2, "y": tp % 4, "z": tp // 4}
    sib = (ph + 1 - 2 * c, tp)

    def near(axis, step):
        at = dict(me)
        at[axis] = (me[axis] + step + 4) % 4
        return (at["x"] * 2 + c, at["z"] * 4 + at["y"])

    def rel(axis, step):
        return (me[axis] + step + 4) % 4

    def gat(core, at, rows):
        return G.at[core, at["x"], at["z"], at["y"], pl.ds(*rows), :]

    def remote(src, dst, ssem, rsem, to):
        return pltpu.make_async_remote_copy(
            src_ref=src, dst_ref=dst, send_sem=ssem, recv_sem=rsem, device_id=to, device_id_type=MESH
        )

    wt_loads = [pltpu.make_async_copy(wt_hbm.at[i], wt.at[i], w_sem.at[i]) for i in range(4)]
    ws_load = pltpu.make_async_copy(ws_hbm, ws, w_sem.at[4])
    for load in wt_loads:
        load.start()
    ws_load.start()

    barrier = pltpu.get_barrier_semaphore()

    def greet_tp(d, _):
        pl.semaphore_signal(barrier, inc=1, device_id=(ph, (tp + d) % 16), device_id_type=MESH)
        return 0

    def greet_ph(d, _):
        pl.semaphore_signal(barrier, inc=1, device_id=((ph + d) % 8, tp), device_id_type=MESH)
        return 0

    lax.fori_loop(1, 16, greet_tp, 0)
    lax.fori_loop(1, 8, greet_ph, 0)

    mine = G.at[c, me["x"], me["z"], me["y"]]
    wide = t_rows[...].astype(F32)
    scaled = (wide * t_gain[...].astype(F32)).astype(BF16)
    for (row, size), token in zip(PART_T, TOKEN_T):
        mine[pl.ds(row, size), :] = scaled[token : token + size]
    srow = s_rows[...]
    mine[0:48, :] = srow[0:48, 0:128]
    mine[208:224, :] = srow[48:64, 0:128]
    mine[224:256, :] = srow[0:32, 128:256]
    mine[416:448, :] = srow[32:64, 128:256]
    gains[tp] = s_gain[...]
    acc_t[...] = jnp.zeros_like(acc_t)

    pl.semaphore_wait(barrier, 22)

    def p1(p, i):
        axis = ORDER[p][0]
        block = gat(c, me, PART[p])
        return remote(block, block, s1.at[p, i], r1.at[p, i], near(axis, (1, -1, 2)[i]))

    for i in range(3):
        for p in range(3):
            p1(p, i).start()

    def gain_copy(d):
        return remote(gains.at[tp], gains.at[tp], gain_s.at[d], gain_r.at[d], (ph, (tp + d) % 16))

    def gain_start(d, _):
        gain_copy(d).start()
        return 0

    lax.fori_loop(1, 16, gain_start, 0)

    st[...] = jnp.broadcast_to(jnp.sum(wide * wide, axis=1, keepdims=True), st.shape)

    def line(p, two, three, rows, core=None, half=ALL):
        one, second, third = ORDER[p]
        return gat(c if core is None else core, {one: half, second: two, third: three}, rows)

    def p2(p, i):
        axis, third = ORDER[p][1], me[ORDER[p][2]]
        where = (me[axis], me[axis], rel(axis, -1), rel(axis, 1))[i]
        block = line(p, where, third, PART[p], half=(ALL, ALL, LOW, HIGH)[i])
        return remote(block, block, s2.at[p, i], r2.at[p, i], near(axis, (1, -1, 1, -1)[i]))

    def p2_in(p, i):
        axis, third = ORDER[p][1], me[ORDER[p][2]]
        where = (rel(axis, -1), rel(axis, 1), rel(axis, 2), rel(axis, 2))[i]
        block = line(p, where, third, PART[p], half=(ALL, ALL, LOW, HIGH)[i])
        return remote(block, block, s2.at[p, i], r2.at[p, i], near(axis, (1, -1, 1, -1)[i]))

    def plane(p, three, half):
        one, second, third = ORDER[p]
        return gat(c, {one: half, second: ALL, third: three}, PART_S[p])

    def p3s(p, i, receive=False):
        axis = ORDER[p][2]
        if receive:
            where = (rel(axis, -1), rel(axis, 1), rel(axis, 2), rel(axis, 2))[i]
        else:
            where = (me[axis], me[axis], rel(axis, -1), rel(axis, 1))[i]
        block = plane(p, where, (ALL, ALL, LOW, HIGH)[i])
        return remote(block, block, s3s.at[p, i], r3s.at[p, i], near(axis, (1, -1, 1, -1)[i]))

    STEP2 = (0, -1, 1, 2)

    def p3t(p, j, i, receive=False):
        axis = ORDER[p][2]
        if receive:
            where = (rel(axis, -1), rel(axis, 1), rel(axis, 2), rel(axis, 2))[i]
        else:
            where = (me[axis], me[axis], rel(axis, -1), rel(axis, 1))[i]
        block = line(p, rel(ORDER[p][1], STEP2[j]), where, PART_T[p], half=(ALL, ALL, LOW, HIGH)[i])
        return remote(block, block, s3t.at[p, 4 * j + i], r3t.at[p, 4 * j + i], near(axis, (1, -1, 1, -1)[i]))

    def sib_t(p, j, k, receive=False):
        block = line(
            p, rel(ORDER[p][1], STEP2[j]), rel(ORDER[p][2], STEP2[k]), PART_T[p], core=1 - c if receive else c
        )
        return remote(block, block, sibt_s.at[p, 4 * j + k], sibt_r.at[p, 4 * j + k], sib)

    def sib_s(p, receive=False):
        block = G.at[1 - c if receive else c, :, :, :, pl.ds(*PART_S[p]), :]
        return remote(block, block, sibs_s.at[p], sibs_r.at[p], sib)

    def p3t_send(j):
        for p in range(3):
            p3t(p, j, 0).start()
            p3t(p, j, 1).start()

    def consume(j, k):
        for p in range(3):
            sib_t(p, j, k, receive=True).wait_recv()

        def one_core(core, _):
            for p in range(3):
                one, second, third = ORDER[p]
                at = {one: ALL, second: rel(second, STEP2[j]), third: rel(third, STEP2[k])}
                rows = G[core, at["x"], at["z"], at["y"], pl.ds(*PART_T[p]), :]
                lhs = jnp.concatenate([rows[i] for i in range(4)], axis=1)
                rhs = wt[at["x"], core, at["z"], at["y"]].reshape(512, LOCAL_V)
                acc_t[pl.ds(TOKEN_T[p], PART_T[p][1]), :] += jnp.dot(lhs, rhs, preferred_element_type=F32)
            return 0

        lax.fori_loop(0, 2, one_core, 0)

    for p in range(3):
        for i in range(3):
            p1(p, i).wait_recv()
        p2(p, 0).start()
        p2(p, 1).start()
    p3t_send(0)
    for i in (0, 1):
        for p in range(3):
            p2_in(p, i).wait_recv()
            p2(p, i + 2).start()
    for p in range(3):
        sib_t(p, 0, 0).start()
    for p in range(3):
        p2_in(p, 2).wait_recv()
        p2_in(p, 3).wait_recv()
        p3s(p, 0).start()
        p3s(p, 1).start()
    p3t_send(1)
    for load in wt_loads:
        load.wait()
    ws_load.wait()
    consume(0, 0)
    for j in (1, 2, 3):
        for p in range(3):
            sib_t(p, j, 0).start()
    for i in (0, 1):
        for p in range(3):
            p3s(p, i, True).wait_recv()
            p3s(p, i + 2).start()
    consume(1, 0)

    def forward(j):
        for i in (0, 1):
            for p in range(3):
                p3t(p, j, i, True).wait_recv()
                p3t(p, j, i + 2).start()
                sib_t(p, j, i + 1).start()

    def opposite(j):
        for p in range(3):
            p3t(p, j, 2, True).wait_recv()
            p3t(p, j, 3, True).wait_recv()
            sib_t(p, j, 3).start()

    forward(0)
    for p in range(3):
        p3s(p, 2, True).wait_recv()
        p3s(p, 3, True).wait_recv()
        sib_s(p).start()
    p3t_send(2)
    consume(0, 1)
    consume(0, 2)
    opposite(0)
    p3t_send(3)

    def gain_wait(d, _):
        gain_copy(d).wait()
        return 0

    lax.fori_loop(1, 16, gain_wait, 0)
    for p in range(3):
        sib_s(p, True).wait_recv()

    def halves(q, t):
        block = G.at[q % 2, q // 2, t // 4, t % 4]
        first = jnp.concatenate([block[0:48, :], block[208:224, :]], axis=0)
        second = jnp.concatenate([block[224:256, :], block[416:448, :]], axis=0)
        return first.astype(F32), second.astype(F32)

    def norm_slab(q, _):
        def squares(t, total):
            first, second = halves(q, t)
            return total + first * first + second * second

        total = lax.fori_loop(0, 16, squares, jnp.zeros((SLAB, 128), F32))
        scale = lax.rsqrt(jnp.sum(total, axis=1, keepdims=True) / DS + NORM_EPSILON)
        rows = pl.ds(pl.multiple_of(q * SLAB, SLAB), SLAB)
        scale_s[rows, :] = scale

        def normed(t, _):
            first, second = halves(q, t)
            gain = gains[t].astype(F32)
            xs[t, rows, 0:128] = (first * scale * gain[0:1, :]).astype(BF16)
            xs[t, rows, 128:256] = (second * scale * gain[1:2, :]).astype(BF16)
            return 0

        lax.fori_loop(0, 16, normed, 0)
        return 0

    lax.fori_loop(0, 8, norm_slab, 0)
    xs_copy = pltpu.make_async_copy(xs, xs_out, out_sem.at[0])
    xs_copy.start()
    forward(1)

    sl[...] = jnp.dot(xs[0], ws[0], preferred_element_type=F32)

    def student_dot(t, _):
        sl[...] += jnp.dot(xs[t], ws[t], preferred_element_type=F32)
        return 0

    lax.fori_loop(1, 16, student_dot, 0)
    vocab_first = (ph * 16 + tp) * LOCAL_V
    lane = lax.broadcasted_iota(jnp.int32, (SLAB, 128), 1)

    def slab(q):
        return pl.ds(pl.multiple_of(q * SLAB, SLAB), SLAB)

    def label_hit(rows):
        ids = vocab_first + lax.broadcasted_iota(jnp.int32, (SLAB, LOCAL_V), 1)
        return labels[rows, :] == ids

    def pack(columns):
        out = jnp.zeros((SLAB, 128), F32)
        for i, column in enumerate(columns):
            out = jnp.where(lane == i, column, out)
        return out

    def rowsum(value):
        return jnp.sum(value, axis=1, keepdims=True)

    def student_stats(q, _):
        rows = slab(q)
        logits = sl[rows, :]
        top = jnp.max(logits, axis=1, keepdims=True)
        e = jnp.exp(logits - top)
        picked = jnp.where(label_hit(rows), logits, 0.0)
        st[rows, :] = pack([top, rowsum(e), rowsum(e * logits), rowsum(picked), st[rows, 0:1]])
        return 0

    lax.fori_loop(0, 8, student_stats, 0)

    def exchange_start(buf, own_slot, count, number, to):
        def start(d, _):
            remote(buf.at[own_slot], buf.at[own_slot], ex_s.at[number, d], ex_r.at[number, d], to(d)).start()
            return 0

        lax.fori_loop(1, count, start, 0)

    def exchange_wait(buf, own_slot, count, number, to):
        def wait(d, _):
            remote(buf.at[own_slot], buf.at[own_slot], ex_s.at[number, d], ex_r.at[number, d], to(d)).wait()
            return 0

        lax.fori_loop(1, count, wait, 0)

    def to_tp(d):
        return (ph, (tp + d) % 16)

    def to_ph(d):
        return ((ph + d) % 8, tp)

    sub = lax.broadcasted_iota(jnp.int32, (8, TOKENS), 0)

    def merge(buf, count, weighted):
        top = buf[0][0:1, :]
        for i in range(1, count):
            top = jnp.maximum(top, buf[i][0:1, :])
        total = jnp.zeros((8, TOKENS), F32)
        for i in range(count):
            part = buf[i]
            weight = jnp.exp(part[0:1, :] - top)
            total = total + part * jnp.where(sub <= weighted, weight, 1.0)
        return jnp.where(sub == 0, top, total)

    def transposed_stats():
        return jnp.transpose(st[...])[0:8, :]

    ex_tp0[tp] = transposed_stats()
    exchange_start(ex_tp0, tp, 16, 0, to_tp)
    opposite(1)
    consume(0, 3)
    consume(1, 1)
    consume(1, 2)
    exchange_wait(ex_tp0, tp, 16, 0, to_tp)
    ex_ph0[ph] = merge(ex_tp0, 16, 2)
    exchange_start(ex_ph0, ph, 8, 1, to_ph)
    forward(2)
    consume(2, 0)
    consume(1, 3)
    consume(2, 1)
    consume(2, 2)
    exchange_wait(ex_ph0, ph, 8, 1, to_ph)
    early = merge(ex_ph0, 8, 2)
    student_top, student_total, student_inner = early[0:1], early[1:2], early[2:3] / early[1:2]
    picked_all, squares_all = early[3:4], early[4:5]
    student_lse = student_top + jnp.log(student_total)
    teacher_scale = lax.rsqrt(squares_all / DT + NORM_EPSILON)

    def to_columns(rows):
        block = jnp.concatenate(rows + [jnp.zeros((128 - len(rows), TOKENS), F32)], axis=0)
        return jnp.transpose(block)

    col[...] = to_columns([student_lse, teacher_scale])

    def student_grad(q, _):
        rows = slab(q)
        prob = jnp.exp(sl[rows, :] - col[rows, 0:1])
        base[rows, :] = (1.0 + LABEL_WEIGHT) * prob - LABEL_WEIGHT * label_hit(rows).astype(F32)
        return 0

    lax.fori_loop(0, 8, student_grad, 0)
    forward(3)
    opposite(2)
    consume(3, 0)
    consume(3, 1)
    consume(3, 2)
    consume(2, 3)
    opposite(3)
    consume(3, 3)

    def teacher_stats(q, _):
        rows = slab(q)
        logits = acc_t[rows, :] * col[rows, 1:2]
        student = sl[rows, :]
        top = jnp.max(logits, axis=1, keepdims=True)
        e = jnp.exp(logits - top)
        acc_t[rows, :] = e
        st[rows, :] = pack([top, rowsum(e), rowsum(e * (logits - student)), rowsum(e * student)])
        return 0

    lax.fori_loop(0, 8, teacher_stats, 0)
    local_stats = transposed_stats()
    ex_tp1[tp] = local_stats
    exchange_start(ex_tp1, tp, 16, 2, to_tp)
    exchange_wait(ex_tp1, tp, 16, 2, to_tp)
    ex_ph1[ph] = merge(ex_tp1, 16, 3)
    exchange_start(ex_ph1, ph, 8, 3, to_ph)
    exchange_wait(ex_ph1, ph, 8, 3, to_ph)
    late = merge(ex_ph1, 8, 3)
    teacher_top, teacher_total = late[0:1], late[1:2]
    teacher_lse = teacher_top + jnp.log(teacher_total)
    loss = (
        late[2:3] / teacher_total - teacher_lse + student_lse + LABEL_WEIGHT * (student_lse - picked_all)
    )
    inner = (1.0 + LABEL_WEIGHT) * student_inner - late[3:4] / teacher_total - LABEL_WEIGHT * picked_all
    factor = jnp.exp(local_stats[0:1] - teacher_top) / teacher_total
    col[...] = to_columns([factor, inner, loss])

    def logit_grad(q, _):
        rows = slab(q)
        g = (base[rows, :] - acc_t[rows, :] * col[rows, 0:1]).astype(BF16)
        g_ref[rows, :] = g
        gp[(q + c) % 2, pl.ds(pl.multiple_of((q // 2) * SLAB, SLAB), SLAB), :] = g
        return 0

    lax.fori_loop(0, 8, logit_grad, 0)
    g_copy = pltpu.make_async_copy(g_ref, g_out, out_sem.at[1])
    g_copy.start()

    def sib_chunks(t):
        return wt.at[:, 0, t // 4, t % 4, :, pl.ds(0, 128)]

    def rs_sib(t):
        return remote(sib_chunks(t), sib_in.at[:, t // 4, t % 4], rs_sib_s.at[t], rs_sib_r.at[t], sib)

    def nt_dot(lhs, rhs):
        return lax.dot_general(lhs, rhs, (((1,), (1,)), ((), ())), preferred_element_type=F32)

    def sib_part(t, _):
        r = nt_dot(gp[1], ws[t]).astype(BF16)
        for xt in range(4):
            wt[xt, 0, t // 4, t % 4, 0:64, 0:128] = r[xt * 64 : xt * 64 + 64, 0:128]
            wt[xt, 0, t // 4, t % 4, 64:128, 0:128] = r[xt * 64 : xt * 64 + 64, 128:256]
        rs_sib(t).start()
        return 0

    lax.fori_loop(0, 16, sib_part, 0)

    def own_part(t, _):
        r = nt_dot(gp[0], ws[t])
        rs_sib(t).wait_recv()
        for xt in range(4):
            other = sib_in[xt, t // 4, t % 4].astype(F32)
            own[xt, t // 4, t % 4, 0:64] = r[xt * 64 : xt * 64 + 64, 0:128] + other[0:64]
            own[xt, t // 4, t % 4, 64:128] = r[xt * 64 : xt * 64 + 64, 128:256] + other[64:128]
        return 0

    lax.fori_loop(0, 16, own_part, 0)

    def at3(p, one, two, three):
        a, b, d = ORDER[p]
        at = {a: one, b: two, d: three}
        return at["x"], at["z"], at["y"]

    def stage_ref(p, one, two, three):
        ix, iz, iy = at3(p, one, two, three)
        return wt.at[ix, 0, iz, iy, pl.ds(*RS_PART[p]), pl.ds(128, 128)]

    def own_ref(p, one, two, three):
        ix, iz, iy = at3(p, one, two, three)
        return own.at[ix, iz, iy, pl.ds(*RS_PART[p]), :]

    def rest(p, two, three):
        at = {ORDER[p][1]: two, ORDER[p][2]: three}
        return tuple(at[k] for k in ("x", "z", "y") if k in at)

    rs_a = (rs_a0, rs_a1, rs_a2)

    def stage(p, one, two, three):
        stage_ref(p, one, two, three)[...] = own_ref(p, one, two, three)[...].astype(BF16)

    def rs_copy(src, dst, p, i, to):
        return remote(src, dst, rs_s.at[p, i], rs_r.at[p, i], to)

    def rs1(p, i):
        axis = ORDER[p][0]
        src = stage_ref(p, rel(axis, 2), (LOW, HIGH)[i], ALL)
        return rs_copy(src, rs_a[p].at[i], p, i, near(axis, (1, -1)[i]))

    def rs2(p, i):
        axis = ORDER[p][0]
        src = stage_ref(p, rel(axis, (1, -1)[i]), ALL, ALL)
        return rs_copy(src, rs_b.at[i, :, :, pl.ds(*RS_PART[p]), :], p, 2 + i, near(axis, (1, -1)[i]))

    def rs3(p, i):
        axis = ORDER[p][1]
        src = stage_ref(p, me[ORDER[p][0]], rel(axis, (1, -1, 2)[i]), ALL)
        return rs_copy(src, rs_c.at[i, :, pl.ds(*RS_PART[p]), :], p, 4 + i, near(axis, (1, -1, 2)[i]))

    def rs4(p, i):
        axis = ORDER[p][2]
        src = stage_ref(p, me[ORDER[p][0]], me[ORDER[p][1]], rel(axis, (1, -1, 2)[i]))
        return rs_copy(src, rs_d.at[i, pl.ds(*RS_PART[p]), :], p, 7 + i, near(axis, (1, -1, 2)[i]))

    for p in range(3):
        def far(n, _, p=p):
            stage(p, rel(ORDER[p][0], 2), n // 4, n % 4)
            return 0

        lax.fori_loop(0, 16, far, 0)
        rs1(p, 0).start()
        rs1(p, 1).start()
    for p in range(3):
        rows = pl.ds(*RS_PART[p])
        for i in range(2):
            rs1(p, i).wait_recv()

            def pass_on(n, _, p=p, i=i, rows=rows):
                target = rel(ORDER[p][0], (1, -1)[i])
                near_half = n // 4
                two = near_half + 2 * i
                stage_ref(p, target, two, n % 4)[...] = (
                    own_ref(p, target, two, n % 4)[...] + rs_a[p][(i, *rest(p, near_half, n % 4))].astype(F32)
                ).astype(BF16)
                stage(p, target, near_half + 2 * (1 - i), n % 4)
                return 0

            lax.fori_loop(0, 8, pass_on, 0)
            rs2(p, i).start()
    for p in range(3):
        rows = pl.ds(*RS_PART[p])
        rs2(p, 0).wait_recv()
        rs2(p, 1).wait_recv()

        def add_first(n, _, p=p, rows=rows):
            ref = own_ref(p, me[ORDER[p][0]], n // 4, n % 4)
            total = (
                ref[...]
                + rs_b[(0, *rest(p, n // 4, n % 4), rows, ALL)].astype(F32)
                + rs_b[(1, *rest(p, n // 4, n % 4), rows, ALL)].astype(F32)
            )
            ref[...] = total
            stage_ref(p, me[ORDER[p][0]], n // 4, n % 4)[...] = total.astype(BF16)
            return 0

        lax.fori_loop(0, 16, add_first, 0)
        for i in (2, 0, 1):
            rs3(p, i).start()
    for p in range(3):
        rows = pl.ds(*RS_PART[p])
        for i in range(3):
            rs3(p, i).wait_recv()

        def add_second(n, _, p=p, rows=rows):
            ref = own_ref(p, me[ORDER[p][0]], me[ORDER[p][1]], n)
            total = ref[...]
            for i in range(3):
                total = total + rs_c[i, n, rows, :].astype(F32)
            ref[...] = total
            stage_ref(p, me[ORDER[p][0]], me[ORDER[p][1]], n)[...] = total.astype(BF16)
            return 0

        lax.fori_loop(0, 4, add_second, 0)
        for i in (2, 0, 1):
            rs4(p, i).start()
    for p in range(3):
        rows = pl.ds(*RS_PART[p])
        for i in range(3):
            rs4(p, i).wait_recv()
        total = own_ref(p, me[ORDER[p][0]], me[ORDER[p][1]], me[ORDER[p][2]])[...]
        for i in range(3):
            total = total + rs_d[i, rows, :].astype(F32)
        fin[rows, :] = total

    rows = slab(ph)
    scale = scale_s[rows, :]
    inner_own = col[rows, 1:2]
    raw = s_rows[...].astype(F32)
    gain = s_gain[...].astype(F32)
    coefficient = scale * scale * inner_own / DS
    parts = []
    for h in range(2):
        grad = fin[h * 64 : h * 64 + 64, :]
        wide_h = raw[:, h * 128 : h * 128 + 128]
        rows_out[:, h * 128 : h * 128 + 128] = (scale * gain[h : h + 1] * grad - wide_h * coefficient).astype(BF16)
        parts.append(jnp.sum(grad * wide_h * scale, axis=0, keepdims=True))
    ex_gain[ph] = jnp.broadcast_to(jnp.concatenate(parts, axis=1), (8, 256))
    exchange_start(ex_gain, ph, 8, 4, to_ph)
    base[0:8, :] = jnp.broadcast_to(loss, (8, TOKENS))
    window = base[0:1, pl.ds(pl.multiple_of(me["x"] * 128, 128), 128)]
    loss_out[...] = jnp.where(c == 1, window[:, 64:128], window[:, 0:64])
    exchange_wait(ex_gain, ph, 8, 4, to_ph)
    total = ex_gain[0]
    for i in range(1, 8):
        total = total + ex_gain[i]
    gain_out[...] = total[0:1]

    for p in range(3):
        for i in range(3):
            p1(p, i).wait_send()
        for i in range(4):
            p2(p, i).wait_send()
            p3s(p, i).wait_send()
        sib_s(p).wait_send()
        for j in range(4):
            for i in range(4):
                p3t(p, j, i).wait_send()
                sib_t(p, j, i).wait_send()
        for i in range(2):
            rs1(p, i).wait_send()
            rs2(p, i).wait_send()
        for i in range(3):
            rs3(p, i).wait_send()
            rs4(p, i).wait_send()

    def sib_sent(t, _):
        rs_sib(t).wait_send()
        return 0

    lax.fori_loop(0, 16, sib_sent, 0)
    xs_copy.wait()
    g_copy.wait()


def head_kernel(xs_ref, g_ref, out_ref):
    out_ref[...] = lax.dot_general(
        xs_ref[0], g_ref[...], (((0,), (0,)), ((), ())), preferred_element_type=F32
    ).astype(BF16)


def local(teacher_rows, teacher_gain, teacher_head, student_rows, student_gain, student_head, labels):
    vmem = pl.BlockSpec(memory_space=pltpu.VMEM)
    hbm = pl.BlockSpec(memory_space=pl.ANY)
    dma = pltpu.SemaphoreType.DMA
    loss, rows_grad, gain_grad, xs, g = pl.pallas_call(
        comm_kernel,
        out_shape=(
            jax.ShapeDtypeStruct((1, SLAB), F32),
            jax.ShapeDtypeStruct((SLAB, 256), BF16),
            jax.ShapeDtypeStruct((1, 256), F32),
            jax.ShapeDtypeStruct((16, TOKENS, 256), BF16),
            jax.ShapeDtypeStruct((TOKENS, LOCAL_V), BF16),
        ),
        in_specs=[vmem, vmem, hbm, vmem, vmem, hbm, vmem],
        out_specs=(vmem, vmem, vmem, hbm, hbm),
        scratch_shapes=[
            pltpu.VMEM((2, 4, 4, 4, 640, 128), BF16),
            pltpu.VMEM((4, 2, 4, 4, 128, LOCAL_V), BF16),
            pltpu.VMEM((16, 256, LOCAL_V), BF16),
            pltpu.VMEM((16, TOKENS, 256), BF16),
            pltpu.VMEM((TOKENS, LOCAL_V), F32),
            pltpu.VMEM((TOKENS, LOCAL_V), F32),
            pltpu.VMEM((TOKENS, LOCAL_V), F32),
            pltpu.VMEM((TOKENS, 128), F32),
            pltpu.VMEM((TOKENS, 128), F32),
            pltpu.VMEM((TOKENS, 1), F32),
            pltpu.VMEM((16, 2, 128), BF16),
            pltpu.VMEM((TOKENS, LOCAL_V), BF16),
            pltpu.VMEM((2, 256, LOCAL_V), BF16),
            pltpu.VMEM((4, 4, 4, 128, 128), F32),
            pltpu.VMEM((4, 4, 4, 128, 128), BF16),
            pltpu.VMEM((2, 4, 2, 48, 128), BF16),
            pltpu.VMEM((2, 4, 2, 48, 128), BF16),
            pltpu.VMEM((2, 2, 4, 32, 128), BF16),
            pltpu.VMEM((2, 4, 4, 128, 128), BF16),
            pltpu.VMEM((3, 4, 128, 128), BF16),
            pltpu.VMEM((3, 128, 128), BF16),
            pltpu.VMEM((128, 128), F32),
            pltpu.VMEM((16, 8, TOKENS), F32),
            pltpu.VMEM((8, 8, TOKENS), F32),
            pltpu.VMEM((16, 8, TOKENS), F32),
            pltpu.VMEM((8, 8, TOKENS), F32),
            pltpu.VMEM((8, 8, 256), F32),
            dma((5,)), dma((2,)), dma((16,)), dma((16,)),
            dma((3, 3)), dma((3, 3)), dma((3, 4)), dma((3, 4)), dma((3, 4)), dma((3, 4)),
            dma((3, 16)), dma((3, 16)), dma((3,)), dma((3,)), dma((3, 16)), dma((3, 16)),
            dma((5, 16)), dma((5, 16)), dma((16,)), dma((16,)), dma((3, 10)), dma((3, 10)),
        ],
        compiler_params=pltpu.CompilerParams(
            collective_id=0, has_side_effects=True, vmem_limit_bytes=63 << 20
        ),
        name="distill",
    )(
        teacher_rows,
        teacher_gain.reshape(1, 128),
        teacher_head.reshape(4, 2, 4, 4, 128, LOCAL_V),
        student_rows,
        student_gain.reshape(2, 128),
        student_head.reshape(16, 256, LOCAL_V),
        labels.reshape(TOKENS, 1),
    )
    head_grad = pl.pallas_call(
        head_kernel,
        grid=(16,),
        out_shape=jax.ShapeDtypeStruct((DS, LOCAL_V), BF16),
        in_specs=[
            pl.BlockSpec((1, TOKENS, 256), lambda t: (t, 0, 0)),
            pl.BlockSpec((TOKENS, LOCAL_V), lambda t: (0, 0)),
        ],
        out_specs=pl.BlockSpec((256, LOCAL_V), lambda t: (t, 0)),
        name="head_grad",
    )(xs, g)
    return loss.reshape(SLAB), head_grad, rows_grad, gain_grad.reshape(256)


def solution(mesh):
    placed = (
        P(None, ("phase", "tp")),
        P(("phase", "tp")),
        P(None, ("phase", "tp")),
        P("phase", "tp"),
        P("tp"),
        P(None, ("phase", "tp")),
        P(),
    )
    return jax.shard_map(
        local,
        mesh=mesh,
        in_specs=placed,
        out_specs=(P("phase"), P(None, ("phase", "tp")), P("phase", "tp"), P("tp")),
        check_vma=False,
    )
```

```python
import jax
import jax.numpy as jnp
from jax import lax
from jax.experimental import pallas as pl
from jax.experimental.pallas import tpu as pltpu
from jax.sharding import PartitionSpec as P

NORM_EPSILON = 1e-05
LABEL_WEIGHT = 0.5
F32 = jnp.float32
BF16 = jnp.bfloat16
MESH = pl.DeviceIdType.MESH

DT, DS, TOKENS, LOCAL_V = 16384, 4096, 512, 512
SLAB = 64
PART = ((0, 208), (208, 208), (416, 224))
PART_S = ((0, 48), (208, 48), (416, 32))
PART_T = ((48, 160), (256, 160), (448, 192))
TOKEN_T = (0, 160, 320)
ORDER = (("x", "y", "z"), ("y", "z", "x"), ("z", "x", "y"))
RS_PART = ((0, 48), (48, 48), (96, 32))
ALL = slice(None)
LOW, HIGH = pl.ds(0, 2), pl.ds(2, 2)


def comm_kernel(
    t_rows, t_gain, wt_hbm, s_rows, s_gain, ws_hbm, labels,
    loss_out, rows_out, gain_out, xst_out, g_out,
    G, wt, ws, ws_sib, xs, xst, acc_t, sl, es, st, col, lab, scale_s, g_ref, gp, gp_in, own,
    rs_b, rs_c, rs_d, fin, ex_tp0, ex_ph0, ex_tp1, ex_ph1, ex_gain,
    w_sem, out_sem, s1, r1, s2, r2, s2f, r2f, s3s, r3s, s3t, r3t, sibs_s, sibs_r, sibt_s, sibt_r,
    ex_s, ex_r, misc_s, misc_r, rs_s, rs_r,
):
    ph = lax.axis_index("phase")
    tp = lax.axis_index("tp")
    c = ph % 2
    me = {"x": ph // 2, "y": tp % 4, "z": tp // 4}
    sib = (ph + 1 - 2 * c, tp)
    PARTS = range(3)
    STEP = (0, -1, 1, 2)

    def rel(axis, step):
        return (me[axis] + step + 4) % 4

    def near(axis, step):
        at = dict(me)
        at[axis] = rel(axis, step)
        return (at["x"] * 2 + c, at["z"] * 4 + at["y"])

    def remote(src, dst, ssem, rsem, to):
        return pltpu.make_async_remote_copy(
            src_ref=src, dst_ref=dst, send_sem=ssem, recv_sem=rsem, device_id=to, device_id_type=MESH
        )

    wt_loads = [pltpu.make_async_copy(wt_hbm.at[i], wt.at[i], w_sem.at[i]) for i in range(4)]
    ws_load = pltpu.make_async_copy(ws_hbm, ws, w_sem.at[4])
    ws_load.start()
    for load in wt_loads:
        load.start()

    barrier = pltpu.get_barrier_semaphore()
    partners = [sib] + [near(axis, step) for axis in "xyz" for step in (1, -1, 2)]
    for to in partners:
        pl.semaphore_signal(barrier, inc=1, device_id=to, device_id_type=MESH)

    mine = G.at[c, me["x"], me["z"], me["y"]]
    wide = t_rows[...].astype(F32)
    scaled = (wide * t_gain[...].astype(F32)).astype(BF16)
    for (row, size), token in zip(PART_T, TOKEN_T):
        mine[pl.ds(row, size), :] = scaled[token : token + size]
    srow = s_rows[...]
    mine[0:48, :] = srow[0:48, 0:128]
    mine[208:224, :] = srow[48:64, 0:128]
    mine[224:256, :] = srow[0:32, 128:256]
    mine[416:448, :] = srow[32:64, 128:256]

    pl.semaphore_wait(barrier, len(partners))

    def block(p, one, two, three, rows, core=None):
        a, b, d = ORDER[p]
        at = {a: one, b: two, d: three}
        return G.at[c if core is None else core, at["x"], at["z"], at["y"], pl.ds(*rows), :]

    def own_at(p):
        return tuple(me[axis] for axis in ORDER[p])

    def p1(p, i):
        ref = block(p, *own_at(p), PART[p])
        return remote(ref, ref, s1.at[p, i], r1.at[p, i], near(ORDER[p][0], (-1, 1, 2)[i]))

    def p2(p, n, i):
        a, b, d = ORDER[p]
        ref = block(p, rel(a, STEP[n]), me[b], me[d], PART[p])
        return remote(ref, ref, s2.at[p, 2 * n + i], r2.at[p, 2 * n + i], near(b, (1, -1)[i]))

    def p2f(p, i):
        a, b, d = ORDER[p]
        ref = block(p, (LOW, HIGH)[i], rel(b, (-1, 1)[i]), me[d], PART[p])
        return remote(ref, ref, s2f.at[p, i], r2f.at[p, i], near(b, (1, -1)[i]))

    def p3s(p, i):
        d = ORDER[p][2]
        ref = block(p, (ALL, ALL, LOW, HIGH)[i], ALL, rel(d, (0, 0, -1, 1)[i]), PART_S[p])
        return remote(ref, ref, s3s.at[p, i], r3s.at[p, i], near(d, (1, -1, 1, -1)[i]))

    def p3t(p, j, i):
        a, b, d = ORDER[p]
        ref = block(p, (ALL, ALL, LOW, HIGH)[i], rel(b, STEP[j]), rel(d, (0, 0, -1, 1)[i]), PART_T[p])
        return remote(ref, ref, s3t.at[p, 4 * j + i], r3t.at[p, 4 * j + i], near(d, (1, -1, 1, -1)[i]))

    def p2_wait(p, n, i):
        a, b, d = ORDER[p]
        ref = block(p, rel(a, STEP[n]), rel(b, (-1, 1)[i]), me[d], PART[p])
        remote(ref, ref, s2.at[p, 2 * n + i], r2.at[p, 2 * n + i], sib).wait_recv()

    def p2f_wait(p, i):
        a, b, d = ORDER[p]
        ref = block(p, (LOW, HIGH)[i], rel(b, 2), me[d], PART[p])
        remote(ref, ref, s2f.at[p, i], r2f.at[p, i], sib).wait_recv()

    def p3s_wait(p, i):
        d = ORDER[p][2]
        ref = block(p, (ALL, ALL, LOW, HIGH)[i], ALL, rel(d, (-1, 1, 2, 2)[i]), PART_S[p])
        remote(ref, ref, s3s.at[p, i], r3s.at[p, i], sib).wait_recv()

    def p3t_wait(p, j, i):
        a, b, d = ORDER[p]
        ref = block(p, (ALL, ALL, LOW, HIGH)[i], rel(b, STEP[j]), rel(d, (-1, 1, 2, 2)[i]), PART_T[p])
        remote(ref, ref, s3t.at[p, 4 * j + i], r3t.at[p, 4 * j + i], sib).wait_recv()

    def sib_t(p, j, k, core=None):
        a, b, d = ORDER[p]
        ref = block(p, ALL, rel(b, STEP[j]), rel(d, STEP[k]), PART_T[p], core)
        return remote(ref, ref, sibt_s.at[p, 4 * j + k], sibt_r.at[p, 4 * j + k], sib)

    def sib_s(p, core):
        ref = G.at[core, :, :, :, pl.ds(*PART_S[p]), :]
        return remote(ref, ref, sibs_s.at[p], sibs_r.at[p], sib)

    def p3t_send(j):
        for p in PARTS:
            p3t(p, j, 0).start()
            p3t(p, j, 1).start()

    def products(j, k, core):
        for p in PARTS:
            a, b, d = ORDER[p]
            at = {a: ALL, b: rel(b, STEP[j]), d: rel(d, STEP[k])}
            rows = G[core, at["x"], at["z"], at["y"], pl.ds(*PART_T[p]), :]
            lhs = jnp.concatenate([rows[i] for i in range(4)], axis=1)
            rhs = wt[at["x"], core, at["z"], at["y"]].reshape(512, LOCAL_V)
            acc_t[pl.ds(TOKEN_T[p], PART_T[p][1]), :] += jnp.dot(lhs, rhs, preferred_element_type=F32)

    def sib_wait(j, k):
        for p in PARTS:
            sib_t(p, j, k, core=1 - c).wait_recv()

    def consume(j, k):
        sib_wait(j, k)

        def one_core(core, _):
            products(j, k, core)
            return 0

        lax.fori_loop(0, 2, one_core, 0)

    def rowsum(value):
        return jnp.sum(value, axis=1, keepdims=True)

    def to_tp(d):
        return (ph, (tp + d) % 16)

    def to_ph(d):
        return ((ph + d) % 8, tp)

    def exchange(buf, slot, count, number, to):
        def copy(d):
            return remote(buf.at[slot], buf.at[slot], ex_s.at[number, d], ex_r.at[number, d], to(d))

        def start():
            for d in range(1, count):
                copy(d).start()

        def wait():
            for d in range(1, count):
                copy(d).wait_recv()

        def sent():
            for d in range(1, count):
                copy(d).wait_send()

        return start, wait, sent

    early_tp = exchange(ex_tp0, tp, 16, 0, to_tp)
    early_ph = exchange(ex_ph0, ph, 8, 1, to_ph)
    late_tp = exchange(ex_tp1, tp, 16, 2, to_tp)
    late_ph = exchange(ex_ph1, ph, 8, 3, to_ph)
    gain_ph = exchange(ex_gain, ph, 8, 4, to_ph)

    def to_columns(rows):
        filled = jnp.concatenate(rows + [jnp.zeros((128 - len(rows), TOKENS), F32)], axis=0)
        return jnp.transpose(filled)

    for i in range(3):
        for p in PARTS:
            p1(p, i).start()
    for p in PARTS:
        p2(p, 0, 0).start()
        p2(p, 0, 1).start()
    st[...] = jnp.broadcast_to(rowsum(wide * wide), st.shape)
    squares = jnp.transpose(st[...])[0:1]
    ex_tp0[tp] = jnp.concatenate(
        [squares[:, 128 * i : 128 * i + 128] for i in range(4)]
        + [s_gain[...].astype(F32), jnp.zeros((2, 128), F32)],
        axis=0,
    )
    lab[...] = to_columns([labels[...].astype(F32)])
    acc_t[...] = jnp.zeros_like(acc_t)
    for n in (1, 2, 3):
        for p in PARTS:
            a, b, d = ORDER[p]
            ref = block(p, rel(a, STEP[n]), me[b], me[d], PART[p])
            remote(ref, ref, s1.at[p, (1, 0, 2)[n - 1]], r1.at[p, (1, 0, 2)[n - 1]], sib).wait_recv()
            p2(p, n, 0).start()
            p2(p, n, 1).start()
    p3t_send(0)
    for p in PARTS:
        sib_t(p, 0, 0).start()
    for i in (0, 1):
        for p in PARTS:
            for n in range(4):
                p2_wait(p, n, i)
            p2f(p, i).start()
            sib_t(p, i + 1, 0).start()
    for p in PARTS:
        p2f_wait(p, 0)
        p2f_wait(p, 1)
        p3s(p, 0).start()
        p3s(p, 1).start()
        sib_t(p, 3, 0).start()
    p3t_send(1)
    early_tp[0]()
    ws_load.wait()
    ws_push = remote(ws, ws_sib, misc_s.at[0], misc_r.at[0], sib)
    ws_push.start()
    for load in wt_loads:
        load.wait()
    consume(0, 0)

    def forward(j):
        for i in (0, 1):
            for p in PARTS:
                p3t_wait(p, j, i)
                p3t(p, j, i + 2).start()
                sib_t(p, j, i + 1).start()

    def opposite(j):
        for p in PARTS:
            p3t_wait(p, j, 2)
            p3t_wait(p, j, 3)
            sib_t(p, j, 3).start()

    forward(0)
    p3t_send(2)
    consume(1, 0)
    consume(2, 0)
    early_tp[1]()
    early = ex_tp0[0]
    for i in range(1, 16):
        early = early + ex_tp0[i]
    ex_ph0[ph] = early
    early_ph[0]()
    for i in (0, 1):
        for p in PARTS:
            p3s_wait(p, i)
            p3s(p, i + 2).start()
    consume(3, 0)
    consume(0, 1)
    consume(0, 2)
    forward(1)
    p3t_send(3)
    consume(1, 1)
    for p in PARTS:
        p3s_wait(p, 2)
        p3s_wait(p, 3)
        sib_s(p, c).start()
    opposite(0)
    consume(1, 2)
    early_ph[1]()
    early = ex_ph0[0]
    for i in range(1, 8):
        early = early + ex_ph0[i]
    teacher_scale = lax.rsqrt(jnp.concatenate([early[i : i + 1] for i in range(4)], axis=1) / DT + NORM_EPSILON)
    col[...] = to_columns([teacher_scale])
    for p in PARTS:
        sib_s(p, 1 - c).wait_recv()

    def slab(q):
        return pl.ds(pl.multiple_of(q * SLAB, SLAB), SLAB)

    def halves(q, z, y):
        ref = G.at[q % 2, q // 2, z, y]
        first = jnp.concatenate([ref[0:48, :], ref[208:224, :]], axis=0)
        second = jnp.concatenate([ref[224:256, :], ref[416:448, :]], axis=0)
        return first.astype(F32), second.astype(F32)

    def norm_slab(q, _):
        def squares(z, total):
            for y in range(4):
                first, second = halves(q, z, y)
                total = total + (first * first + second * second)
            return total

        total = lax.fori_loop(0, 4, squares, jnp.zeros((SLAB, 128), F32))
        scale = lax.rsqrt(rowsum(total) / DS + NORM_EPSILON)
        rows = slab(q)
        scale_s[rows, :] = scale
        wide_scale = jnp.broadcast_to(scale, (SLAB, 128))

        def normed(z, _):
            for y in range(4):
                t = 4 * z + y
                first, second = halves(q, z, y)
                xs[t, rows, 0:128] = (first * wide_scale * ex_tp0[t, 4:5, :]).astype(BF16)
                xs[t, rows, 128:256] = (second * wide_scale * ex_tp0[t, 5:6, :]).astype(BF16)
            return 0

        lax.fori_loop(0, 4, normed, 0)
        return 0

    lax.fori_loop(0, 4, norm_slab, 0)
    forward(2)
    lax.fori_loop(4, 8, norm_slab, 0)

    def student_dot(t):
        lhs = jnp.concatenate([xs[2 * t], xs[2 * t + 1]], axis=1)
        rhs = jnp.concatenate([ws[2 * t], ws[2 * t + 1]], axis=0)
        return jnp.dot(lhs, rhs, preferred_element_type=F32)

    def student_dots(t, _):
        sl[...] += student_dot(t)
        return 0

    def nt_dot(lhs, rhs):
        return lax.dot_general(lhs, rhs, (((1,), (1,)), ((), ())), preferred_element_type=F32)

    eye = (
        lax.broadcasted_iota(jnp.int32, (256, 256), 0) == lax.broadcasted_iota(jnp.int32, (256, 256), 1)
    ).astype(F32).astype(BF16)

    def xst_copy(t):
        return pltpu.make_async_copy(xst.at[t % 2], xst_out.at[t], out_sem.at[t % 2])

    def turn(t, _):
        @pl.when(t >= 2)
        def _():
            xst_copy(t - 2).wait()

        xst[t % 2] = nt_dot(eye, xs[t]).astype(BF16)
        xst_copy(t).start()
        return 0

    sl[...] = student_dot(0)
    lax.fori_loop(1, 8, student_dots, 0)
    opposite(1)
    consume(0, 3)
    lane = lax.broadcasted_iota(jnp.int32, (SLAB, 128), 1)
    vocab_first = ((ph * 16 + tp) * LOCAL_V).astype(F32)

    def label_hit(rows):
        ids = lax.broadcasted_iota(jnp.int32, (SLAB, LOCAL_V), 1).astype(F32) + vocab_first
        return lab[rows, 0:1] == ids

    def pack(columns, first, out):
        for i, column in enumerate(columns):
            out = jnp.where(lane == first + i, column, out)
        return out

    def student_stats(q, _):
        rows = slab(q)
        logits = sl[rows, :]
        top = jnp.max(logits, axis=1, keepdims=True)
        e = jnp.exp(logits - top)
        es[rows, :] = e
        picked = jnp.where(label_hit(rows), logits, 0.0)
        st[rows, :] = pack(
            [top, rowsum(e), rowsum(e * logits), rowsum(picked)], 4, jnp.zeros((SLAB, 128), F32)
        )
        return 0

    lax.fori_loop(0, 8, student_stats, 0)
    consume(2, 1)
    consume(2, 2)
    forward(3)
    lax.fori_loop(0, 16, turn, 0)
    consume(1, 3)
    opposite(2)
    consume(3, 1)
    consume(3, 2)
    consume(2, 3)
    opposite(3)
    products(3, 3, c)
    sib_wait(3, 3)
    products(3, 3, 1 - c)

    def teacher_stats(q, _):
        rows = slab(q)
        logits = acc_t[rows, :] * col[rows, 0:1]
        student = sl[rows, :]
        top = jnp.max(logits, axis=1, keepdims=True)
        e = jnp.exp(logits - top)
        acc_t[rows, :] = e
        st[rows, :] = pack([top, rowsum(e), rowsum(e * (logits - student)), rowsum(e * student)], 0, st[rows, :])
        return 0

    lax.fori_loop(0, 8, teacher_stats, 0)
    stats = jnp.transpose(st[...])[0:8, :]
    sub = lax.broadcasted_iota(jnp.int32, (8, TOKENS), 0)

    def merge(buf, count):
        t_top, s_top = buf[0, 0:1, :], buf[0, 4:5, :]
        for i in range(1, count):
            t_top = jnp.maximum(t_top, buf[i, 0:1, :])
            s_top = jnp.maximum(s_top, buf[i, 4:5, :])
        total = jnp.zeros((8, TOKENS), F32)
        for i in range(count):
            weight = jnp.where(sub < 4, jnp.exp(buf[i, 0:1, :] - t_top), jnp.exp(buf[i, 4:5, :] - s_top))
            total = total + buf[i] * jnp.where(sub == 7, 1.0, weight)
        return jnp.where(sub == 0, t_top, jnp.where(sub == 4, s_top, total))

    ex_tp1[tp] = stats
    late_tp[0]()
    late_tp[1]()
    ex_ph1[ph] = merge(ex_tp1, 16)
    late_ph[0]()
    late_ph[1]()
    late = merge(ex_ph1, 8)
    teacher_top, teacher_total, student_top, student_total = late[0:1], late[1:2], late[4:5], late[5:6]
    picked_all = late[7:8]
    teacher_lse = teacher_top + jnp.log(teacher_total)
    student_lse = student_top + jnp.log(student_total)
    loss = (
        late[2:3] / teacher_total - teacher_lse + student_lse + LABEL_WEIGHT * (student_lse - picked_all)
    )
    inner = (
        (1.0 + LABEL_WEIGHT) * late[6:7] / student_total - late[3:4] / teacher_total - LABEL_WEIGHT * picked_all
    )
    t_factor = jnp.exp(stats[0:1] - teacher_top) / teacher_total
    s_factor = (1.0 + LABEL_WEIGHT) * jnp.exp(stats[4:5] - student_top) / student_total
    col[...] = to_columns([t_factor, s_factor, inner])

    def logit_grad(n, which):
        q = 2 * n + (c if which == 0 else 1 - c)
        rows = slab(q)
        g = (
            es[rows, :] * col[rows, 1:2]
            - acc_t[rows, :] * col[rows, 0:1]
            - LABEL_WEIGHT * label_hit(rows).astype(F32)
        ).astype(BF16)
        g_ref[rows, :] = g
        gp[which, slab(n), :] = g

    for which in (1, 0):

        def grad_step(n, _, which=which):
            logit_grad(n, which)
            return 0

        lax.fori_loop(0, 4, grad_step, 0)
        if which == 1:
            gp_push = remote(gp.at[1], gp_in, misc_s.at[1], misc_r.at[1], sib)
            gp_push.start()
    g_copy = pltpu.make_async_copy(g_ref, g_out, out_sem.at[2])
    g_copy.start()

    def own_first(t, _):
        r = nt_dot(gp[0], ws[t])
        for xt in range(4):
            own[xt, t // 4, t % 4, 0:64] = r[xt * 64 : xt * 64 + 64, 0:128]
            own[xt, t // 4, t % 4, 64:128] = r[xt * 64 : xt * 64 + 64, 128:256]
        return 0

    def own_second(t, _):
        r = nt_dot(gp_in[...], ws_sib[t])
        for xt in range(4):
            for h in range(2):
                at = pl.ds(64 * h, 64)
                total = own[xt, t // 4, t % 4, at, :] + r[xt * 64 : xt * 64 + 64, 128 * h : 128 * h + 128]
                own[xt, t // 4, t % 4, at, :] = total
                wt[xt, 0, t // 4, t % 4, at, 0:128] = total.astype(BF16)
        return 0

    lax.fori_loop(0, 16, own_first, 0)
    ws_push.wait_recv()
    gp_push.wait_recv()
    lax.fori_loop(0, 16, own_second, 0)

    def at3(p, one, two, three):
        a, b, d = ORDER[p]
        at = {a: one, b: two, d: three}
        return at["x"], at["z"], at["y"]

    def rest(p, two, three):
        at = {ORDER[p][1]: two, ORDER[p][2]: three}
        return tuple(at[axis] for axis in ("x", "z", "y") if axis in at)

    def stage_ref(p, one, two, three):
        ix, iz, iy = at3(p, one, two, three)
        return wt.at[ix, 0, iz, iy, pl.ds(*RS_PART[p]), pl.ds(0, 128)]

    def own_ref(p, one, two, three):
        ix, iz, iy = at3(p, one, two, three)
        return own.at[ix, iz, iy, pl.ds(*RS_PART[p]), :]

    HOP = (2, 1, -1)
    SUBSET = (2, 1, -1, 0)

    def rs1(p, k, i):
        a, b, d = ORDER[p]
        two = rel(b, SUBSET[k])
        src = stage_ref(p, rel(a, HOP[i]), two, ALL)
        dst = rs_b.at[(i, *rest(p, two, ALL), pl.ds(*RS_PART[p]), ALL)]
        return remote(src, dst, rs_s.at[p, 3 * k + i], rs_r.at[p, 3 * k + i], near(a, HOP[i]))

    def rs1_wait(p, k, i):
        dst = rs_b.at[(i, *rest(p, rel(ORDER[p][1], SUBSET[k]), ALL), pl.ds(*RS_PART[p]), ALL)]
        remote(dst, dst, rs_s.at[p, 3 * k + i], rs_r.at[p, 3 * k + i], sib).wait_recv()

    def rs2(p, i):
        a, b, d = ORDER[p]
        src = stage_ref(p, me[a], rel(b, HOP[i]), ALL)
        dst = rs_c.at[i, :, pl.ds(*RS_PART[p]), :]
        return remote(src, dst, rs_s.at[p, 12 + i], rs_r.at[p, 12 + i], near(b, HOP[i]))

    def rs3(p, i):
        a, b, d = ORDER[p]
        src = stage_ref(p, me[a], me[b], rel(d, HOP[i]))
        dst = rs_d.at[i, pl.ds(*RS_PART[p]), :]
        return remote(src, dst, rs_s.at[p, 15 + i], rs_r.at[p, 15 + i], near(d, HOP[i]))

    for k in range(4):
        for p in PARTS:
            for i in range(3):
                rs1(p, k, i).start()
    for k in range(4):
        for p in PARTS:
            rows = pl.ds(*RS_PART[p])
            for i in range(3):
                rs1_wait(p, k, i)

            def add_first(n, _, p=p, k=k, rows=rows):
                two = rel(ORDER[p][1], SUBSET[k])
                ref = own_ref(p, me[ORDER[p][0]], two, n)
                total = ref[...]
                for i in range(3):
                    total = total + rs_b[(i, *rest(p, two, n), rows, ALL)].astype(F32)
                if k == 3:
                    ref[...] = total
                else:
                    stage_ref(p, me[ORDER[p][0]], two, n)[...] = total.astype(BF16)
                return 0

            lax.fori_loop(0, 4, add_first, 0)
            if k < 3:
                rs2(p, k).start()
    for p in PARTS:
        rows = pl.ds(*RS_PART[p])
        for i in range(3):
            rs2(p, i).wait_recv()

        def add_second(n, _, p=p, rows=rows):
            ref = own_ref(p, me[ORDER[p][0]], me[ORDER[p][1]], n)
            total = ref[...]
            for i in range(3):
                total = total + rs_c[i, n, rows, :].astype(F32)
            ref[...] = total
            stage_ref(p, me[ORDER[p][0]], me[ORDER[p][1]], n)[...] = total.astype(BF16)
            return 0

        lax.fori_loop(0, 4, add_second, 0)
        for i in range(3):
            rs3(p, i).start()
    for p in PARTS:
        rows = pl.ds(*RS_PART[p])
        for i in range(3):
            rs3(p, i).wait_recv()
        total = own_ref(p, *own_at(p))[...]
        for i in range(3):
            total = total + rs_d[i, rows, :].astype(F32)
        fin[rows, :] = total

    rows = slab(ph)
    scale = scale_s[rows, :]
    raw = s_rows[...].astype(F32)
    gain = s_gain[...].astype(F32)
    sums = []
    for h in range(2):
        sums.append(rowsum_tokens(fin[h * 64 : h * 64 + 64, :] * raw[:, h * 128 : h * 128 + 128] * scale))
    ex_gain[ph] = jnp.broadcast_to(jnp.concatenate(sums, axis=1), (8, 256))
    gain_ph[0]()
    coefficient = scale * scale * col[rows, 2:3] / DS
    for h in range(2):
        cols = pl.ds(h * 128, 128)
        grad = fin[h * 64 : h * 64 + 64, :]
        rows_out[:, cols] = (scale * gain[h : h + 1] * grad - raw[:, h * 128 : h * 128 + 128] * coefficient).astype(BF16)
    sl[0:8, :] = jnp.broadcast_to(loss, (8, TOKENS))
    window = sl[0:1, pl.ds(pl.multiple_of(me["x"] * 128, 128), 128)]
    loss_out[...] = jnp.where(c == 1, window[:, 64:128], window[:, 0:64])

    for p in PARTS:
        for i in range(3):
            p1(p, i).wait_send()
        for i in range(8):
            p2(p, i // 2, i % 2).wait_send()
        for i in range(2):
            p2f(p, i).wait_send()
        for i in range(4):
            p3s(p, i).wait_send()
        sib_s(p, c).wait_send()
        for j in range(4):
            for i in range(4):
                p3t(p, j, i).wait_send()
                sib_t(p, j, i).wait_send()
        for i in range(3):
            for k in range(4):
                rs1(p, k, i).wait_send()
            rs2(p, i).wait_send()
            rs3(p, i).wait_send()
    for ex in (early_tp, early_ph, late_tp, late_ph):
        ex[2]()
    ws_push.wait_send()
    gp_push.wait_send()
    xst_copy(14).wait()
    xst_copy(15).wait()
    g_copy.wait()
    gain_ph[1]()
    total = ex_gain[0]
    for i in range(1, 8):
        total = total + ex_gain[i]
    gain_out[...] = total[0:1]
    gain_ph[2]()


def rowsum_tokens(value):
    return jnp.sum(value, axis=0, keepdims=True)


def head_kernel(xst_ref, g_ref, out_ref):
    out_ref[...] = jnp.dot(
        xst_ref[...].reshape(512, TOKENS), g_ref[...], preferred_element_type=F32
    ).astype(BF16)


def local(teacher_rows, teacher_gain, teacher_head, student_rows, student_gain, student_head, labels):
    vmem = pl.BlockSpec(memory_space=pltpu.VMEM)
    hbm = pl.BlockSpec(memory_space=pl.ANY)
    dma = pltpu.SemaphoreType.DMA
    loss, rows_grad, gain_grad, xst, g = pl.pallas_call(
        comm_kernel,
        out_shape=(
            jax.ShapeDtypeStruct((1, SLAB), F32),
            jax.ShapeDtypeStruct((SLAB, 256), BF16),
            jax.ShapeDtypeStruct((1, 256), F32),
            jax.ShapeDtypeStruct((16, 256, TOKENS), BF16),
            jax.ShapeDtypeStruct((TOKENS, LOCAL_V), BF16),
        ),
        in_specs=[vmem, vmem, hbm, vmem, vmem, hbm, vmem],
        out_specs=(vmem, vmem, vmem, hbm, hbm),
        scratch_shapes=[
            pltpu.VMEM((2, 4, 4, 4, 640, 128), BF16),
            pltpu.VMEM((4, 2, 4, 4, 128, LOCAL_V), BF16),
            pltpu.VMEM((16, 256, LOCAL_V), BF16),
            pltpu.VMEM((16, 256, LOCAL_V), BF16),
            pltpu.VMEM((16, TOKENS, 256), BF16),
            pltpu.VMEM((2, 256, TOKENS), BF16),
            pltpu.VMEM((TOKENS, LOCAL_V), F32),
            pltpu.VMEM((TOKENS, LOCAL_V), F32),
            pltpu.VMEM((TOKENS, LOCAL_V), F32),
            pltpu.VMEM((TOKENS, 128), F32),
            pltpu.VMEM((TOKENS, 128), F32),
            pltpu.VMEM((TOKENS, 128), F32),
            pltpu.VMEM((TOKENS, 1), F32),
            pltpu.VMEM((TOKENS, LOCAL_V), BF16),
            pltpu.VMEM((2, 256, LOCAL_V), BF16),
            pltpu.VMEM((256, LOCAL_V), BF16),
            pltpu.VMEM((4, 4, 4, 128, 128), F32),
            pltpu.VMEM((3, 4, 4, 128, 128), BF16),
            pltpu.VMEM((3, 4, 128, 128), BF16),
            pltpu.VMEM((3, 128, 128), BF16),
            pltpu.VMEM((128, 128), F32),
            pltpu.VMEM((16, 8, 128), F32),
            pltpu.VMEM((8, 8, 128), F32),
            pltpu.VMEM((16, 8, TOKENS), F32),
            pltpu.VMEM((8, 8, TOKENS), F32),
            pltpu.VMEM((8, 8, 256), F32),
            dma((5,)), dma((3,)),
            dma((3, 3)), dma((3, 3)), dma((3, 8)), dma((3, 8)), dma((3, 2)), dma((3, 2)),
            dma((3, 4)), dma((3, 4)), dma((3, 16)), dma((3, 16)), dma((3,)), dma((3,)), dma((3, 16)), dma((3, 16)),
            dma((5, 16)), dma((5, 16)), dma((2,)), dma((2,)), dma((3, 18)), dma((3, 18)),
        ],
        compiler_params=pltpu.CompilerParams(
            collective_id=0, has_side_effects=True, vmem_limit_bytes=63 << 20
        ),
        name="distill",
    )(
        teacher_rows,
        teacher_gain.reshape(1, 128),
        teacher_head.reshape(4, 2, 4, 4, 128, LOCAL_V),
        student_rows,
        student_gain.reshape(2, 128),
        student_head.reshape(16, 256, LOCAL_V),
        labels.reshape(1, TOKENS),
    )
    head_grad = pl.pallas_call(
        head_kernel,
        grid=(8,),
        out_shape=jax.ShapeDtypeStruct((DS, LOCAL_V), BF16),
        in_specs=[
            pl.BlockSpec((2, 256, TOKENS), lambda t: (t, 0, 0)),
            pl.BlockSpec((TOKENS, LOCAL_V), lambda t: (0, 0)),
        ],
        out_specs=pl.BlockSpec((512, LOCAL_V), lambda t: (t, 0)),
        name="head_grad",
    )(xst, g)
    return loss.reshape(SLAB), head_grad, rows_grad, gain_grad.reshape(256)


def solution(mesh):
    placed = (
        P(None, ("phase", "tp")),
        P(("phase", "tp")),
        P(None, ("phase", "tp")),
        P("phase", "tp"),
        P("tp"),
        P(None, ("phase", "tp")),
        P(),
    )
    return jax.shard_map(
        local,
        mesh=mesh,
        in_specs=placed,
        out_specs=(P("phase"), P(None, ("phase", "tp")), P("phase", "tp"), P("tp")),
        check_vma=False,
    )
```

```python
import jax
import jax.numpy as jnp
from jax import lax
from jax.experimental import pallas as pl
from jax.experimental.pallas import tpu as pltpu
from jax.sharding import PartitionSpec as P

NORM_EPSILON = 1e-05
LABEL_WEIGHT = 0.5
F32 = jnp.float32
BF16 = jnp.bfloat16
MESH = pl.DeviceIdType.MESH

DT, DS, TOKENS, LOCAL_V = 16384, 4096, 512, 512
SLAB = 64
PART = ((0, 208), (208, 208), (416, 224))
PART_S = ((0, 48), (208, 48), (416, 32))
PART_T = ((48, 160), (256, 160), (448, 192))
TOKEN_T = (0, 160, 320)
ORDER = (("x", "y", "z"), ("y", "z", "x"), ("z", "x", "y"))
RS_PART = ((0, 48), (48, 48), (96, 32))
ALL = slice(None)
LOW, HIGH = pl.ds(0, 2), pl.ds(2, 2)


def comm_kernel(
    t_rows, t_gain, wt_hbm, s_rows, s_gain, ws_hbm, labels,
    loss_out, rows_out, gain_out, xst_out, g_out,
    G, wt, ws, ws_sib, xst, acc_t, sl, es, st, col, lab, scale_s, g_ref, gp, gp_in, own,
    rs_b, rs_c, rs_d, fin, ex_y0, ex_z0, ex_ph0, ex_tp1, ex_ph1, ex_gain,
    w_sem, out_sem, send, r1, r2, r2f, r1s, r2s, r3s, r3t, sibs_r, sibt_r, ex_s, ex_r, misc_s, misc_r, rs_r,
):
    ph = lax.axis_index("phase")
    tp = lax.axis_index("tp")
    c = ph % 2
    me = {"x": ph // 2, "y": tp % 4, "z": tp // 4}
    sib = (ph + 1 - 2 * c, tp)
    PARTS = range(3)
    STEP = (0, -1, 1, 2)

    def rel(axis, step):
        return (me[axis] + step + 4) % 4

    def near(axis, step):
        at = dict(me)
        at[axis] = rel(axis, step)
        return (at["x"] * 2 + c, at["z"] * 4 + at["y"])

    def remote(src, dst, ssem, rsem, to):
        return pltpu.make_async_remote_copy(
            src_ref=src, dst_ref=dst, send_sem=ssem, recv_sem=rsem, device_id=to, device_id_type=MESH
        )

    wt_loads = [pltpu.make_async_copy(wt_hbm.at[i], wt.at[i], w_sem.at[i]) for i in range(4)]
    ws_load = pltpu.make_async_copy(ws_hbm, ws, w_sem.at[4])
    ws_load.start()
    for load in wt_loads:
        load.start()

    barrier = pltpu.get_barrier_semaphore()
    partners = [sib] + [near(axis, step) for axis in "xyz" for step in (1, -1, 2)]
    for to in partners:
        pl.semaphore_signal(barrier, inc=1, device_id=to, device_id_type=MESH)

    mine = G.at[c, me["x"], me["z"], me["y"]]
    wide = t_rows[...].astype(F32)
    scaled = (wide * t_gain[...].astype(F32)).astype(BF16)
    for (row, size), token in zip(PART_T, TOKEN_T):
        mine[pl.ds(row, size), :] = scaled[token : token + size]
    pl.semaphore_wait(barrier, len(partners))

    def block(p, one, two, three, rows, core=None):
        a, b, d = ORDER[p]
        at = {a: one, b: two, d: three}
        return G.at[c if core is None else core, at["x"], at["z"], at["y"], pl.ds(*rows), :]

    def own_at(p):
        return tuple(me[axis] for axis in ORDER[p])

    def p1(p, i):
        ref = block(p, *own_at(p), PART_T[p])
        return remote(ref, ref, send.at[p, 0], r1.at[p, i], near(ORDER[p][0], (-1, 1, 2)[i]))

    def p2(p, n, i):
        a, b, d = ORDER[p]
        ref = block(p, rel(a, STEP[n]), me[b], me[d], PART_T[p])
        return remote(ref, ref, send.at[p, 1], r2.at[p, i], near(b, (1, -1)[i]))

    def p2f(p, i):
        a, b, d = ORDER[p]
        ref = block(p, (LOW, HIGH)[i], rel(b, (-1, 1)[i]), me[d], PART_T[p])
        return remote(ref, ref, send.at[p, 1], r2f.at[p, i], near(b, (1, -1)[i]))

    def p1s(p, i):
        ref = block(p, *own_at(p), PART_S[p])
        return remote(ref, ref, send.at[p, 2], r1s.at[p, i], near(ORDER[p][0], (-1, 1, 2)[i]))

    def p2s(p, i):
        a, b, d = ORDER[p]
        ref = block(p, ALL, me[b], me[d], PART_S[p])
        return remote(ref, ref, send.at[p, 2], r2s.at[p, i], near(b, (-1, 1, 2)[i]))

    def p3s(p, i):
        d = ORDER[p][2]
        ref = block(p, (ALL, ALL, LOW, HIGH)[i], ALL, rel(d, (0, 0, -1, 1)[i]), PART_S[p])
        return remote(ref, ref, send.at[p, 2], r3s.at[p, i], near(d, (1, -1, 1, -1)[i]))

    def p3t(p, j, i):
        a, b, d = ORDER[p]
        ref = block(p, (ALL, ALL, LOW, HIGH)[i], rel(b, STEP[j]), rel(d, (0, 0, -1, 1)[i]), PART_T[p])
        return remote(ref, ref, send.at[p, 3], r3t.at[p, 4 * j + i], near(d, (1, -1, 1, -1)[i]))

    def arrive(ref, sem):
        pltpu.make_async_copy(ref, ref, sem).wait()

    def p2_wait(p, i):
        a, b, d = ORDER[p]
        arrive(block(p, ALL, rel(b, (-1, 1)[i]), me[d], PART_T[p]), r2.at[p, i])

    def p2f_wait(p, i):
        a, b, d = ORDER[p]
        arrive(block(p, (LOW, HIGH)[i], rel(b, 2), me[d], PART_T[p]), r2f.at[p, i])

    def p1s_wait(p, i):
        a, b, d = ORDER[p]
        arrive(block(p, rel(a, (1, -1, 2)[i]), me[b], me[d], PART_S[p]), r1s.at[p, i])

    def p2s_wait(p, i):
        a, b, d = ORDER[p]
        arrive(block(p, ALL, rel(b, (1, -1, 2)[i]), me[d], PART_S[p]), r2s.at[p, i])

    def p3s_wait(p, i):
        d = ORDER[p][2]
        arrive(block(p, (ALL, ALL, LOW, HIGH)[i], ALL, rel(d, (-1, 1, 2, 2)[i]), PART_S[p]), r3s.at[p, i])

    def p3t_wait(p, j, i):
        a, b, d = ORDER[p]
        ref = block(p, (ALL, ALL, LOW, HIGH)[i], rel(b, STEP[j]), rel(d, (-1, 1, 2, 2)[i]), PART_T[p])
        arrive(ref, r3t.at[p, 4 * j + i])

    def sib_t(p, j, k, core=None):
        a, b, d = ORDER[p]
        ref = block(p, ALL, rel(b, STEP[j]), rel(d, STEP[k]), PART_T[p], core)
        return remote(ref, ref, send.at[p, 4], sibt_r.at[p, 4 * j + k], sib)

    def sib_s(p, core):
        ref = G.at[core, :, :, :, pl.ds(*PART_S[p]), :]
        return remote(ref, ref, send.at[p, 5], sibs_r.at[p], sib)

    def p3t_send(j):
        for p in PARTS:
            p3t(p, j, 0).start()
            p3t(p, j, 1).start()

    def products(j, k, core):
        for p in PARTS:
            a, b, d = ORDER[p]
            at = {a: ALL, b: rel(b, STEP[j]), d: rel(d, STEP[k])}
            rows = G[core, at["x"], at["z"], at["y"], pl.ds(*PART_T[p]), :]
            lhs = jnp.concatenate([rows[i] for i in range(4)], axis=1)
            rhs = wt[at["x"], core, at["z"], at["y"]].reshape(512, LOCAL_V)
            acc_t[pl.ds(TOKEN_T[p], PART_T[p][1]), :] += jnp.dot(lhs, rhs, preferred_element_type=F32)

    def sib_wait(j, k):
        for p in PARTS:
            a, b, d = ORDER[p]
            arrive(block(p, ALL, rel(b, STEP[j]), rel(d, STEP[k]), PART_T[p], 1 - c), sibt_r.at[p, 4 * j + k])

    def consume(j, k):
        sib_wait(j, k)

        def one_core(core, _):
            products(j, k, core)
            return 0

        lax.fori_loop(0, 2, one_core, 0)

    def rowsum(value):
        return jnp.sum(value, axis=1, keepdims=True)

    def to_tp(d):
        return (ph, (tp + d) % 16)

    def to_ph(d):
        return ((ph + d) % 8, tp)

    def exchange(buf, slot, count, number, to):
        def copy(d):
            return remote(buf.at[slot], buf.at[slot], ex_s.at[number], ex_r.at[number, d], to(d))

        def start():
            for d in range(1, count):
                copy(d).start()

        def wait():
            for d in range(1, count):
                copy(d).wait_recv()

        def sent():
            arrive(buf.at[pl.ds(0, count - 1)], ex_s.at[number])

        return start, wait, sent

    early_y = exchange(ex_y0, me["y"], 4, 0, lambda d: near("y", d))
    early_z = exchange(ex_z0, me["z"], 4, 5, lambda d: near("z", d))
    early_ph = exchange(ex_ph0, ph, 8, 1, to_ph)
    late_tp = exchange(ex_tp1, tp, 16, 2, to_tp)
    late_ph = exchange(ex_ph1, ph, 8, 3, to_ph)
    gain_ph = exchange(ex_gain, ph, 8, 4, to_ph)

    def to_columns(rows):
        filled = jnp.concatenate(rows + [jnp.zeros((128 - len(rows), TOKENS), F32)], axis=0)
        return jnp.transpose(filled)

    for i in range(3):
        for p in PARTS:
            p1(p, i).start()
    for p in PARTS:
        p2(p, 0, 0).start()
        p2(p, 0, 1).start()
    raw = s_rows[...].astype(F32)
    raw_squares = rowsum(raw * raw)
    lane_t = lax.broadcasted_iota(jnp.int32, (TOKENS, 128), 1)
    st[...] = jnp.where(lane_t == 0, rowsum(wide * wide), 0.0)
    st[0:SLAB, :] = jnp.where(lane_t[0:SLAB] == 1, raw_squares, st[0:SLAB, :])
    squares = jnp.transpose(st[...])
    ex_y0[me["y"]] = jnp.concatenate(
        [squares[0:1, 128 * i : 128 * i + 128] for i in range(4)]
        + [squares[1:2, 0:128], jnp.zeros((3, 128), F32)],
        axis=0,
    )
    early_y[0]()
    lab[...] = to_columns([labels[...].astype(F32)])
    acc_t[...] = jnp.zeros_like(acc_t)
    for n in (1, 2, 3):
        for p in PARTS:
            a, b, d = ORDER[p]
            arrive(block(p, rel(a, STEP[n]), me[b], me[d], PART_T[p]), r1.at[p, (1, 0, 2)[n - 1]])
            p2(p, n, 0).start()
            p2(p, n, 1).start()
    p3t_send(0)
    early_y[1]()
    ex_z0[me["z"]] = ex_y0[0] + ex_y0[1] + ex_y0[2] + ex_y0[3]
    early_z[0]()
    for p in PARTS:
        sib_t(p, 0, 0).start()
    for i in (0, 1):
        for p in PARTS:
            p2_wait(p, i)
            p2f(p, i).start()
            sib_t(p, i + 1, 0).start()
    early_z[1]()
    early = ex_z0[0] + ex_z0[1] + ex_z0[2] + ex_z0[3]
    ex_ph0[ph] = early
    turned = jnp.transpose(jnp.concatenate([early, jnp.zeros((120, 128), F32)], axis=0))
    own_scale = lax.rsqrt(turned[0:SLAB, 4:5] / DS + NORM_EPSILON)
    scale_s[...] = own_scale
    gain = s_gain[...].astype(F32)
    left = (raw[:, 0:128] * own_scale * gain[0:1]).astype(BF16)
    right = (raw[:, 128:256] * own_scale * gain[1:2]).astype(BF16)
    mine[0:48, :] = left[0:48]
    mine[208:224, :] = left[48:64]
    mine[224:256, :] = right[0:32]
    mine[416:448, :] = right[32:64]
    for i in range(3):
        for p in PARTS:
            p1s(p, i).start()
    for p in PARTS:
        p2f_wait(p, 0)
        p2f_wait(p, 1)
        sib_t(p, 3, 0).start()
    p3t_send(1)
    ws_load.wait()
    ws_push = remote(ws, ws_sib, misc_s.at[0], misc_r.at[0], sib)
    ws_push.start()
    for load in wt_loads:
        load.wait()
    for p in PARTS:
        for i in range(3):
            p1s_wait(p, i)
        for i in range(3):
            p2s(p, i).start()
    consume(0, 0)

    def forward(j):
        for i in (0, 1):
            for p in PARTS:
                p3t_wait(p, j, i)
                p3t(p, j, i + 2).start()
                sib_t(p, j, i + 1).start()

    def opposite(j):
        for p in PARTS:
            p3t_wait(p, j, 2)
            p3t_wait(p, j, 3)
            sib_t(p, j, 3).start()

    forward(0)
    consume(1, 0)
    for p in PARTS:
        for i in range(3):
            p2s_wait(p, i)
        p3s(p, 0).start()
        p3s(p, 1).start()
    p3t_send(2)
    early_ph[0]()
    consume(2, 0)
    consume(3, 0)
    forward(1)
    for i in (0, 1):
        for p in PARTS:
            p3s_wait(p, i)
            p3s(p, i + 2).start()
    p3t_send(3)
    consume(0, 1)
    consume(0, 2)
    opposite(0)
    consume(1, 1)
    early_ph[1]()
    early = ex_ph0[0]
    for i in range(1, 8):
        early = early + ex_ph0[i]
    teacher_scale = lax.rsqrt(jnp.concatenate([early[i : i + 1] for i in range(4)], axis=1) / DT + NORM_EPSILON)
    col[...] = to_columns([teacher_scale])
    for p in PARTS:
        p3s_wait(p, 2)
        p3s_wait(p, 3)
        sib_s(p, c).start()
    consume(1, 2)
    consume(0, 3)
    for p in PARTS:
        arrive(G.at[1 - c, :, :, :, pl.ds(*PART_S[p]), :], sibs_r.at[p])

    def slab(q):
        return pl.ds(pl.multiple_of(q * SLAB, SLAB), SLAB)

    def normed(z, y):
        slabs = []
        for q in range(8):
            ref = G.at[q % 2, q // 2, z, y]
            first = jnp.concatenate([ref[0:48, :], ref[208:224, :]], axis=0)
            second = jnp.concatenate([ref[224:256, :], ref[416:448, :]], axis=0)
            slabs.append(jnp.concatenate([first, second], axis=1))
        return jnp.concatenate(slabs, axis=0)

    def student_dot(z, half):
        t = 4 * z + 2 * half
        lhs = jnp.concatenate([normed(z, 2 * half), normed(z, 2 * half + 1)], axis=1)
        rhs = jnp.concatenate([ws[t], ws[t + 1]], axis=0)
        return jnp.dot(lhs, rhs, preferred_element_type=F32)

    def student_dots(z, _):
        sl[...] += student_dot(z, 0)
        sl[...] += student_dot(z, 1)
        return 0

    def nt_dot(lhs, rhs):
        return lax.dot_general(lhs, rhs, (((1,), (1,)), ((), ())), preferred_element_type=F32)

    eye = (
        lax.broadcasted_iota(jnp.int32, (256, 256), 0) == lax.broadcasted_iota(jnp.int32, (256, 256), 1)
    ).astype(F32).astype(BF16)

    def xst_copy(t):
        return pltpu.make_async_copy(xst.at[t % 2], xst_out.at[t], out_sem.at[t % 2])

    def turn(z, _):
        for y in range(4):
            t = 4 * z + y
            if y >= 2:
                xst_copy(t - 2).wait()
            else:

                @pl.when(z >= 1)
                def _(t=t):
                    xst_copy(t - 2).wait()

            xst[t % 2] = nt_dot(eye, normed(z, y)).astype(BF16)
            xst_copy(t).start()
        return 0

    sl[...] = student_dot(0, 0)
    sl[...] += student_dot(0, 1)
    forward(2)
    lax.fori_loop(1, 4, student_dots, 0)
    opposite(1)
    lane = lax.broadcasted_iota(jnp.int32, (SLAB, 128), 1)
    vocab_first = ((ph * 16 + tp) * LOCAL_V).astype(F32)

    def label_hit(rows):
        ids = lax.broadcasted_iota(jnp.int32, (SLAB, LOCAL_V), 1).astype(F32) + vocab_first
        return lab[rows, 0:1] == ids

    def pack(columns, first, out):
        for i, column in enumerate(columns):
            out = jnp.where(lane == first + i, column, out)
        return out

    def student_stats(q, _):
        rows = slab(q)
        logits = sl[rows, :]
        top = jnp.max(logits, axis=1, keepdims=True)
        e = jnp.exp(logits - top)
        es[rows, :] = e
        picked = jnp.where(label_hit(rows), logits, 0.0)
        st[rows, :] = pack(
            [top, rowsum(e), rowsum(e * logits), rowsum(picked)], 4, jnp.zeros((SLAB, 128), F32)
        )
        return 0

    lax.fori_loop(0, 8, student_stats, 0)
    consume(2, 1)
    consume(2, 2)
    forward(3)
    consume(1, 3)
    opposite(2)
    consume(3, 1)
    consume(3, 2)
    consume(2, 3)
    opposite(3)
    products(3, 3, c)
    sib_wait(3, 3)
    products(3, 3, 1 - c)

    def teacher_stats(q, _):
        rows = slab(q)
        logits = acc_t[rows, :] * col[rows, 0:1]
        student = sl[rows, :]
        top = jnp.max(logits, axis=1, keepdims=True)
        e = jnp.exp(logits - top)
        acc_t[rows, :] = e
        st[rows, :] = pack([top, rowsum(e), rowsum(e * (logits - student)), rowsum(e * student)], 0, st[rows, :])
        return 0

    lax.fori_loop(0, 8, teacher_stats, 0)
    stats = jnp.transpose(st[...])[0:8, :]
    sub = lax.broadcasted_iota(jnp.int32, (8, TOKENS), 0)

    def merge(buf, count):
        t_top, s_top = buf[0, 0:1, :], buf[0, 4:5, :]
        for i in range(1, count):
            t_top = jnp.maximum(t_top, buf[i, 0:1, :])
            s_top = jnp.maximum(s_top, buf[i, 4:5, :])
        total = jnp.zeros((8, TOKENS), F32)
        for i in range(count):
            weight = jnp.where(sub < 4, jnp.exp(buf[i, 0:1, :] - t_top), jnp.exp(buf[i, 4:5, :] - s_top))
            total = total + buf[i] * jnp.where(sub == 7, 1.0, weight)
        return jnp.where(sub == 0, t_top, jnp.where(sub == 4, s_top, total))

    ex_tp1[tp] = stats
    late_tp[0]()
    late_tp[1]()
    ex_ph1[ph] = merge(ex_tp1, 16)
    late_ph[0]()
    late_ph[1]()
    late = merge(ex_ph1, 8)
    teacher_top, teacher_total, student_top, student_total = late[0:1], late[1:2], late[4:5], late[5:6]
    picked_all = late[7:8]
    teacher_lse = teacher_top + jnp.log(teacher_total)
    student_lse = student_top + jnp.log(student_total)
    loss = (
        late[2:3] / teacher_total - teacher_lse + student_lse + LABEL_WEIGHT * (student_lse - picked_all)
    )
    inner = (
        (1.0 + LABEL_WEIGHT) * late[6:7] / student_total - late[3:4] / teacher_total - LABEL_WEIGHT * picked_all
    )
    t_factor = jnp.exp(stats[0:1] - teacher_top) / teacher_total
    s_factor = (1.0 + LABEL_WEIGHT) * jnp.exp(stats[4:5] - student_top) / student_total
    col[...] = to_columns([t_factor, s_factor, inner])

    def logit_grad(n, which):
        q = 2 * n + (c if which == 0 else 1 - c)
        rows = slab(q)
        g = (
            es[rows, :] * col[rows, 1:2]
            - acc_t[rows, :] * col[rows, 0:1]
            - LABEL_WEIGHT * label_hit(rows).astype(F32)
        ).astype(BF16)
        g_ref[rows, :] = g
        gp[which, slab(n), :] = g

    for which in (1, 0):

        def grad_step(n, _, which=which):
            logit_grad(n, which)
            return 0

        lax.fori_loop(0, 4, grad_step, 0)
        if which == 1:
            gp_push = remote(gp.at[1], gp_in, misc_s.at[1], misc_r.at[1], sib)
            gp_push.start()
    g_copy = pltpu.make_async_copy(g_ref, g_out, out_sem.at[2])
    g_copy.start()

    def own_first(z, _):
        for y in range(4):
            r = nt_dot(gp[0], ws[4 * z + y])
            for xt in range(4):
                own[xt, z, y, 0:64] = r[xt * 64 : xt * 64 + 64, 0:128]
                own[xt, z, y, 64:128] = r[xt * 64 : xt * 64 + 64, 128:256]
        return 0

    def own_second(z):
        for y in range(4):
            r = nt_dot(gp_in[...], ws_sib[4 * z + y])
            for xt in range(4):
                for h in range(2):
                    at = pl.ds(64 * h, 64)
                    total = own[xt, z, y, at, :] + r[xt * 64 : xt * 64 + 64, 128 * h : 128 * h + 128]
                    own[xt, z, y, at, :] = total
                    wt[xt, 0, z, y, at, 0:128] = total.astype(BF16)

    lax.fori_loop(0, 4, own_first, 0)
    ws_push.wait_recv()
    gp_push.wait_recv()

    def at3(p, one, two, three):
        a, b, d = ORDER[p]
        at = {a: one, b: two, d: three}
        return at["x"], at["z"], at["y"]

    def rest(p, two, three):
        at = {ORDER[p][1]: two, ORDER[p][2]: three}
        return tuple(at[axis] for axis in ("x", "z", "y") if axis in at)

    def stage_ref(p, one, two, three):
        ix, iz, iy = at3(p, one, two, three)
        return wt.at[ix, 0, iz, iy, pl.ds(*RS_PART[p]), pl.ds(0, 128)]

    def own_ref(p, one, two, three):
        ix, iz, iy = at3(p, one, two, three)
        return own.at[ix, iz, iy, pl.ds(*RS_PART[p]), :]

    HOP = (2, 1, -1)
    SUBSET = (2, 1, -1, 0)

    def rs1(p, k, i):
        a, b, d = ORDER[p]
        two = rel(b, SUBSET[k])
        src = stage_ref(p, rel(a, HOP[i]), two, ALL)
        dst = rs_b.at[(i, *rest(p, two, ALL), pl.ds(*RS_PART[p]), ALL)]
        return remote(src, dst, send.at[p, 6], rs_r.at[p, 3 * k + i], near(a, HOP[i]))

    def rs1_wait(p, k, i):
        dst = rs_b.at[(i, *rest(p, rel(ORDER[p][1], SUBSET[k]), ALL), pl.ds(*RS_PART[p]), ALL)]
        arrive(dst, rs_r.at[p, 3 * k + i])

    def rs2(p, i):
        a, b, d = ORDER[p]
        src = stage_ref(p, me[a], rel(b, HOP[i]), ALL)
        dst = rs_c.at[i, :, pl.ds(*RS_PART[p]), :]
        return remote(src, dst, send.at[p, 7], rs_r.at[p, 12 + i], near(b, HOP[i]))

    def rs3(p, i):
        a, b, d = ORDER[p]
        src = stage_ref(p, me[a], me[b], rel(d, HOP[i]))
        dst = rs_d.at[i, pl.ds(*RS_PART[p]), :]
        return remote(src, dst, send.at[p, 8], rs_r.at[p, 15 + i], near(d, HOP[i]))

    for k in range(4):
        own_second(rel("z", SUBSET[k]))
        for i in range(3):
            rs1(1, k, i).start()
        if k < 3:
            for m in range(4):
                rs1(2, m, k).start()
    for k in range(4):
        for i in range(3):
            rs1(0, k, i).start()
    lax.fori_loop(0, 4, turn, 0)
    for k in range(4):
        for p in PARTS:
            rows = pl.ds(*RS_PART[p])
            for i in range(3):
                rs1_wait(p, k, i)

            def add_first(n, _, p=p, k=k, rows=rows):
                two = rel(ORDER[p][1], SUBSET[k])
                ref = own_ref(p, me[ORDER[p][0]], two, n)
                total = ref[...]
                for i in range(3):
                    total = total + rs_b[(i, *rest(p, two, n), rows, ALL)].astype(F32)
                if k == 3:
                    ref[...] = total
                else:
                    stage_ref(p, me[ORDER[p][0]], two, n)[...] = total.astype(BF16)
                return 0

            lax.fori_loop(0, 4, add_first, 0)
            if k < 3:
                rs2(p, k).start()
    for p in PARTS:
        rows = pl.ds(*RS_PART[p])
        for i in range(3):
            arrive(rs_c.at[i, :, rows, :], rs_r.at[p, 12 + i])

        def add_second(n, _, p=p, rows=rows):
            ref = own_ref(p, me[ORDER[p][0]], me[ORDER[p][1]], n)
            total = ref[...]
            for i in range(3):
                total = total + rs_c[i, n, rows, :].astype(F32)
            ref[...] = total
            stage_ref(p, me[ORDER[p][0]], me[ORDER[p][1]], n)[...] = total.astype(BF16)
            return 0

        lax.fori_loop(0, 4, add_second, 0)
        for i in range(3):
            rs3(p, i).start()
    for p in PARTS:
        rows = pl.ds(*RS_PART[p])
        for i in range(3):
            arrive(rs_d.at[i, rows, :], rs_r.at[p, 15 + i])
        total = own_ref(p, *own_at(p))[...]
        for i in range(3):
            total = total + rs_d[i, rows, :].astype(F32)
        fin[rows, :] = total

    rows = slab(ph)
    scale = scale_s[...]
    sums = []
    for h in range(2):
        sums.append(rowsum_tokens(fin[h * 64 : h * 64 + 64, :] * raw[:, h * 128 : h * 128 + 128] * scale))
    ex_gain[ph] = jnp.broadcast_to(jnp.concatenate(sums, axis=1), (8, 256))
    gain_ph[0]()
    coefficient = scale * scale * col[rows, 2:3] / DS
    for h in range(2):
        cols = pl.ds(h * 128, 128)
        grad = fin[h * 64 : h * 64 + 64, :]
        rows_out[:, cols] = (scale * gain[h : h + 1] * grad - raw[:, h * 128 : h * 128 + 128] * coefficient).astype(BF16)
    sl[0:8, :] = jnp.broadcast_to(loss, (8, TOKENS))
    window = sl[0:1, pl.ds(pl.multiple_of(me["x"] * 128, 128), 128)]
    loss_out[...] = jnp.where(c == 1, window[:, 64:128], window[:, 0:64])

    for p in PARTS:
        rows = pl.ds(*PART_T[p])
        arrive(G.at[0, 0, 0, 0:3, rows, :], send.at[p, 0])
        arrive(G.at[0, 0:3, 0, :, rows, :], send.at[p, 1])
        arrive(G.at[0, 0:3, :, :, rows, :], send.at[p, 3])
        arrive(G.at[0, :, :, :, rows, :], send.at[p, 4])
        rows = pl.ds(*PART_S[p])
        arrive(G.at[0, 0:3, :, :, rows, :], send.at[p, 2])
        arrive(G.at[0, 0:3, 0:1, :, rows, :], send.at[p, 2])
        arrive(G.at[0, 0, 0, 0:3, rows, :], send.at[p, 2])
        arrive(G.at[0, :, :, :, rows, :], send.at[p, 5])
        rows = pl.ds(*RS_PART[p])
        arrive(rs_b.at[:, :, :, rows, :], send.at[p, 6])
        arrive(rs_c.at[:, :, rows, :], send.at[p, 7])
        arrive(rs_d.at[:, rows, :], send.at[p, 8])
    for ex in (early_y, early_z, early_ph, late_tp, late_ph):
        ex[2]()
    ws_push.wait_send()
    gp_push.wait_send()
    xst_copy(14).wait()
    xst_copy(15).wait()
    g_copy.wait()
    gain_ph[1]()
    total = ex_gain[0]
    for i in range(1, 8):
        total = total + ex_gain[i]
    gain_out[...] = total[0:1]
    gain_ph[2]()


def rowsum_tokens(value):
    return jnp.sum(value, axis=0, keepdims=True)


def head_kernel(
    xst_hbm, g_hbm, loss_in, rows_in, gain_in, out_hbm, loss_out, rows_out, gain_out, xst, g, out, in_sem, out_sem
):
    g_load = pltpu.make_async_copy(g_hbm, g, in_sem.at[8])
    g_load.start()
    loads = [
        pltpu.make_async_copy(xst_hbm.at[pl.ds(2 * i, 2)], xst.at[pl.ds(2 * i, 2)], in_sem.at[i]) for i in range(8)
    ]
    stores = [
        pltpu.make_async_copy(out.at[pl.ds(512 * i, 512)], out_hbm.at[pl.ds(512 * i, 512)], out_sem.at[i])
        for i in range(8)
    ]
    for load in loads:
        load.start()
    loss_out[...] = loss_in[...]
    rows_out[...] = rows_in[...]
    gain_out[...] = gain_in[...]
    g_load.wait()
    for i in range(8):
        loads[i].wait()
        out[512 * i : 512 * i + 512, :] = jnp.dot(
            xst[2 * i : 2 * i + 2].reshape(512, TOKENS), g[...], preferred_element_type=F32
        ).astype(BF16)
        stores[i].start()
    for store in stores:
        store.wait()


def local(teacher_rows, teacher_gain, teacher_head, student_rows, student_gain, student_head, labels):
    vmem = pl.BlockSpec(memory_space=pltpu.VMEM)
    hbm = pl.BlockSpec(memory_space=pl.ANY)
    dma = pltpu.SemaphoreType.DMA
    loss, rows_grad, gain_grad, xst, g = pl.pallas_call(
        comm_kernel,
        out_shape=(
            jax.ShapeDtypeStruct((1, SLAB), F32),
            jax.ShapeDtypeStruct((SLAB, 256), BF16),
            jax.ShapeDtypeStruct((1, 256), F32),
            jax.ShapeDtypeStruct((16, 256, TOKENS), BF16),
            jax.ShapeDtypeStruct((TOKENS, LOCAL_V), BF16),
        ),
        in_specs=[vmem, vmem, hbm, vmem, vmem, hbm, vmem],
        out_specs=(vmem, vmem, vmem, hbm, hbm),
        scratch_shapes=[
            pltpu.VMEM((2, 4, 4, 4, 640, 128), BF16),
            pltpu.VMEM((4, 2, 4, 4, 128, LOCAL_V), BF16),
            pltpu.VMEM((16, 256, LOCAL_V), BF16),
            pltpu.VMEM((16, 256, LOCAL_V), BF16),
            pltpu.VMEM((2, 256, TOKENS), BF16),
            pltpu.VMEM((TOKENS, LOCAL_V), F32),
            pltpu.VMEM((TOKENS, LOCAL_V), F32),
            pltpu.VMEM((TOKENS, LOCAL_V), F32),
            pltpu.VMEM((TOKENS, 128), F32),
            pltpu.VMEM((TOKENS, 128), F32),
            pltpu.VMEM((TOKENS, 128), F32),
            pltpu.VMEM((SLAB, 1), F32),
            pltpu.VMEM((TOKENS, LOCAL_V), BF16),
            pltpu.VMEM((2, 256, LOCAL_V), BF16),
            pltpu.VMEM((256, LOCAL_V), BF16),
            pltpu.VMEM((4, 4, 4, 128, 128), F32),
            pltpu.VMEM((3, 4, 4, 128, 128), BF16),
            pltpu.VMEM((3, 4, 128, 128), BF16),
            pltpu.VMEM((3, 128, 128), BF16),
            pltpu.VMEM((128, 128), F32),
            pltpu.VMEM((4, 8, 128), F32),
            pltpu.VMEM((4, 8, 128), F32),
            pltpu.VMEM((8, 8, 128), F32),
            pltpu.VMEM((16, 8, TOKENS), F32),
            pltpu.VMEM((8, 8, TOKENS), F32),
            pltpu.VMEM((8, 8, 256), F32),
            dma((5,)), dma((3,)), dma((3, 9)),
            dma((3, 3)), dma((3, 2)), dma((3, 2)), dma((3, 3)), dma((3, 3)), dma((3, 4)), dma((3, 16)),
            dma((3,)), dma((3, 16)), dma((6,)), dma((6, 16)), dma((2,)), dma((2,)), dma((3, 18)),
        ],
        compiler_params=pltpu.CompilerParams(
            collective_id=0, has_side_effects=True, vmem_limit_bytes=63 << 20
        ),
        name="distill",
    )(
        teacher_rows,
        teacher_gain.reshape(1, 128),
        teacher_head.reshape(4, 2, 4, 4, 128, LOCAL_V),
        student_rows,
        student_gain.reshape(2, 128),
        student_head.reshape(16, 256, LOCAL_V),
        labels.reshape(1, TOKENS),
    )
    head_grad, loss, rows_grad, gain_grad = pl.pallas_call(
        head_kernel,
        out_shape=(
            jax.ShapeDtypeStruct((DS, LOCAL_V), BF16),
            jax.ShapeDtypeStruct((1, SLAB), F32),
            jax.ShapeDtypeStruct((SLAB, 256), BF16),
            jax.ShapeDtypeStruct((1, 256), F32),
        ),
        in_specs=[hbm, hbm, vmem, vmem, vmem],
        out_specs=(hbm, vmem, vmem, vmem),
        scratch_shapes=[
            pltpu.VMEM((16, 256, TOKENS), BF16),
            pltpu.VMEM((TOKENS, LOCAL_V), BF16),
            pltpu.VMEM((DS, LOCAL_V), BF16),
            dma((9,)),
            dma((8,)),
        ],
        compiler_params=pltpu.CompilerParams(vmem_limit_bytes=32 << 20),
        name="head_grad",
    )(xst, g, loss, rows_grad, gain_grad)
    return loss.reshape(SLAB), head_grad, rows_grad, gain_grad.reshape(256)


def solution(mesh):
    placed = (
        P(None, ("phase", "tp")),
        P(("phase", "tp")),
        P(None, ("phase", "tp")),
        P("phase", "tp"),
        P("tp"),
        P(None, ("phase", "tp")),
        P(),
    )
    return jax.shard_map(
        local,
        mesh=mesh,
        in_specs=placed,
        out_specs=(P("phase"), P(None, ("phase", "tp")), P("phase", "tp"), P("tp")),
        check_vma=False,
    )
```

```python
import jax
import jax.numpy as jnp
from jax import lax
from jax.experimental import pallas as pl
from jax.experimental.pallas import tpu as pltpu
from jax.sharding import PartitionSpec as P

NORM_EPSILON = 1e-05
LABEL_WEIGHT = 0.5
F32 = jnp.float32
BF16 = jnp.bfloat16
MESH = pl.DeviceIdType.MESH

DT, DS, TOKENS, LOCAL_V = 16384, 4096, 512, 512
SLAB = 64
PART = ((0, 208), (208, 208), (416, 224))
PART_S = ((0, 48), (208, 48), (416, 32))
PART_T = ((48, 160), (256, 160), (448, 192))
TOKEN_T = (0, 160, 320)
ORDER = (("x", "y", "z"), ("y", "z", "x"), ("z", "x", "y"))
RS_PART = ((0, 48), (48, 48), (96, 32))
ALL = slice(None)
LOW, HIGH = pl.ds(0, 2), pl.ds(2, 2)


def comm_kernel(
    t_rows, t_gain, wt_hbm, s_rows, s_gain, ws_hbm, labels,
    loss_out, rows_out, gain_out, head_out,
    G, wt, ws, ws_sib, head_part, acc_t, sl, es, st, col, lab, scale_s, g_ref, gp, gp_in, own,
    rs_b, rs_c, rs_d, fin, ex_y0, ex_z0, ex_ph0, ex_tp1, ex_ph1, gain_col, gain_own, ex_gain, ex_gain_ph,
    w_sem, out_sem, send, r1, r2, r2f, r1s, r2s, r3s, r3t, sibs_r, sibt_r, ex_s, ex_r, misc_s, misc_r, rs_r,
):
    ph = lax.axis_index("phase")
    tp = lax.axis_index("tp")
    c = ph % 2
    me = {"x": ph // 2, "y": tp % 4, "z": tp // 4}
    sib = (ph + 1 - 2 * c, tp)
    PARTS = range(3)
    STEP = (0, -1, 1, 2)

    def rel(axis, step):
        return (me[axis] + step + 4) % 4

    def near(axis, step):
        at = dict(me)
        at[axis] = rel(axis, step)
        return (at["x"] * 2 + c, at["z"] * 4 + at["y"])

    def remote(src, dst, ssem, rsem, to):
        return pltpu.make_async_remote_copy(
            src_ref=src, dst_ref=dst, send_sem=ssem, recv_sem=rsem, device_id=to, device_id_type=MESH
        )

    wt_loads = [pltpu.make_async_copy(wt_hbm.at[i], wt.at[i], w_sem.at[i]) for i in range(4)]
    ws_load = pltpu.make_async_copy(ws_hbm, ws, w_sem.at[4])
    ws_load.start()
    for load in wt_loads:
        load.start()

    barrier = pltpu.get_barrier_semaphore()
    partners = [sib] + [near(axis, step) for axis in "xyz" for step in (1, -1, 2)]
    for to in partners:
        pl.semaphore_signal(barrier, inc=1, device_id=to, device_id_type=MESH)

    mine = G.at[c, me["x"], me["z"], me["y"]]
    wide = t_rows[...].astype(F32)
    scaled = (wide * t_gain[...].astype(F32)).astype(BF16)
    for (row, size), token in zip(PART_T, TOKEN_T):
        mine[pl.ds(row, size), :] = scaled[token : token + size]
    pl.semaphore_wait(barrier, len(partners))

    def block(p, one, two, three, rows, core=None):
        a, b, d = ORDER[p]
        at = {a: one, b: two, d: three}
        return G.at[c if core is None else core, at["x"], at["z"], at["y"], pl.ds(*rows), :]

    def own_at(p):
        return tuple(me[axis] for axis in ORDER[p])

    def p1(p, i):
        ref = block(p, *own_at(p), PART_T[p])
        return remote(ref, ref, send.at[p, 0], r1.at[p, i], near(ORDER[p][0], (-1, 1, 2)[i]))

    def p2(p, n, i):
        a, b, d = ORDER[p]
        ref = block(p, rel(a, STEP[n]), me[b], me[d], PART_T[p])
        return remote(ref, ref, send.at[p, 1], r2.at[p, i], near(b, (1, -1)[i]))

    def p2f(p, i):
        a, b, d = ORDER[p]
        ref = block(p, (LOW, HIGH)[i], rel(b, (-1, 1)[i]), me[d], PART_T[p])
        return remote(ref, ref, send.at[p, 1], r2f.at[p, i], near(b, (1, -1)[i]))

    def p1s(p, i):
        ref = block(p, *own_at(p), PART_S[p])
        return remote(ref, ref, send.at[p, 2], r1s.at[p, i], near(ORDER[p][0], (-1, 1, 2)[i]))

    def p2s(p, i):
        a, b, d = ORDER[p]
        ref = block(p, ALL, me[b], me[d], PART_S[p])
        return remote(ref, ref, send.at[p, 2], r2s.at[p, i], near(b, (-1, 1, 2)[i]))

    def p3s(p, i):
        d = ORDER[p][2]
        ref = block(p, (ALL, ALL, LOW, HIGH)[i], ALL, rel(d, (0, 0, -1, 1)[i]), PART_S[p])
        return remote(ref, ref, send.at[p, 2], r3s.at[p, i], near(d, (1, -1, 1, -1)[i]))

    def p3t(p, j, i):
        a, b, d = ORDER[p]
        ref = block(p, (ALL, ALL, LOW, HIGH)[i], rel(b, STEP[j]), rel(d, (0, 0, -1, 1)[i]), PART_T[p])
        return remote(ref, ref, send.at[p, 3], r3t.at[p, 4 * j + i], near(d, (1, -1, 1, -1)[i]))

    def arrive(ref, sem):
        pltpu.make_async_copy(ref, ref, sem).wait()

    def p2_wait(p, i):
        a, b, d = ORDER[p]
        arrive(block(p, ALL, rel(b, (-1, 1)[i]), me[d], PART_T[p]), r2.at[p, i])

    def p2f_wait(p, i):
        a, b, d = ORDER[p]
        arrive(block(p, (LOW, HIGH)[i], rel(b, 2), me[d], PART_T[p]), r2f.at[p, i])

    def p1s_wait(p, i):
        a, b, d = ORDER[p]
        arrive(block(p, rel(a, (1, -1, 2)[i]), me[b], me[d], PART_S[p]), r1s.at[p, i])

    def p2s_wait(p, i):
        a, b, d = ORDER[p]
        arrive(block(p, ALL, rel(b, (1, -1, 2)[i]), me[d], PART_S[p]), r2s.at[p, i])

    def p3s_wait(p, i):
        d = ORDER[p][2]
        arrive(block(p, (ALL, ALL, LOW, HIGH)[i], ALL, rel(d, (-1, 1, 2, 2)[i]), PART_S[p]), r3s.at[p, i])

    def p3t_wait(p, j, i):
        a, b, d = ORDER[p]
        ref = block(p, (ALL, ALL, LOW, HIGH)[i], rel(b, STEP[j]), rel(d, (-1, 1, 2, 2)[i]), PART_T[p])
        arrive(ref, r3t.at[p, 4 * j + i])

    def sib_t(p, j, k, core=None):
        a, b, d = ORDER[p]
        ref = block(p, ALL, rel(b, STEP[j]), rel(d, STEP[k]), PART_T[p], core)
        return remote(ref, ref, send.at[p, 4], sibt_r.at[p, 4 * j + k], sib)

    def sib_s(p, core):
        ref = G.at[core, :, :, :, pl.ds(*PART_S[p]), :]
        return remote(ref, ref, send.at[p, 5], sibs_r.at[p], sib)

    def p3t_send(j):
        for p in PARTS:
            p3t(p, j, 0).start()
            p3t(p, j, 1).start()

    def products(j, k, core):
        for p in PARTS:
            a, b, d = ORDER[p]
            at = {a: ALL, b: rel(b, STEP[j]), d: rel(d, STEP[k])}
            rows = G[core, at["x"], at["z"], at["y"], pl.ds(*PART_T[p]), :]
            lhs = jnp.concatenate([rows[i] for i in range(4)], axis=1)
            rhs = wt[at["x"], core, at["z"], at["y"]].reshape(512, LOCAL_V)
            acc_t[pl.ds(TOKEN_T[p], PART_T[p][1]), :] += jnp.dot(lhs, rhs, preferred_element_type=F32)

    def sib_wait(j, k):
        for p in PARTS:
            a, b, d = ORDER[p]
            arrive(block(p, ALL, rel(b, STEP[j]), rel(d, STEP[k]), PART_T[p], 1 - c), sibt_r.at[p, 4 * j + k])

    def consume(j, k):
        sib_wait(j, k)

        def one_core(core, _):
            products(j, k, core)
            return 0

        lax.fori_loop(0, 2, one_core, 0)

    def rowsum(value):
        return jnp.sum(value, axis=1, keepdims=True)

    def to_tp(d):
        return (ph, (tp + d) % 16)

    def to_ph(d):
        return ((ph + d) % 8, tp)

    def exchange(buf, slot, count, number, to):
        def copy(d):
            return remote(buf.at[slot], buf.at[slot], ex_s.at[number], ex_r.at[number, d], to(d))

        def start():
            for d in range(1, count):
                copy(d).start()

        def wait():
            for d in range(1, count):
                copy(d).wait_recv()

        def sent():
            arrive(buf.at[pl.ds(0, count - 1)], ex_s.at[number])

        return start, wait, sent

    early_y = exchange(ex_y0, me["y"], 4, 0, lambda d: near("y", d))
    early_z = exchange(ex_z0, me["z"], 4, 5, lambda d: near("z", d))
    early_ph = exchange(ex_ph0, ph, 8, 1, to_ph)
    late_tp = exchange(ex_tp1, tp, 16, 2, to_tp)
    late_ph = exchange(ex_ph1, ph, 8, 3, to_ph)
    gain_ph = exchange(ex_gain_ph, ph, 8, 4, to_ph)

    def to_columns(rows):
        filled = jnp.concatenate(rows + [jnp.zeros((128 - len(rows), TOKENS), F32)], axis=0)
        return jnp.transpose(filled)

    for i in range(3):
        for p in PARTS:
            p1(p, i).start()
    for p in PARTS:
        p2(p, 0, 0).start()
        p2(p, 0, 1).start()
    raw = s_rows[...].astype(F32)
    raw_squares = rowsum(raw * raw)
    lane_t = lax.broadcasted_iota(jnp.int32, (TOKENS, 128), 1)
    st[...] = jnp.where(lane_t == 0, rowsum(wide * wide), 0.0)
    st[0:SLAB, :] = jnp.where(lane_t[0:SLAB] == 1, raw_squares, st[0:SLAB, :])
    squares = jnp.transpose(st[...])
    ex_y0[me["y"]] = jnp.concatenate(
        [squares[0:1, 128 * i : 128 * i + 128] for i in range(4)]
        + [squares[1:2, 0:128], jnp.zeros((3, 128), F32)],
        axis=0,
    )
    early_y[0]()
    lab[...] = to_columns([labels[...].astype(F32)])
    acc_t[...] = jnp.zeros_like(acc_t)
    for n in (1, 2, 3):
        for p in PARTS:
            a, b, d = ORDER[p]
            arrive(block(p, rel(a, STEP[n]), me[b], me[d], PART_T[p]), r1.at[p, (1, 0, 2)[n - 1]])
            p2(p, n, 0).start()
            p2(p, n, 1).start()
    p3t_send(0)
    early_y[1]()
    ex_z0[me["z"]] = ex_y0[0] + ex_y0[1] + ex_y0[2] + ex_y0[3]
    early_z[0]()
    for p in PARTS:
        sib_t(p, 0, 0).start()
    for i in (0, 1):
        for p in PARTS:
            p2_wait(p, i)
            p2f(p, i).start()
            sib_t(p, i + 1, 0).start()
    early_z[1]()
    early = ex_z0[0] + ex_z0[1] + ex_z0[2] + ex_z0[3]
    ex_ph0[ph] = early
    turned = jnp.transpose(jnp.concatenate([early, jnp.zeros((120, 128), F32)], axis=0))
    own_scale = lax.rsqrt(turned[0:SLAB, 4:5] / DS + NORM_EPSILON)
    scale_s[...] = own_scale
    gain = s_gain[...].astype(F32)
    left = (raw[:, 0:128] * own_scale * gain[0:1]).astype(BF16)
    right = (raw[:, 128:256] * own_scale * gain[1:2]).astype(BF16)
    mine[0:48, :] = left[0:48]
    mine[208:224, :] = left[48:64]
    mine[224:256, :] = right[0:32]
    mine[416:448, :] = right[32:64]
    for i in range(3):
        for p in PARTS:
            p1s(p, i).start()
    for p in PARTS:
        p2f_wait(p, 0)
        p2f_wait(p, 1)
        sib_t(p, 3, 0).start()
    p3t_send(1)
    ws_load.wait()
    ws_push = remote(ws, ws_sib, misc_s.at[0], misc_r.at[0], sib)
    ws_push.start()
    for load in wt_loads:
        load.wait()
    for p in PARTS:
        for i in range(3):
            p1s_wait(p, i)
        for i in range(3):
            p2s(p, i).start()
    consume(0, 0)

    def forward(j):
        for i in (0, 1):
            for p in PARTS:
                p3t_wait(p, j, i)
                p3t(p, j, i + 2).start()
                sib_t(p, j, i + 1).start()

    def opposite(j):
        for p in PARTS:
            p3t_wait(p, j, 2)
            p3t_wait(p, j, 3)
            sib_t(p, j, 3).start()

    forward(0)
    consume(1, 0)
    for p in PARTS:
        for i in range(3):
            p2s_wait(p, i)
        p3s(p, 0).start()
        p3s(p, 1).start()
    p3t_send(2)
    early_ph[0]()
    consume(2, 0)
    consume(3, 0)
    forward(1)
    for i in (0, 1):
        for p in PARTS:
            p3s_wait(p, i)
            p3s(p, i + 2).start()
    p3t_send(3)
    consume(0, 1)
    consume(0, 2)
    opposite(0)
    consume(1, 1)
    early_ph[1]()
    early = ex_ph0[0]
    for i in range(1, 8):
        early = early + ex_ph0[i]
    teacher_scale = lax.rsqrt(jnp.concatenate([early[i : i + 1] for i in range(4)], axis=1) / DT + NORM_EPSILON)
    col[...] = to_columns([teacher_scale])
    for p in PARTS:
        p3s_wait(p, 2)
        p3s_wait(p, 3)
        sib_s(p, c).start()
    consume(1, 2)
    consume(0, 3)
    for p in PARTS:
        arrive(G.at[1 - c, :, :, :, pl.ds(*PART_S[p]), :], sibs_r.at[p])

    def slab(q):
        return pl.ds(pl.multiple_of(q * SLAB, SLAB), SLAB)

    def normed(z, y):
        slabs = []
        for q in range(8):
            ref = G.at[q % 2, q // 2, z, y]
            first = jnp.concatenate([ref[0:48, :], ref[208:224, :]], axis=0)
            second = jnp.concatenate([ref[224:256, :], ref[416:448, :]], axis=0)
            slabs.append(jnp.concatenate([first, second], axis=1))
        return jnp.concatenate(slabs, axis=0)

    def student_dot(z, half):
        t = 4 * z + 2 * half
        lhs = jnp.concatenate([normed(z, 2 * half), normed(z, 2 * half + 1)], axis=1)
        rhs = jnp.concatenate([ws[t], ws[t + 1]], axis=0)
        return jnp.dot(lhs, rhs, preferred_element_type=F32)

    def student_dots(z, _):
        sl[...] += student_dot(z, 0)
        sl[...] += student_dot(z, 1)
        return 0

    def nt_dot(lhs, rhs):
        return lax.dot_general(lhs, rhs, (((1,), (1,)), ((), ())), preferred_element_type=F32)

    eye = (
        lax.broadcasted_iota(jnp.int32, (256, 256), 0) == lax.broadcasted_iota(jnp.int32, (256, 256), 1)
    ).astype(F32).astype(BF16)

    def head_copy(t):
        return pltpu.make_async_copy(head_part.at[t % 2], head_out.at[t], out_sem.at[t % 2])

    lane_c = lax.broadcasted_iota(jnp.int32, (256, 128), 1)

    def head_layer(z, _):
        for y in range(4):
            t = 4 * z + y
            if y >= 2:
                head_copy(t - 2).wait()
            else:

                @pl.when(z >= 1)
                def _(t=t):
                    head_copy(t - 2).wait()

            turned = nt_dot(eye, normed(z, y)).astype(BF16)
            grad = jnp.dot(turned, g_ref[...], preferred_element_type=F32)
            head_part[t % 2] = grad.astype(BF16)
            head_copy(t).start()
            gain_col[...] = jnp.where(lane_c == t, rowsum(grad * ws[t].astype(F32)), gain_col[...])
        return 0

    sl[...] = student_dot(0, 0)
    sl[...] += student_dot(0, 1)
    forward(2)
    lax.fori_loop(1, 4, student_dots, 0)
    opposite(1)
    lane = lax.broadcasted_iota(jnp.int32, (SLAB, 128), 1)
    vocab_first = ((ph * 16 + tp) * LOCAL_V).astype(F32)

    def label_hit(rows):
        ids = lax.broadcasted_iota(jnp.int32, (SLAB, LOCAL_V), 1).astype(F32) + vocab_first
        return lab[rows, 0:1] == ids

    def pack(columns, first, out):
        for i, column in enumerate(columns):
            out = jnp.where(lane == first + i, column, out)
        return out

    def student_stats(q, _):
        rows = slab(q)
        logits = sl[rows, :]
        top = jnp.max(logits, axis=1, keepdims=True)
        e = jnp.exp(logits - top)
        es[rows, :] = e
        picked = jnp.where(label_hit(rows), logits, 0.0)
        st[rows, :] = pack(
            [top, rowsum(e), rowsum(e * logits), rowsum(picked)], 4, jnp.zeros((SLAB, 128), F32)
        )
        return 0

    lax.fori_loop(0, 8, student_stats, 0)
    consume(2, 1)
    consume(2, 2)
    forward(3)
    consume(1, 3)
    opposite(2)
    consume(3, 1)
    consume(3, 2)
    consume(2, 3)
    opposite(3)
    products(3, 3, c)
    sib_wait(3, 3)
    products(3, 3, 1 - c)

    def teacher_stats(q, _):
        rows = slab(q)
        logits = acc_t[rows, :] * col[rows, 0:1]
        student = sl[rows, :]
        top = jnp.max(logits, axis=1, keepdims=True)
        e = jnp.exp(logits - top)
        acc_t[rows, :] = e
        st[rows, :] = pack([top, rowsum(e), rowsum(e * (logits - student)), rowsum(e * student)], 0, st[rows, :])
        return 0

    lax.fori_loop(0, 8, teacher_stats, 0)
    stats = jnp.transpose(st[...])[0:8, :]
    sub = lax.broadcasted_iota(jnp.int32, (8, TOKENS), 0)

    def merge(buf, count):
        t_top, s_top = buf[0, 0:1, :], buf[0, 4:5, :]
        for i in range(1, count):
            t_top = jnp.maximum(t_top, buf[i, 0:1, :])
            s_top = jnp.maximum(s_top, buf[i, 4:5, :])
        total = jnp.zeros((8, TOKENS), F32)
        for i in range(count):
            weight = jnp.where(sub < 4, jnp.exp(buf[i, 0:1, :] - t_top), jnp.exp(buf[i, 4:5, :] - s_top))
            total = total + buf[i] * jnp.where(sub == 7, 1.0, weight)
        return jnp.where(sub == 0, t_top, jnp.where(sub == 4, s_top, total))

    ex_tp1[tp] = stats
    late_tp[0]()
    late_tp[1]()
    ex_ph1[ph] = merge(ex_tp1, 16)
    late_ph[0]()
    late_ph[1]()
    late = merge(ex_ph1, 8)
    teacher_top, teacher_total, student_top, student_total = late[0:1], late[1:2], late[4:5], late[5:6]
    picked_all = late[7:8]
    teacher_lse = teacher_top + jnp.log(teacher_total)
    student_lse = student_top + jnp.log(student_total)
    loss = (
        late[2:3] / teacher_total - teacher_lse + student_lse + LABEL_WEIGHT * (student_lse - picked_all)
    )
    inner = (
        (1.0 + LABEL_WEIGHT) * late[6:7] / student_total - late[3:4] / teacher_total - LABEL_WEIGHT * picked_all
    )
    t_factor = jnp.exp(stats[0:1] - teacher_top) / teacher_total
    s_factor = (1.0 + LABEL_WEIGHT) * jnp.exp(stats[4:5] - student_top) / student_total
    col[...] = to_columns([t_factor, s_factor, inner])

    def logit_grad(n, which):
        q = 2 * n + (c if which == 0 else 1 - c)
        rows = slab(q)
        g = (
            es[rows, :] * col[rows, 1:2]
            - acc_t[rows, :] * col[rows, 0:1]
            - LABEL_WEIGHT * label_hit(rows).astype(F32)
        ).astype(BF16)
        g_ref[rows, :] = g
        gp[which, slab(n), :] = g

    for which in (1, 0):

        def grad_step(n, _, which=which):
            logit_grad(n, which)
            return 0

        lax.fori_loop(0, 4, grad_step, 0)
        if which == 1:
            gp_push = remote(gp.at[1], gp_in, misc_s.at[1], misc_r.at[1], sib)
            gp_push.start()
    gain_col[...] = jnp.zeros_like(gain_col)

    def own_first(z, _):
        for y in range(4):
            r = nt_dot(gp[0], ws[4 * z + y])
            for xt in range(4):
                own[xt, z, y, 0:64] = r[xt * 64 : xt * 64 + 64, 0:128]
                own[xt, z, y, 64:128] = r[xt * 64 : xt * 64 + 64, 128:256]
        return 0

    def own_second(z):
        for y in range(4):
            r = nt_dot(gp_in[...], ws_sib[4 * z + y])
            for xt in range(4):
                for h in range(2):
                    at = pl.ds(64 * h, 64)
                    total = own[xt, z, y, at, :] + r[xt * 64 : xt * 64 + 64, 128 * h : 128 * h + 128]
                    own[xt, z, y, at, :] = total
                    wt[xt, 0, z, y, at, 0:128] = total.astype(BF16)

    lax.fori_loop(0, 4, own_first, 0)
    ws_push.wait_recv()
    gp_push.wait_recv()

    def at3(p, one, two, three):
        a, b, d = ORDER[p]
        at = {a: one, b: two, d: three}
        return at["x"], at["z"], at["y"]

    def rest(p, two, three):
        at = {ORDER[p][1]: two, ORDER[p][2]: three}
        return tuple(at[axis] for axis in ("x", "z", "y") if axis in at)

    def stage_ref(p, one, two, three):
        ix, iz, iy = at3(p, one, two, three)
        return wt.at[ix, 0, iz, iy, pl.ds(*RS_PART[p]), pl.ds(0, 128)]

    def own_ref(p, one, two, three):
        ix, iz, iy = at3(p, one, two, three)
        return own.at[ix, iz, iy, pl.ds(*RS_PART[p]), :]

    HOP = (2, 1, -1)
    SUBSET = (2, 1, -1, 0)

    def rs1(p, k, i):
        a, b, d = ORDER[p]
        two = rel(b, SUBSET[k])
        src = stage_ref(p, rel(a, HOP[i]), two, ALL)
        dst = rs_b.at[(i, *rest(p, two, ALL), pl.ds(*RS_PART[p]), ALL)]
        return remote(src, dst, send.at[p, 6], rs_r.at[p, 3 * k + i], near(a, HOP[i]))

    def rs1_wait(p, k, i):
        dst = rs_b.at[(i, *rest(p, rel(ORDER[p][1], SUBSET[k]), ALL), pl.ds(*RS_PART[p]), ALL)]
        arrive(dst, rs_r.at[p, 3 * k + i])

    def rs2(p, i):
        a, b, d = ORDER[p]
        src = stage_ref(p, me[a], rel(b, HOP[i]), ALL)
        dst = rs_c.at[i, :, pl.ds(*RS_PART[p]), :]
        return remote(src, dst, send.at[p, 7], rs_r.at[p, 12 + i], near(b, HOP[i]))

    def rs3(p, i):
        a, b, d = ORDER[p]
        src = stage_ref(p, me[a], me[b], rel(d, HOP[i]))
        dst = rs_d.at[i, pl.ds(*RS_PART[p]), :]
        return remote(src, dst, send.at[p, 8], rs_r.at[p, 15 + i], near(d, HOP[i]))

    for k in range(4):
        own_second(rel("z", SUBSET[k]))
        for i in range(3):
            rs1(1, k, i).start()
        if k < 3:
            for m in range(4):
                rs1(2, m, k).start()
    for k in range(4):
        for i in range(3):
            rs1(0, k, i).start()
    lax.fori_loop(0, 2, head_layer, 0)
    def gain_copy(d):
        to = (tp + d) % 16
        return remote(gain_own.at[to], ex_gain.at[tp], misc_s.at[2], ex_r.at[6, d], (ph, to))

    for k in range(4):
        if k in (1, 2):
            lax.fori_loop(k + 1, k + 2, head_layer, 0)
        if k == 2:
            turned = jnp.transpose(gain_col[...])
            for t in range(16):
                gain_own[t] = jnp.broadcast_to(turned[t : t + 1], (8, 256))
            ex_gain[tp] = gain_own[tp]
            for d in range(1, 16):
                gain_copy(d).start()
        for p in PARTS:
            rows = pl.ds(*RS_PART[p])
            for i in range(3):
                rs1_wait(p, k, i)

            def add_first(n, _, p=p, k=k, rows=rows):
                two = rel(ORDER[p][1], SUBSET[k])
                ref = own_ref(p, me[ORDER[p][0]], two, n)
                total = ref[...]
                for i in range(3):
                    total = total + rs_b[(i, *rest(p, two, n), rows, ALL)].astype(F32)
                if k == 3:
                    ref[...] = total
                else:
                    stage_ref(p, me[ORDER[p][0]], two, n)[...] = total.astype(BF16)
                return 0

            lax.fori_loop(0, 4, add_first, 0)
            if k < 3:
                rs2(p, k).start()
    for p in PARTS:
        rows = pl.ds(*RS_PART[p])
        for i in range(3):
            arrive(rs_c.at[i, :, rows, :], rs_r.at[p, 12 + i])

        def add_second(n, _, p=p, rows=rows):
            ref = own_ref(p, me[ORDER[p][0]], me[ORDER[p][1]], n)
            total = ref[...]
            for i in range(3):
                total = total + rs_c[i, n, rows, :].astype(F32)
            ref[...] = total
            stage_ref(p, me[ORDER[p][0]], me[ORDER[p][1]], n)[...] = total.astype(BF16)
            return 0

        lax.fori_loop(0, 4, add_second, 0)
        for i in range(3):
            rs3(p, i).start()
    for d in range(1, 16):
        gain_copy(d).wait_recv()
    total = ex_gain[0]
    for i in range(1, 16):
        total = total + ex_gain[i]
    ex_gain_ph[ph] = total
    gain_ph[0]()
    for p in PARTS:
        rows = pl.ds(*RS_PART[p])
        for i in range(3):
            arrive(rs_d.at[i, rows, :], rs_r.at[p, 15 + i])
        total = own_ref(p, *own_at(p))[...]
        for i in range(3):
            total = total + rs_d[i, rows, :].astype(F32)
        fin[rows, :] = total

    rows = slab(ph)
    scale = scale_s[...]
    coefficient = scale * scale * col[rows, 2:3] / DS
    for h in range(2):
        cols = pl.ds(h * 128, 128)
        grad = fin[h * 64 : h * 64 + 64, :]
        rows_out[:, cols] = (scale * gain[h : h + 1] * grad - raw[:, h * 128 : h * 128 + 128] * coefficient).astype(BF16)
    sl[0:8, :] = jnp.broadcast_to(loss, (8, TOKENS))
    window = sl[0:1, pl.ds(pl.multiple_of(me["x"] * 128, 128), 128)]
    loss_out[...] = jnp.where(c == 1, window[:, 64:128], window[:, 0:64])

    for p in PARTS:
        rows = pl.ds(*PART_T[p])
        arrive(G.at[0, 0, 0, 0:3, rows, :], send.at[p, 0])
        arrive(G.at[0, 0:3, 0, :, rows, :], send.at[p, 1])
        arrive(G.at[0, 0:3, :, :, rows, :], send.at[p, 3])
        arrive(G.at[0, :, :, :, rows, :], send.at[p, 4])
        rows = pl.ds(*PART_S[p])
        arrive(G.at[0, 0:3, :, :, rows, :], send.at[p, 2])
        arrive(G.at[0, 0:3, 0:1, :, rows, :], send.at[p, 2])
        arrive(G.at[0, 0, 0, 0:3, rows, :], send.at[p, 2])
        arrive(G.at[0, :, :, :, rows, :], send.at[p, 5])
        rows = pl.ds(*RS_PART[p])
        arrive(rs_b.at[:, :, :, rows, :], send.at[p, 6])
        arrive(rs_c.at[:, :, rows, :], send.at[p, 7])
        arrive(rs_d.at[:, rows, :], send.at[p, 8])
    for ex in (early_y, early_z, early_ph, late_tp, late_ph):
        ex[2]()
    ws_push.wait_send()
    gp_push.wait_send()
    head_copy(14).wait()
    head_copy(15).wait()
    arrive(ex_gain.at[pl.ds(0, 15)], misc_s.at[2])
    gain_ph[1]()
    total = ex_gain_ph[0]
    for i in range(1, 8):
        total = total + ex_gain_ph[i]
    gain_out[...] = total[0:1] / jnp.concatenate([gain[0:1], gain[1:2]], axis=1)
    gain_ph[2]()


def out_kernel(head_in, loss_in, rows_in, gain_in, head_out, loss_out, rows_out, gain_out, held, in_sem, out_sem):
    def part(ref, i):
        return ref.at[pl.ds(1024 * i, 1024)]

    loads = [pltpu.make_async_copy(part(head_in, i), part(held, i), in_sem.at[i]) for i in range(4)]
    stores = [pltpu.make_async_copy(part(held, i), part(head_out, i), out_sem.at[i]) for i in range(4)]
    for load in loads:
        load.start()
    loss_out[...] = loss_in[...]
    rows_out[...] = rows_in[...]
    gain_out[...] = gain_in[...]
    for load, store in zip(loads, stores):
        load.wait()
        store.start()
    for store in stores:
        store.wait()


def local(teacher_rows, teacher_gain, teacher_head, student_rows, student_gain, student_head, labels):
    vmem = pl.BlockSpec(memory_space=pltpu.VMEM)
    hbm = pl.BlockSpec(memory_space=pl.ANY)
    dma = pltpu.SemaphoreType.DMA
    loss, rows_grad, gain_grad, head_grad = pl.pallas_call(
        comm_kernel,
        out_shape=(
            jax.ShapeDtypeStruct((1, SLAB), F32),
            jax.ShapeDtypeStruct((SLAB, 256), BF16),
            jax.ShapeDtypeStruct((1, 256), F32),
            jax.ShapeDtypeStruct((16, 256, LOCAL_V), BF16),
        ),
        in_specs=[vmem, vmem, hbm, vmem, vmem, hbm, vmem],
        out_specs=(vmem, vmem, vmem, hbm),
        scratch_shapes=[
            pltpu.VMEM((2, 4, 4, 4, 640, 128), BF16),
            pltpu.VMEM((4, 2, 4, 4, 128, LOCAL_V), BF16),
            pltpu.VMEM((16, 256, LOCAL_V), BF16),
            pltpu.VMEM((16, 256, LOCAL_V), BF16),
            pltpu.VMEM((2, 256, LOCAL_V), BF16),
            pltpu.VMEM((TOKENS, LOCAL_V), F32),
            pltpu.VMEM((TOKENS, LOCAL_V), F32),
            pltpu.VMEM((TOKENS, LOCAL_V), F32),
            pltpu.VMEM((TOKENS, 128), F32),
            pltpu.VMEM((TOKENS, 128), F32),
            pltpu.VMEM((TOKENS, 128), F32),
            pltpu.VMEM((SLAB, 1), F32),
            pltpu.VMEM((TOKENS, LOCAL_V), BF16),
            pltpu.VMEM((2, 256, LOCAL_V), BF16),
            pltpu.VMEM((256, LOCAL_V), BF16),
            pltpu.VMEM((4, 4, 4, 128, 128), F32),
            pltpu.VMEM((3, 4, 4, 128, 128), BF16),
            pltpu.VMEM((3, 4, 128, 128), BF16),
            pltpu.VMEM((3, 128, 128), BF16),
            pltpu.VMEM((128, 128), F32),
            pltpu.VMEM((4, 8, 128), F32),
            pltpu.VMEM((4, 8, 128), F32),
            pltpu.VMEM((8, 8, 128), F32),
            pltpu.VMEM((16, 8, TOKENS), F32),
            pltpu.VMEM((8, 8, TOKENS), F32),
            pltpu.VMEM((256, 128), F32),
            pltpu.VMEM((16, 8, 256), F32),
            pltpu.VMEM((16, 8, 256), F32),
            pltpu.VMEM((8, 8, 256), F32),
            dma((5,)), dma((2,)), dma((3, 9)),
            dma((3, 3)), dma((3, 2)), dma((3, 2)), dma((3, 3)), dma((3, 3)), dma((3, 4)), dma((3, 16)),
            dma((3,)), dma((3, 16)), dma((6,)), dma((7, 16)), dma((3,)), dma((2,)), dma((3, 18)),
        ],
        compiler_params=pltpu.CompilerParams(
            collective_id=0, has_side_effects=True, vmem_limit_bytes=63 << 20
        ),
        name="distill",
    )(
        teacher_rows,
        teacher_gain.reshape(1, 128),
        teacher_head.reshape(4, 2, 4, 4, 128, LOCAL_V),
        student_rows,
        student_gain.reshape(2, 128),
        student_head.reshape(16, 256, LOCAL_V),
        labels.reshape(1, TOKENS),
    )
    head_grad, loss, rows_grad, gain_grad = pl.pallas_call(
        out_kernel,
        out_shape=(
            jax.ShapeDtypeStruct((DS, LOCAL_V), BF16),
            jax.ShapeDtypeStruct((1, SLAB), F32),
            jax.ShapeDtypeStruct((SLAB, 256), BF16),
            jax.ShapeDtypeStruct((1, 256), F32),
        ),
        in_specs=[hbm, vmem, vmem, vmem],
        out_specs=(hbm, vmem, vmem, vmem),
        scratch_shapes=[pltpu.VMEM((DS, LOCAL_V), BF16), dma((4,)), dma((4,))],
        compiler_params=pltpu.CompilerParams(vmem_limit_bytes=63 << 20),
        name="outputs",
    )(head_grad.reshape(DS, LOCAL_V), loss, rows_grad, gain_grad)
    return loss.reshape(SLAB), head_grad, rows_grad, gain_grad.reshape(256)


def solution(mesh):
    placed = (
        P(None, ("phase", "tp")),
        P(("phase", "tp")),
        P(None, ("phase", "tp")),
        P("phase", "tp"),
        P("tp"),
        P(None, ("phase", "tp")),
        P(),
    )
    return jax.shard_map(
        local,
        mesh=mesh,
        in_specs=placed,
        out_specs=(P("phase"), P(None, ("phase", "tp")), P("phase", "tp"), P("tp")),
        check_vma=False,
    )
```

```python
import jax
import jax.numpy as jnp
from jax import lax
from jax.experimental import pallas as pl
from jax.experimental.pallas import tpu as pltpu
from jax.sharding import PartitionSpec as P

NORM_EPSILON = 1e-05
LABEL_WEIGHT = 0.5
F32 = jnp.float32
BF16 = jnp.bfloat16
MESH = pl.DeviceIdType.MESH

DT, DS, TOKENS, LOCAL_V = 16384, 4096, 512, 512
SLAB = 64
PART = ((0, 208), (208, 208), (416, 224))
PART_S = ((0, 48), (208, 48), (416, 32))
PART_T = ((48, 160), (256, 160), (448, 192))
TOKEN_T = (0, 160, 320)
ORDER = (("x", "y", "z"), ("y", "z", "x"), ("z", "x", "y"))
RS_ORDER = (("x", "z", "y"), ("y", "z", "x"), ("z", "x", "y"))
RS_PART = ((0, 48), (48, 48), (96, 32))
ALL = slice(None)
LOW, HIGH = pl.ds(0, 2), pl.ds(2, 2)


def comm_kernel(
    t_rows, t_gain, wt_hbm, s_rows, s_gain, ws_hbm, labels,
    loss_out, rows_out, gain_out, head_out,
    G, wt, ws, ws_sib, head_part, acc_t, sl, es, st, col, lab, scale_s, g_ref, gp, gp_in, own,
    rs_b, rs_c, rs_d, fin, ex_y0, ex_z0, ex_ph0, ex_tp1, ex_ph1, gain_col, gain_own, ex_gain, ex_gain_ph,
    w_sem, out_sem, send, r1, r2, r2f, r1s, r2s, r3s, r3t, sibs_r, sibt_r, ex_s, ex_r, misc_s, misc_r, rs_r,
):
    ph = lax.axis_index("phase")
    tp = lax.axis_index("tp")
    c = ph % 2
    me = {"x": ph // 2, "y": tp % 4, "z": tp // 4}
    sib = (ph + 1 - 2 * c, tp)
    PARTS = range(3)
    STEP = (0, -1, 1, 2)

    def rel(axis, step):
        return (me[axis] + step + 4) % 4

    def near(axis, step):
        at = dict(me)
        at[axis] = rel(axis, step)
        return (at["x"] * 2 + c, at["z"] * 4 + at["y"])

    def remote(src, dst, ssem, rsem, to):
        return pltpu.make_async_remote_copy(
            src_ref=src, dst_ref=dst, send_sem=ssem, recv_sem=rsem, device_id=to, device_id_type=MESH
        )

    wt_loads = [pltpu.make_async_copy(wt_hbm.at[i], wt.at[i], w_sem.at[i]) for i in range(4)]
    ws_load = pltpu.make_async_copy(ws_hbm, ws, w_sem.at[4])
    ws_load.start()
    for load in wt_loads:
        load.start()

    barrier = pltpu.get_barrier_semaphore()
    partners = [sib] + [near(axis, step) for axis in "xyz" for step in (1, -1, 2)]
    for to in partners:
        pl.semaphore_signal(barrier, inc=1, device_id=to, device_id_type=MESH)

    mine = G.at[c, me["x"], me["z"], me["y"]]
    wide = t_rows[...].astype(F32)
    scaled = (wide * t_gain[...].astype(F32)).astype(BF16)
    for (row, size), token in zip(PART_T, TOKEN_T):
        mine[pl.ds(row, size), :] = scaled[token : token + size]
    pl.semaphore_wait(barrier, len(partners))

    def block(p, one, two, three, rows, core=None):
        a, b, d = ORDER[p]
        at = {a: one, b: two, d: three}
        return G.at[c if core is None else core, at["x"], at["z"], at["y"], pl.ds(*rows), :]

    def own_at(p):
        return tuple(me[axis] for axis in ORDER[p])

    def p1(p, i):
        ref = block(p, *own_at(p), PART_T[p])
        return remote(ref, ref, send.at[p, 0], r1.at[p, i], near(ORDER[p][0], (-1, 1, 2)[i]))

    def p2(p, n, i):
        a, b, d = ORDER[p]
        ref = block(p, rel(a, STEP[n]), me[b], me[d], PART_T[p])
        return remote(ref, ref, send.at[p, 1], r2.at[p, i], near(b, (1, -1)[i]))

    def p2f(p, i):
        a, b, d = ORDER[p]
        ref = block(p, (LOW, HIGH)[i], rel(b, (-1, 1)[i]), me[d], PART_T[p])
        return remote(ref, ref, send.at[p, 1], r2f.at[p, i], near(b, (1, -1)[i]))

    def p1s(p, i):
        ref = block(p, *own_at(p), PART_S[p])
        return remote(ref, ref, send.at[p, 2], r1s.at[p, i], near(ORDER[p][0], (-1, 1, 2)[i]))

    def p2s(p, i):
        a, b, d = ORDER[p]
        ref = block(p, ALL, me[b], me[d], PART_S[p])
        return remote(ref, ref, send.at[p, 2], r2s.at[p, i], near(b, (-1, 1, 2)[i]))

    def p3s(p, i):
        d = ORDER[p][2]
        ref = block(p, (ALL, ALL, LOW, HIGH)[i], ALL, rel(d, (0, 0, -1, 1)[i]), PART_S[p])
        return remote(ref, ref, send.at[p, 2], r3s.at[p, i], near(d, (1, -1, 1, -1)[i]))

    def p3t(p, j, i):
        a, b, d = ORDER[p]
        ref = block(p, (ALL, ALL, LOW, HIGH)[i], rel(b, STEP[j]), rel(d, (0, 0, -1, 1)[i]), PART_T[p])
        return remote(ref, ref, send.at[p, 3], r3t.at[p, 4 * j + i], near(d, (1, -1, 1, -1)[i]))

    def arrive(ref, sem):
        pltpu.make_async_copy(ref, ref, sem).wait()

    def p2_wait(p, i):
        a, b, d = ORDER[p]
        arrive(block(p, ALL, rel(b, (-1, 1)[i]), me[d], PART_T[p]), r2.at[p, i])

    def p2f_wait(p, i):
        a, b, d = ORDER[p]
        arrive(block(p, (LOW, HIGH)[i], rel(b, 2), me[d], PART_T[p]), r2f.at[p, i])

    def p1s_wait(p, i):
        a, b, d = ORDER[p]
        arrive(block(p, rel(a, (1, -1, 2)[i]), me[b], me[d], PART_S[p]), r1s.at[p, i])

    def p2s_wait(p, i):
        a, b, d = ORDER[p]
        arrive(block(p, ALL, rel(b, (1, -1, 2)[i]), me[d], PART_S[p]), r2s.at[p, i])

    def p3s_wait(p, i):
        d = ORDER[p][2]
        arrive(block(p, (ALL, ALL, LOW, HIGH)[i], ALL, rel(d, (-1, 1, 2, 2)[i]), PART_S[p]), r3s.at[p, i])

    def p3t_wait(p, j, i):
        a, b, d = ORDER[p]
        ref = block(p, (ALL, ALL, LOW, HIGH)[i], rel(b, STEP[j]), rel(d, (-1, 1, 2, 2)[i]), PART_T[p])
        arrive(ref, r3t.at[p, 4 * j + i])

    def sib_t(p, j, k, core=None):
        a, b, d = ORDER[p]
        ref = block(p, ALL, rel(b, STEP[j]), rel(d, STEP[k]), PART_T[p], core)
        return remote(ref, ref, send.at[p, 4], sibt_r.at[p, 4 * j + k], sib)

    def sib_s(p, core):
        ref = G.at[core, :, :, :, pl.ds(*PART_S[p]), :]
        return remote(ref, ref, send.at[p, 5], sibs_r.at[p], sib)

    def p3t_send(j):
        for p in PARTS:
            p3t(p, j, 0).start()
            p3t(p, j, 1).start()

    def products(j, k, core):
        for p in PARTS:
            a, b, d = ORDER[p]
            at = {a: ALL, b: rel(b, STEP[j]), d: rel(d, STEP[k])}
            rows = G[core, at["x"], at["z"], at["y"], pl.ds(*PART_T[p]), :]
            lhs = jnp.concatenate([rows[i] for i in range(4)], axis=1)
            rhs = wt[at["x"], core, at["z"], at["y"]].reshape(512, LOCAL_V)
            acc_t[pl.ds(TOKEN_T[p], PART_T[p][1]), :] += jnp.dot(lhs, rhs, preferred_element_type=F32)

    def sib_wait(j, k):
        for p in PARTS:
            a, b, d = ORDER[p]
            arrive(block(p, ALL, rel(b, STEP[j]), rel(d, STEP[k]), PART_T[p], 1 - c), sibt_r.at[p, 4 * j + k])

    def consume(j, k):
        sib_wait(j, k)

        def one_core(core, _):
            products(j, k, core)
            return 0

        lax.fori_loop(0, 2, one_core, 0)

    def rowsum(value):
        return jnp.sum(value, axis=1, keepdims=True)

    def to_tp(d):
        return (ph, (tp + d) % 16)

    def to_ph(d):
        return ((ph + d) % 8, tp)

    def exchange(buf, slot, count, number, to):
        def copy(d):
            return remote(buf.at[slot], buf.at[slot], ex_s.at[number], ex_r.at[number, d], to(d))

        def start():
            for d in range(1, count):
                copy(d).start()

        def wait():
            for d in range(1, count):
                copy(d).wait_recv()

        def sent():
            arrive(buf.at[pl.ds(0, count - 1)], ex_s.at[number])

        return start, wait, sent

    early_y = exchange(ex_y0, me["y"], 4, 0, lambda d: near("y", d))
    early_z = exchange(ex_z0, me["z"], 4, 5, lambda d: near("z", d))
    early_ph = exchange(ex_ph0, ph, 8, 1, to_ph)
    late_tp = exchange(ex_tp1, tp, 16, 2, to_tp)
    late_ph = exchange(ex_ph1, ph, 8, 3, to_ph)
    gain_ph = exchange(ex_gain_ph, ph, 8, 4, to_ph)

    def to_columns(rows):
        filled = jnp.concatenate(rows + [jnp.zeros((128 - len(rows), TOKENS), F32)], axis=0)
        return jnp.transpose(filled)

    for i in range(3):
        for p in PARTS:
            p1(p, i).start()
    for p in PARTS:
        p2(p, 0, 0).start()
        p2(p, 0, 1).start()
    raw = s_rows[...].astype(F32)
    raw_squares = rowsum(raw * raw)
    lane_t = lax.broadcasted_iota(jnp.int32, (TOKENS, 128), 1)
    st[...] = jnp.where(lane_t == 0, rowsum(wide * wide), 0.0)
    st[0:SLAB, :] = jnp.where(lane_t[0:SLAB] == 1, raw_squares, st[0:SLAB, :])
    squares = jnp.transpose(st[...])
    ex_y0[me["y"]] = jnp.concatenate(
        [squares[0:1, 128 * i : 128 * i + 128] for i in range(4)]
        + [squares[1:2, 0:128], jnp.zeros((3, 128), F32)],
        axis=0,
    )
    early_y[0]()
    lab[...] = to_columns([labels[...].astype(F32)])
    acc_t[...] = jnp.zeros_like(acc_t)
    for n in (1, 2, 3):
        for p in PARTS:
            a, b, d = ORDER[p]
            arrive(block(p, rel(a, STEP[n]), me[b], me[d], PART_T[p]), r1.at[p, (1, 0, 2)[n - 1]])
            p2(p, n, 0).start()
            p2(p, n, 1).start()
    p3t_send(0)
    early_y[1]()
    ex_z0[me["z"]] = ex_y0[0] + ex_y0[1] + ex_y0[2] + ex_y0[3]
    early_z[0]()
    for p in PARTS:
        sib_t(p, 0, 0).start()
    for i in (0, 1):
        for p in PARTS:
            p2_wait(p, i)
            p2f(p, i).start()
            sib_t(p, i + 1, 0).start()
    early_z[1]()
    early = ex_z0[0] + ex_z0[1] + ex_z0[2] + ex_z0[3]
    ex_ph0[ph] = early
    turned = jnp.transpose(jnp.concatenate([early, jnp.zeros((120, 128), F32)], axis=0))
    own_scale = lax.rsqrt(turned[0:SLAB, 4:5] / DS + NORM_EPSILON)
    scale_s[...] = own_scale
    gain = s_gain[...].astype(F32)
    left = (raw[:, 0:128] * own_scale * gain[0:1]).astype(BF16)
    right = (raw[:, 128:256] * own_scale * gain[1:2]).astype(BF16)
    mine[0:48, :] = left[0:48]
    mine[208:224, :] = left[48:64]
    mine[224:256, :] = right[0:32]
    mine[416:448, :] = right[32:64]
    for i in range(3):
        for p in PARTS:
            p1s(p, i).start()
    for p in PARTS:
        p2f_wait(p, 0)
        p2f_wait(p, 1)
        sib_t(p, 3, 0).start()
    p3t_send(1)
    ws_load.wait()
    ws_push = remote(ws, ws_sib, misc_s.at[0], misc_r.at[0], sib)
    ws_push.start()
    for load in wt_loads:
        load.wait()
    for p in PARTS:
        for i in range(3):
            p1s_wait(p, i)
        for i in range(3):
            p2s(p, i).start()
    consume(0, 0)

    def forward(j):
        for i in (0, 1):
            for p in PARTS:
                p3t_wait(p, j, i)
                p3t(p, j, i + 2).start()
                sib_t(p, j, i + 1).start()

    def opposite(j):
        for p in PARTS:
            p3t_wait(p, j, 2)
            p3t_wait(p, j, 3)
            sib_t(p, j, 3).start()

    forward(0)
    consume(1, 0)
    for p in PARTS:
        for i in range(3):
            p2s_wait(p, i)
        p3s(p, 0).start()
        p3s(p, 1).start()
    p3t_send(2)
    early_ph[0]()
    consume(2, 0)
    consume(3, 0)
    forward(1)
    for i in (0, 1):
        for p in PARTS:
            p3s_wait(p, i)
            p3s(p, i + 2).start()
    p3t_send(3)
    consume(0, 1)
    consume(0, 2)
    opposite(0)
    consume(1, 1)
    early_ph[1]()
    early = ex_ph0[0]
    for i in range(1, 8):
        early = early + ex_ph0[i]
    teacher_scale = lax.rsqrt(jnp.concatenate([early[i : i + 1] for i in range(4)], axis=1) / DT + NORM_EPSILON)
    col[...] = to_columns([teacher_scale])
    for p in PARTS:
        p3s_wait(p, 2)
        p3s_wait(p, 3)
        sib_s(p, c).start()
    consume(1, 2)
    consume(0, 3)
    for p in PARTS:
        arrive(G.at[1 - c, :, :, :, pl.ds(*PART_S[p]), :], sibs_r.at[p])

    def slab(q):
        return pl.ds(pl.multiple_of(q * SLAB, SLAB), SLAB)

    def normed(z, y):
        slabs = []
        for q in range(8):
            ref = G.at[q % 2, q // 2, z, y]
            first = jnp.concatenate([ref[0:48, :], ref[208:224, :]], axis=0)
            second = jnp.concatenate([ref[224:256, :], ref[416:448, :]], axis=0)
            slabs.append(jnp.concatenate([first, second], axis=1))
        return jnp.concatenate(slabs, axis=0)

    def student_dot(z, half):
        t = 4 * z + 2 * half
        lhs = jnp.concatenate([normed(z, 2 * half), normed(z, 2 * half + 1)], axis=1)
        rhs = jnp.concatenate([ws[t], ws[t + 1]], axis=0)
        return jnp.dot(lhs, rhs, preferred_element_type=F32)

    def student_dots(z, _):
        sl[...] += student_dot(z, 0)
        sl[...] += student_dot(z, 1)
        return 0

    def nt_dot(lhs, rhs):
        return lax.dot_general(lhs, rhs, (((1,), (1,)), ((), ())), preferred_element_type=F32)

    eye = (
        lax.broadcasted_iota(jnp.int32, (256, 256), 0) == lax.broadcasted_iota(jnp.int32, (256, 256), 1)
    ).astype(F32).astype(BF16)

    def head_copy(t):
        return pltpu.make_async_copy(head_part.at[t % 2], head_out.at[t], out_sem.at[t % 2])

    lane_c = lax.broadcasted_iota(jnp.int32, (256, 128), 1)

    def head_layer(z, _):
        for y in range(4):
            t = 4 * z + y
            if y >= 2:
                head_copy(t - 2).wait()
            else:

                @pl.when(z >= 1)
                def _(t=t):
                    head_copy(t - 2).wait()

            turned = nt_dot(eye, normed(z, y)).astype(BF16)
            grad = jnp.dot(turned, g_ref[...], preferred_element_type=F32)
            head_part[t % 2] = grad.astype(BF16)
            head_copy(t).start()
            gain_col[...] = jnp.where(lane_c == t, rowsum(grad * ws[t].astype(F32)), gain_col[...])
        return 0

    sl[...] = student_dot(0, 0)
    sl[...] += student_dot(0, 1)
    forward(2)
    lax.fori_loop(1, 4, student_dots, 0)
    opposite(1)
    lane = lax.broadcasted_iota(jnp.int32, (SLAB, 128), 1)
    vocab_first = ((ph * 16 + tp) * LOCAL_V).astype(F32)

    def label_hit(rows):
        ids = lax.broadcasted_iota(jnp.int32, (SLAB, LOCAL_V), 1).astype(F32) + vocab_first
        return lab[rows, 0:1] == ids

    def pack(columns, first, out):
        for i, column in enumerate(columns):
            out = jnp.where(lane == first + i, column, out)
        return out

    def student_stats(n, _):
        student_slab(2 * n)
        student_slab(2 * n + 1)
        return 0

    def student_slab(q):
        rows = slab(q)
        logits = sl[rows, :]
        top = jnp.max(logits, axis=1, keepdims=True)
        e = jnp.exp(logits - top)
        es[rows, :] = e
        picked = jnp.where(label_hit(rows), logits, 0.0)
        st[rows, :] = pack(
            [top, rowsum(e), rowsum(e * logits), rowsum(picked)], 4, jnp.zeros((SLAB, 128), F32)
        )

    lax.fori_loop(0, 4, student_stats, 0)
    consume(2, 1)
    consume(2, 2)
    forward(3)
    consume(1, 3)
    opposite(2)
    consume(3, 1)
    consume(3, 2)
    consume(2, 3)
    opposite(3)
    products(3, 3, c)
    sib_wait(3, 3)
    products(3, 3, 1 - c)

    def teacher_stats(n, _):
        teacher_slab(2 * n)
        teacher_slab(2 * n + 1)
        return 0

    def teacher_slab(q):
        rows = slab(q)
        logits = acc_t[rows, :] * col[rows, 0:1]
        student = sl[rows, :]
        top = jnp.max(logits, axis=1, keepdims=True)
        e = jnp.exp(logits - top)
        acc_t[rows, :] = e
        st[rows, :] = pack([top, rowsum(e), rowsum(e * (logits - student)), rowsum(e * student)], 0, st[rows, :])

    lax.fori_loop(0, 4, teacher_stats, 0)
    stats = jnp.transpose(st[...])[0:8, :]
    sub = lax.broadcasted_iota(jnp.int32, (8, TOKENS), 0)

    def merge(buf, count):
        t_top, s_top = buf[0, 0:1, :], buf[0, 4:5, :]
        for i in range(1, count):
            t_top = jnp.maximum(t_top, buf[i, 0:1, :])
            s_top = jnp.maximum(s_top, buf[i, 4:5, :])
        total = jnp.zeros((8, TOKENS), F32)
        for i in range(count):
            weight = jnp.where(sub < 4, jnp.exp(buf[i, 0:1, :] - t_top), jnp.exp(buf[i, 4:5, :] - s_top))
            total = total + buf[i] * jnp.where(sub == 7, 1.0, weight)
        return jnp.where(sub == 0, t_top, jnp.where(sub == 4, s_top, total))

    ex_tp1[tp] = stats
    late_tp[0]()
    late_tp[1]()
    ex_ph1[ph] = merge(ex_tp1, 16)
    late_ph[0]()
    late_ph[1]()
    late = merge(ex_ph1, 8)
    teacher_top, teacher_total, student_top, student_total = late[0:1], late[1:2], late[4:5], late[5:6]
    picked_all = late[7:8]
    teacher_lse = teacher_top + jnp.log(teacher_total)
    student_lse = student_top + jnp.log(student_total)
    loss = (
        late[2:3] / teacher_total - teacher_lse + student_lse + LABEL_WEIGHT * (student_lse - picked_all)
    )
    inner = (
        (1.0 + LABEL_WEIGHT) * late[6:7] / student_total - late[3:4] / teacher_total - LABEL_WEIGHT * picked_all
    )
    t_factor = jnp.exp(stats[0:1] - teacher_top) / teacher_total
    s_factor = (1.0 + LABEL_WEIGHT) * jnp.exp(stats[4:5] - student_top) / student_total
    col[...] = to_columns([t_factor, s_factor, inner])

    def logit_grad(n, which):
        q = 2 * n + (c if which == 0 else 1 - c)
        rows = slab(q)
        g = (
            es[rows, :] * col[rows, 1:2]
            - acc_t[rows, :] * col[rows, 0:1]
            - LABEL_WEIGHT * label_hit(rows).astype(F32)
        ).astype(BF16)
        g_ref[rows, :] = g
        gp[which, slab(n), :] = g

    for which in (1, 0):

        def grad_step(n, _, which=which):
            logit_grad(2 * n, which)
            logit_grad(2 * n + 1, which)
            return 0

        lax.fori_loop(0, 2, grad_step, 0)
        if which == 1:
            gp_push = remote(gp.at[1], gp_in, misc_s.at[1], misc_r.at[1], sib)
            gp_push.start()
    gain_col[...] = jnp.zeros_like(gain_col)

    def own_first(z, _):
        for y in range(4):
            r = nt_dot(gp[0], ws[4 * z + y])
            for xt in range(4):
                own[xt, z, y, 0:64] = r[xt * 64 : xt * 64 + 64, 0:128]
                own[xt, z, y, 64:128] = r[xt * 64 : xt * 64 + 64, 128:256]
        return 0

    def own_second(z):
        for y in range(4):
            r = nt_dot(gp_in[...], ws_sib[4 * z + y])
            for xt in range(4):
                for h in range(2):
                    at = pl.ds(64 * h, 64)
                    total = own[xt, z, y, at, :] + r[xt * 64 : xt * 64 + 64, 128 * h : 128 * h + 128]
                    own[xt, z, y, at, :] = total
                    wt[xt, 0, z, y, at, 0:128] = total.astype(BF16)

    lax.fori_loop(0, 4, own_first, 0)
    ws_push.wait_recv()
    gp_push.wait_recv()

    def at3(p, one, two, three):
        a, b, d = RS_ORDER[p]
        at = {a: one, b: two, d: three}
        return at["x"], at["z"], at["y"]

    def rest(p, two, three):
        at = {RS_ORDER[p][1]: two, RS_ORDER[p][2]: three}
        return tuple(at[axis] for axis in ("x", "z", "y") if axis in at)

    def stage_ref(p, one, two, three):
        ix, iz, iy = at3(p, one, two, three)
        return wt.at[ix, 0, iz, iy, pl.ds(*RS_PART[p]), pl.ds(0, 128)]

    def own_ref(p, one, two, three):
        ix, iz, iy = at3(p, one, two, three)
        return own.at[ix, iz, iy, pl.ds(*RS_PART[p]), :]

    HOP = (2, 1, -1)
    SUBSET = (2, 1, -1, 0)

    def rs1(p, k, i):
        a, b, d = RS_ORDER[p]
        two = rel(b, SUBSET[k])
        src = stage_ref(p, rel(a, HOP[i]), two, ALL)
        dst = rs_b.at[(i, *rest(p, two, ALL), pl.ds(*RS_PART[p]), ALL)]
        return remote(src, dst, send.at[p, 6], rs_r.at[p, 3 * k + i], near(a, HOP[i]))

    def rs1_wait(p, k, i):
        dst = rs_b.at[(i, *rest(p, rel(RS_ORDER[p][1], SUBSET[k]), ALL), pl.ds(*RS_PART[p]), ALL)]
        arrive(dst, rs_r.at[p, 3 * k + i])

    def rs2(p, i):
        a, b, d = RS_ORDER[p]
        src = stage_ref(p, me[a], rel(b, HOP[i]), ALL)
        dst = rs_c.at[i, :, pl.ds(*RS_PART[p]), :]
        return remote(src, dst, send.at[p, 7], rs_r.at[p, 12 + i], near(b, HOP[i]))

    def rs3(p, i):
        a, b, d = RS_ORDER[p]
        src = stage_ref(p, me[a], me[b], rel(d, HOP[i]))
        dst = rs_d.at[i, pl.ds(*RS_PART[p]), :]
        return remote(src, dst, send.at[p, 8], rs_r.at[p, 15 + i], near(d, HOP[i]))

    for k in range(4):
        own_second(rel("z", SUBSET[k]))
        for i in range(3):
            rs1(0, k, i).start()
            rs1(1, k, i).start()
        if k < 3:
            for m in range(4):
                rs1(2, m, k).start()
    def gain_copy(d):
        to = (tp + d) % 16
        return remote(gain_own.at[to], ex_gain.at[tp], misc_s.at[2], ex_r.at[6, d], (ph, to))

    for k in range(4):
        lax.fori_loop(k, k + 1, head_layer, 0)
        if k == 3:
            turned = jnp.transpose(gain_col[...])
            for t in range(16):
                gain_own[t] = jnp.broadcast_to(turned[t : t + 1], (8, 256))
            ex_gain[tp] = gain_own[tp]
            for d in range(1, 16):
                gain_copy(d).start()
        for p in PARTS:
            rows = pl.ds(*RS_PART[p])
            for i in range(3):
                rs1_wait(p, k, i)

            def add_first(n, _, p=p, k=k, rows=rows):
                two = rel(RS_ORDER[p][1], SUBSET[k])
                ref = own_ref(p, me[RS_ORDER[p][0]], two, n)
                total = ref[...]
                for i in range(3):
                    total = total + rs_b[(i, *rest(p, two, n), rows, ALL)].astype(F32)
                if k == 3:
                    ref[...] = total
                else:
                    stage_ref(p, me[RS_ORDER[p][0]], two, n)[...] = total.astype(BF16)
                return 0

            lax.fori_loop(0, 4, add_first, 0)
            if k < 3:
                rs2(p, k).start()
    for p in PARTS:
        rows = pl.ds(*RS_PART[p])
        for i in range(3):
            arrive(rs_c.at[i, :, rows, :], rs_r.at[p, 12 + i])

        def add_second(n, _, p=p, rows=rows):
            ref = own_ref(p, me[RS_ORDER[p][0]], me[RS_ORDER[p][1]], n)
            total = ref[...]
            for i in range(3):
                total = total + rs_c[i, n, rows, :].astype(F32)
            ref[...] = total
            stage_ref(p, me[RS_ORDER[p][0]], me[RS_ORDER[p][1]], n)[...] = total.astype(BF16)
            return 0

        lax.fori_loop(0, 4, add_second, 0)
        for i in range(3):
            rs3(p, i).start()
    for d in range(1, 16):
        gain_copy(d).wait_recv()
    total = ex_gain[0]
    for i in range(1, 16):
        total = total + ex_gain[i]
    ex_gain_ph[ph] = total
    gain_ph[0]()
    for p in PARTS:
        rows = pl.ds(*RS_PART[p])
        for i in range(3):
            arrive(rs_d.at[i, rows, :], rs_r.at[p, 15 + i])
        total = own_ref(p, *(me[axis] for axis in RS_ORDER[p]))[...]
        for i in range(3):
            total = total + rs_d[i, rows, :].astype(F32)
        fin[rows, :] = total

    rows = slab(ph)
    scale = scale_s[...]
    coefficient = scale * scale * col[rows, 2:3] / DS
    for h in range(2):
        cols = pl.ds(h * 128, 128)
        grad = fin[h * 64 : h * 64 + 64, :]
        rows_out[:, cols] = (scale * gain[h : h + 1] * grad - raw[:, h * 128 : h * 128 + 128] * coefficient).astype(BF16)
    sl[0:8, :] = jnp.broadcast_to(loss, (8, TOKENS))
    window = sl[0:1, pl.ds(pl.multiple_of(me["x"] * 128, 128), 128)]
    loss_out[...] = jnp.where(c == 1, window[:, 64:128], window[:, 0:64])

    for p in PARTS:
        rows = pl.ds(*PART_T[p])
        arrive(G.at[0, 0, 0, 0:3, rows, :], send.at[p, 0])
        arrive(G.at[0, 0:3, 0, :, rows, :], send.at[p, 1])
        arrive(G.at[0, 0:3, :, :, rows, :], send.at[p, 3])
        arrive(G.at[0, :, :, :, rows, :], send.at[p, 4])
        rows = pl.ds(*PART_S[p])
        arrive(G.at[0, 0:3, :, :, rows, :], send.at[p, 2])
        arrive(G.at[0, 0:3, 0:1, :, rows, :], send.at[p, 2])
        arrive(G.at[0, 0, 0, 0:3, rows, :], send.at[p, 2])
        arrive(G.at[0, :, :, :, rows, :], send.at[p, 5])
        rows = pl.ds(*RS_PART[p])
        arrive(rs_b.at[:, :, :, rows, :], send.at[p, 6])
        arrive(rs_c.at[:, :, rows, :], send.at[p, 7])
        arrive(rs_d.at[:, rows, :], send.at[p, 8])
    for ex in (early_y, early_z, early_ph, late_tp, late_ph):
        ex[2]()
    ws_push.wait_send()
    gp_push.wait_send()
    head_copy(14).wait()
    head_copy(15).wait()
    arrive(ex_gain.at[pl.ds(0, 15)], misc_s.at[2])
    gain_ph[1]()
    total = ex_gain_ph[0]
    for i in range(1, 8):
        total = total + ex_gain_ph[i]
    gain_out[...] = total[0:1] / jnp.concatenate([gain[0:1], gain[1:2]], axis=1)
    gain_ph[2]()


def out_kernel(
    head_in, loss_in, rows_in, gain_in, head_out, loss_out, rows_out, gain_out,
    head, loss, rows, gain, in_sem, out_sem,
):
    def part(ref, i):
        return ref.at[pl.ds(1024 * i, 1024)]

    ways = [(part(head_in, i), part(head, i), part(head_out, i)) for i in range(4)]
    ways += [(loss_in, loss, loss_out), (rows_in, rows, rows_out), (gain_in, gain, gain_out)]
    loads = [pltpu.make_async_copy(src, held, in_sem.at[i]) for i, (src, held, _) in enumerate(ways)]
    stores = [pltpu.make_async_copy(held, dst, out_sem.at[i]) for i, (_, held, dst) in enumerate(ways)]
    for load in loads:
        load.start()
    for load, store in zip(loads, stores):
        load.wait()
        store.start()
    for store in stores:
        store.wait()


def local(teacher_rows, teacher_gain, teacher_head, student_rows, student_gain, student_head, labels):
    vmem = pl.BlockSpec(memory_space=pltpu.VMEM)
    hbm = pl.BlockSpec(memory_space=pl.ANY)
    dma = pltpu.SemaphoreType.DMA
    loss, rows_grad, gain_grad, head_grad = pl.pallas_call(
        comm_kernel,
        out_shape=(
            jax.ShapeDtypeStruct((1, SLAB), F32),
            jax.ShapeDtypeStruct((SLAB, 256), BF16),
            jax.ShapeDtypeStruct((1, 256), F32),
            jax.ShapeDtypeStruct((16, 256, LOCAL_V), BF16),
        ),
        in_specs=[vmem, vmem, hbm, vmem, vmem, hbm, vmem],
        out_specs=(vmem, vmem, vmem, hbm),
        scratch_shapes=[
            pltpu.VMEM((2, 4, 4, 4, 640, 128), BF16),
            pltpu.VMEM((4, 2, 4, 4, 128, LOCAL_V), BF16),
            pltpu.VMEM((16, 256, LOCAL_V), BF16),
            pltpu.VMEM((16, 256, LOCAL_V), BF16),
            pltpu.VMEM((2, 256, LOCAL_V), BF16),
            pltpu.VMEM((TOKENS, LOCAL_V), F32),
            pltpu.VMEM((TOKENS, LOCAL_V), F32),
            pltpu.VMEM((TOKENS, LOCAL_V), F32),
            pltpu.VMEM((TOKENS, 128), F32),
            pltpu.VMEM((TOKENS, 128), F32),
            pltpu.VMEM((TOKENS, 128), F32),
            pltpu.VMEM((SLAB, 1), F32),
            pltpu.VMEM((TOKENS, LOCAL_V), BF16),
            pltpu.VMEM((2, 256, LOCAL_V), BF16),
            pltpu.VMEM((256, LOCAL_V), BF16),
            pltpu.VMEM((4, 4, 4, 128, 128), F32),
            pltpu.VMEM((3, 4, 4, 128, 128), BF16),
            pltpu.VMEM((3, 4, 128, 128), BF16),
            pltpu.VMEM((3, 128, 128), BF16),
            pltpu.VMEM((128, 128), F32),
            pltpu.VMEM((4, 8, 128), F32),
            pltpu.VMEM((4, 8, 128), F32),
            pltpu.VMEM((8, 8, 128), F32),
            pltpu.VMEM((16, 8, TOKENS), F32),
            pltpu.VMEM((8, 8, TOKENS), F32),
            pltpu.VMEM((256, 128), F32),
            pltpu.VMEM((16, 8, 256), F32),
            pltpu.VMEM((16, 8, 256), F32),
            pltpu.VMEM((8, 8, 256), F32),
            dma((5,)), dma((2,)), dma((3, 9)),
            dma((3, 3)), dma((3, 2)), dma((3, 2)), dma((3, 3)), dma((3, 3)), dma((3, 4)), dma((3, 16)),
            dma((3,)), dma((3, 16)), dma((6,)), dma((7, 16)), dma((3,)), dma((2,)), dma((3, 18)),
        ],
        compiler_params=pltpu.CompilerParams(
            collective_id=0, has_side_effects=True, vmem_limit_bytes=63 << 20
        ),
        name="distill",
    )(
        teacher_rows,
        teacher_gain.reshape(1, 128),
        teacher_head.reshape(4, 2, 4, 4, 128, LOCAL_V),
        student_rows,
        student_gain.reshape(2, 128),
        student_head.reshape(16, 256, LOCAL_V),
        labels.reshape(1, TOKENS),
    )
    head_grad, loss, rows_grad, gain_grad = pl.pallas_call(
        out_kernel,
        out_shape=(
            jax.ShapeDtypeStruct((DS, LOCAL_V), BF16),
            jax.ShapeDtypeStruct((1, SLAB), F32),
            jax.ShapeDtypeStruct((SLAB, 256), BF16),
            jax.ShapeDtypeStruct((1, 256), F32),
        ),
        in_specs=[hbm, hbm, hbm, hbm],
        out_specs=(hbm, hbm, hbm, hbm),
        scratch_shapes=[
            pltpu.VMEM((DS, LOCAL_V), BF16),
            pltpu.VMEM((1, SLAB), F32),
            pltpu.VMEM((SLAB, 256), BF16),
            pltpu.VMEM((1, 256), F32),
            dma((7,)),
            dma((7,)),
        ],
        compiler_params=pltpu.CompilerParams(vmem_limit_bytes=63 << 20),
        name="outputs",
    )(head_grad.reshape(DS, LOCAL_V), loss, rows_grad, gain_grad)
    return loss.reshape(SLAB), head_grad, rows_grad, gain_grad.reshape(256)


def solution(mesh):
    placed = (
        P(None, ("phase", "tp")),
        P(("phase", "tp")),
        P(None, ("phase", "tp")),
        P("phase", "tp"),
        P("tp"),
        P(None, ("phase", "tp")),
        P(),
    )
    return jax.shard_map(
        local,
        mesh=mesh,
        in_specs=placed,
        out_specs=(P("phase"), P(None, ("phase", "tp")), P("phase", "tp"), P("tp")),
        check_vma=False,
    )
```

```python
import jax
import jax.numpy as jnp
from jax import lax
from jax.experimental import pallas as pl
from jax.experimental.pallas import tpu as pltpu
from jax.sharding import PartitionSpec as P

NORM_EPSILON = 1e-05
LABEL_WEIGHT = 0.5
F32 = jnp.float32
BF16 = jnp.bfloat16
MESH = pl.DeviceIdType.MESH

DT, DS, TOKENS, LOCAL_V = 16384, 4096, 512, 512
SLAB = 64
PART = ((0, 208), (208, 208), (416, 224))
PART_S = ((0, 48), (208, 48), (416, 32))
PART_T = ((48, 160), (256, 160), (448, 192))
TOKEN_T = (0, 160, 320)
ORDER = (("x", "y", "z"), ("y", "z", "x"), ("z", "x", "y"))
RS_ORDER = (("x", "z", "y"), ("y", "z", "x"), ("z", "x", "y"))
RS_PART = ((0, 48), (48, 48), (96, 48))
ALL = slice(None)
LOW, HIGH = pl.ds(0, 2), pl.ds(2, 2)


def comm_kernel(
    t_rows, t_gain, wt_hbm, s_rows, s_gain, ws_hbm, labels,
    loss_out, rows_out, gain_out, head_out,
    G, wt, ws, ws_sib, head_part, acc_t, sl, es, st, col, lab, scale_s, g_ref, gp, gp_in, own,
    rs_b, rs_c, rs_d, fin, ex_y0, ex_z0, ex_ph0, ex_tp1, ex_ph1, gain_in,
    w_sem, out_sem, send, r1, r2, r2f, r1s, r2s, r3s, r3t, sibs_r, sibt_r, ex_s, ex_r, misc_s, misc_r, rs_r,
):
    ph = lax.axis_index("phase")
    tp = lax.axis_index("tp")
    c = ph % 2
    me = {"x": ph // 2, "y": tp % 4, "z": tp // 4}
    sib = (ph + 1 - 2 * c, tp)
    PARTS = range(3)
    STEP = (0, -1, 1, 2)

    def rel(axis, step):
        return (me[axis] + step + 4) % 4

    def near(axis, step):
        at = dict(me)
        at[axis] = rel(axis, step)
        return (at["x"] * 2 + c, at["z"] * 4 + at["y"])

    def remote(src, dst, ssem, rsem, to):
        return pltpu.make_async_remote_copy(
            src_ref=src, dst_ref=dst, send_sem=ssem, recv_sem=rsem, device_id=to, device_id_type=MESH
        )

    wt_loads = [pltpu.make_async_copy(wt_hbm.at[i], wt.at[i], w_sem.at[i]) for i in range(4)]
    ws_load = pltpu.make_async_copy(ws_hbm, ws, w_sem.at[4])
    ws_load.start()
    for load in wt_loads:
        load.start()

    barrier = pltpu.get_barrier_semaphore()
    partners = [sib] + [near(axis, step) for axis in "xyz" for step in (1, -1, 2)]
    for to in partners:
        pl.semaphore_signal(barrier, inc=1, device_id=to, device_id_type=MESH)

    mine = G.at[c, me["x"], me["z"], me["y"]]
    wide = t_rows[...].astype(F32)
    scaled = (wide * t_gain[...].astype(F32)).astype(BF16)
    for (row, size), token in zip(PART_T, TOKEN_T):
        mine[pl.ds(row, size), :] = scaled[token : token + size]
    pl.semaphore_wait(barrier, len(partners))

    def block(p, one, two, three, rows, core=None):
        a, b, d = ORDER[p]
        at = {a: one, b: two, d: three}
        return G.at[c if core is None else core, at["x"], at["z"], at["y"], pl.ds(*rows), :]

    def own_at(p):
        return tuple(me[axis] for axis in ORDER[p])

    def p1(p, i):
        ref = block(p, *own_at(p), PART_T[p])
        return remote(ref, ref, send.at[p, 0], r1.at[p, i], near(ORDER[p][0], (-1, 1, 2)[i]))

    def p2(p, n, i):
        a, b, d = ORDER[p]
        ref = block(p, rel(a, STEP[n]), me[b], me[d], PART_T[p])
        return remote(ref, ref, send.at[p, 1], r2.at[p, i], near(b, (1, -1)[i]))

    def p2f(p, i):
        a, b, d = ORDER[p]
        ref = block(p, (LOW, HIGH)[i], rel(b, (-1, 1)[i]), me[d], PART_T[p])
        return remote(ref, ref, send.at[p, 1], r2f.at[p, i], near(b, (1, -1)[i]))

    def p1s(p, i):
        ref = block(p, *own_at(p), PART_S[p])
        return remote(ref, ref, send.at[p, 2], r1s.at[p, i], near(ORDER[p][0], (-1, 1, 2)[i]))

    def p2s(p, i):
        a, b, d = ORDER[p]
        ref = block(p, ALL, me[b], me[d], PART_S[p])
        return remote(ref, ref, send.at[p, 2], r2s.at[p, i], near(b, (-1, 1, 2)[i]))

    def p3s(p, i):
        d = ORDER[p][2]
        ref = block(p, (ALL, ALL, LOW, HIGH)[i], ALL, rel(d, (0, 0, -1, 1)[i]), PART_S[p])
        return remote(ref, ref, send.at[p, 2], r3s.at[p, i], near(d, (1, -1, 1, -1)[i]))

    def p3t(p, j, i):
        a, b, d = ORDER[p]
        ref = block(p, (ALL, ALL, LOW, HIGH)[i], rel(b, STEP[j]), rel(d, (0, 0, -1, 1)[i]), PART_T[p])
        return remote(ref, ref, send.at[p, 3], r3t.at[p, 4 * j + i], near(d, (1, -1, 1, -1)[i]))

    def arrive(ref, sem):
        pltpu.make_async_copy(ref, ref, sem).wait()

    def p2_wait(p, i):
        a, b, d = ORDER[p]
        arrive(block(p, ALL, rel(b, (-1, 1)[i]), me[d], PART_T[p]), r2.at[p, i])

    def p2f_wait(p, i):
        a, b, d = ORDER[p]
        arrive(block(p, (LOW, HIGH)[i], rel(b, 2), me[d], PART_T[p]), r2f.at[p, i])

    def p1s_wait(p, i):
        a, b, d = ORDER[p]
        arrive(block(p, rel(a, (1, -1, 2)[i]), me[b], me[d], PART_S[p]), r1s.at[p, i])

    def p2s_wait(p, i):
        a, b, d = ORDER[p]
        arrive(block(p, ALL, rel(b, (1, -1, 2)[i]), me[d], PART_S[p]), r2s.at[p, i])

    def p3s_wait(p, i):
        d = ORDER[p][2]
        arrive(block(p, (ALL, ALL, LOW, HIGH)[i], ALL, rel(d, (-1, 1, 2, 2)[i]), PART_S[p]), r3s.at[p, i])

    def p3t_wait(p, j, i):
        a, b, d = ORDER[p]
        ref = block(p, (ALL, ALL, LOW, HIGH)[i], rel(b, STEP[j]), rel(d, (-1, 1, 2, 2)[i]), PART_T[p])
        arrive(ref, r3t.at[p, 4 * j + i])

    def sib_t(p, j, k, core=None):
        a, b, d = ORDER[p]
        ref = block(p, ALL, rel(b, STEP[j]), rel(d, STEP[k]), PART_T[p], core)
        return remote(ref, ref, send.at[p, 4], sibt_r.at[p, 4 * j + k], sib)

    def sib_s(p, core):
        ref = G.at[core, :, :, :, pl.ds(*PART_S[p]), :]
        return remote(ref, ref, send.at[p, 5], sibs_r.at[p], sib)

    def p3t_send(j):
        for p in PARTS:
            p3t(p, j, 0).start()
            p3t(p, j, 1).start()

    def products(j, k, core):
        for p in PARTS:
            a, b, d = ORDER[p]
            at = {a: ALL, b: rel(b, STEP[j]), d: rel(d, STEP[k])}
            rows = G[core, at["x"], at["z"], at["y"], pl.ds(*PART_T[p]), :]
            lhs = jnp.concatenate([rows[i] for i in range(4)], axis=1)
            rhs = wt[at["x"], core, at["z"], at["y"]].reshape(512, LOCAL_V)
            acc_t[pl.ds(TOKEN_T[p], PART_T[p][1]), :] += jnp.dot(lhs, rhs, preferred_element_type=F32)

    def sib_wait(j, k):
        for p in PARTS:
            a, b, d = ORDER[p]
            arrive(block(p, ALL, rel(b, STEP[j]), rel(d, STEP[k]), PART_T[p], 1 - c), sibt_r.at[p, 4 * j + k])

    def consume(j, k):
        sib_wait(j, k)

        def one_core(core, _):
            products(j, k, core)
            return 0

        lax.fori_loop(0, 2, one_core, 0)

    def rowsum(value):
        return jnp.sum(value, axis=1, keepdims=True)

    def to_tp(d):
        return (ph, (tp + d) % 16)

    def to_ph(d):
        return ((ph + d) % 8, tp)

    def exchange(buf, slot, count, number, to):
        def copy(d):
            return remote(buf.at[slot], buf.at[slot], ex_s.at[number], ex_r.at[number, d], to(d))

        def start():
            for d in range(1, count):
                copy(d).start()

        def wait():
            for d in range(1, count):
                copy(d).wait_recv()

        def sent():
            arrive(buf.at[pl.ds(0, count - 1)], ex_s.at[number])

        return start, wait, sent

    early_y = exchange(ex_y0, me["y"], 4, 0, lambda d: near("y", d))
    early_z = exchange(ex_z0, me["z"], 4, 5, lambda d: near("z", d))
    early_ph = exchange(ex_ph0, ph, 8, 1, to_ph)
    late_tp = exchange(ex_tp1, tp, 16, 2, to_tp)
    late_ph = exchange(ex_ph1, ph, 8, 3, to_ph)

    def to_columns(rows):
        filled = jnp.concatenate(rows + [jnp.zeros((128 - len(rows), TOKENS), F32)], axis=0)
        return jnp.transpose(filled)

    for i in range(3):
        for p in PARTS:
            p1(p, i).start()
    for p in PARTS:
        p2(p, 0, 0).start()
        p2(p, 0, 1).start()
    raw = s_rows[...].astype(F32)
    raw_squares = rowsum(raw * raw)
    lane_t = lax.broadcasted_iota(jnp.int32, (TOKENS, 128), 1)
    st[...] = jnp.where(lane_t == 0, rowsum(wide * wide), 0.0)
    st[0:SLAB, :] = jnp.where(lane_t[0:SLAB] == 1, raw_squares, st[0:SLAB, :])
    squares = jnp.transpose(st[...])
    ex_y0[me["y"]] = jnp.concatenate(
        [squares[0:1, 128 * i : 128 * i + 128] for i in range(4)]
        + [squares[1:2, 0:128], jnp.zeros((3, 128), F32)],
        axis=0,
    )
    early_y[0]()
    lab[...] = to_columns([labels[...].astype(F32)])
    acc_t[...] = jnp.zeros_like(acc_t)
    for n in (1, 2, 3):
        for p in PARTS:
            a, b, d = ORDER[p]
            arrive(block(p, rel(a, STEP[n]), me[b], me[d], PART_T[p]), r1.at[p, (1, 0, 2)[n - 1]])
            p2(p, n, 0).start()
            p2(p, n, 1).start()
    p3t_send(0)
    early_y[1]()
    ex_z0[me["z"]] = ex_y0[0] + ex_y0[1] + ex_y0[2] + ex_y0[3]
    early_z[0]()
    for p in PARTS:
        sib_t(p, 0, 0).start()
    for i in (0, 1):
        for p in PARTS:
            p2_wait(p, i)
            p2f(p, i).start()
            sib_t(p, i + 1, 0).start()
    early_z[1]()
    early = ex_z0[0] + ex_z0[1] + ex_z0[2] + ex_z0[3]
    ex_ph0[ph] = early
    turned = jnp.transpose(jnp.concatenate([early, jnp.zeros((120, 128), F32)], axis=0))
    own_scale = lax.rsqrt(turned[0:SLAB, 4:5] / DS + NORM_EPSILON)
    scale_s[...] = own_scale
    gain = s_gain[...].astype(F32)
    left = (raw[:, 0:128] * own_scale * gain[0:1]).astype(BF16)
    right = (raw[:, 128:256] * own_scale * gain[1:2]).astype(BF16)
    mine[0:48, :] = left[0:48]
    mine[208:224, :] = left[48:64]
    mine[224:256, :] = right[0:32]
    mine[416:448, :] = right[32:64]
    for i in range(3):
        for p in PARTS:
            p1s(p, i).start()
    for p in PARTS:
        p2f_wait(p, 0)
        p2f_wait(p, 1)
        sib_t(p, 3, 0).start()
    p3t_send(1)
    ws_load.wait()
    ws_push = remote(ws, ws_sib, misc_s.at[0], misc_r.at[0], sib)
    ws_push.start()
    for load in wt_loads:
        load.wait()
    for p in PARTS:
        for i in range(3):
            p1s_wait(p, i)
        for i in range(3):
            p2s(p, i).start()
    consume(0, 0)

    def forward(j):
        for i in (0, 1):
            for p in PARTS:
                p3t_wait(p, j, i)
                p3t(p, j, i + 2).start()
                sib_t(p, j, i + 1).start()

    def opposite(j):
        for p in PARTS:
            p3t_wait(p, j, 2)
            p3t_wait(p, j, 3)
            sib_t(p, j, 3).start()

    forward(0)
    consume(1, 0)
    for p in PARTS:
        for i in range(3):
            p2s_wait(p, i)
        p3s(p, 0).start()
        p3s(p, 1).start()
    p3t_send(2)
    early_ph[0]()
    consume(2, 0)
    consume(3, 0)
    forward(1)
    for i in (0, 1):
        for p in PARTS:
            p3s_wait(p, i)
            p3s(p, i + 2).start()
    p3t_send(3)
    consume(0, 1)
    consume(0, 2)
    opposite(0)
    consume(1, 1)
    early_ph[1]()
    early = ex_ph0[0]
    for i in range(1, 8):
        early = early + ex_ph0[i]
    teacher_scale = lax.rsqrt(jnp.concatenate([early[i : i + 1] for i in range(4)], axis=1) / DT + NORM_EPSILON)
    col[...] = to_columns([teacher_scale])
    for p in PARTS:
        p3s_wait(p, 2)
        p3s_wait(p, 3)
        sib_s(p, c).start()
    consume(1, 2)
    consume(0, 3)
    for p in PARTS:
        arrive(G.at[1 - c, :, :, :, pl.ds(*PART_S[p]), :], sibs_r.at[p])

    def slab(q):
        return pl.ds(pl.multiple_of(q * SLAB, SLAB), SLAB)

    def normed(z, y):
        slabs = []
        for q in range(8):
            ref = G.at[q % 2, q // 2, z, y]
            first = jnp.concatenate([ref[0:48, :], ref[208:224, :]], axis=0)
            second = jnp.concatenate([ref[224:256, :], ref[416:448, :]], axis=0)
            slabs.append(jnp.concatenate([first, second], axis=1))
        return jnp.concatenate(slabs, axis=0)

    def student_dot(z, half):
        t = 4 * z + 2 * half
        lhs = jnp.concatenate([normed(z, 2 * half), normed(z, 2 * half + 1)], axis=1)
        rhs = jnp.concatenate([ws[t], ws[t + 1]], axis=0)
        return jnp.dot(lhs, rhs, preferred_element_type=F32)

    def student_dots(z, _):
        sl[...] += student_dot(z, 0)
        sl[...] += student_dot(z, 1)
        return 0

    def nt_dot(lhs, rhs):
        return lax.dot_general(lhs, rhs, (((1,), (1,)), ((), ())), preferred_element_type=F32)

    eye = (
        lax.broadcasted_iota(jnp.int32, (256, 256), 0) == lax.broadcasted_iota(jnp.int32, (256, 256), 1)
    ).astype(F32).astype(BF16)

    def head_copy(t, y):
        return pltpu.make_async_copy(head_part.at[y % 2], head_out.at[t], out_sem.at[y % 2])

    lane_c = lax.broadcasted_iota(jnp.int32, (256, 128), 1)

    def head_layer(z, first):
        sums = jnp.zeros((256, 128), F32)
        for y in range(4):
            t = 4 * z + y
            if y >= 2 or not first:
                head_copy(t, y).wait()
            turned = nt_dot(eye, normed(z, y)).astype(BF16)
            grad = jnp.dot(turned, g_ref[...], preferred_element_type=F32)
            head_part[y % 2] = grad.astype(BF16)
            head_copy(t, y).start()
            sums = jnp.where(lane_c == y, rowsum(grad * ws[t].astype(F32)), sums)
        sums = jnp.transpose(sums)
        for y in range(4):
            band = jnp.concatenate(
                [sums[y : y + 1, 0:128], sums[y : y + 1, 128:256], jnp.zeros((14, 128), F32)], axis=0
            )
            for xt in range(4):
                own[xt, z, y, 128:144] = band
                wt[xt, 0, z, y, 32:48, 128:256] = band.astype(BF16)

    sl[...] = student_dot(0, 0)
    sl[...] += student_dot(0, 1)
    forward(2)
    lax.fori_loop(1, 4, student_dots, 0)
    opposite(1)
    lane = lax.broadcasted_iota(jnp.int32, (SLAB, 128), 1)
    vocab_first = ((ph * 16 + tp) * LOCAL_V).astype(F32)

    def label_hit(rows):
        ids = lax.broadcasted_iota(jnp.int32, (SLAB, LOCAL_V), 1).astype(F32) + vocab_first
        return lab[rows, 0:1] == ids

    def pack(columns, first, out):
        for i, column in enumerate(columns):
            out = jnp.where(lane == first + i, column, out)
        return out

    def student_stats(n, _):
        student_slab(2 * n)
        student_slab(2 * n + 1)
        return 0

    def student_slab(q):
        rows = slab(q)
        logits = sl[rows, :]
        top = jnp.max(logits, axis=1, keepdims=True)
        e = jnp.exp(logits - top)
        es[rows, :] = e
        picked = jnp.where(label_hit(rows), logits, 0.0)
        st[rows, :] = pack(
            [top, rowsum(e), rowsum(e * logits), rowsum(picked)], 4, jnp.zeros((SLAB, 128), F32)
        )

    lax.fori_loop(0, 4, student_stats, 0)
    consume(2, 1)
    consume(2, 2)
    forward(3)
    consume(1, 3)
    opposite(2)
    consume(3, 1)
    consume(3, 2)
    consume(2, 3)
    opposite(3)
    products(3, 3, c)
    sib_wait(3, 3)
    products(3, 3, 1 - c)

    def teacher_stats(n, _):
        teacher_slab(2 * n)
        teacher_slab(2 * n + 1)
        return 0

    def teacher_slab(q):
        rows = slab(q)
        logits = acc_t[rows, :] * col[rows, 0:1]
        student = sl[rows, :]
        top = jnp.max(logits, axis=1, keepdims=True)
        e = jnp.exp(logits - top)
        acc_t[rows, :] = e
        st[rows, :] = pack([top, rowsum(e), rowsum(e * (logits - student)), rowsum(e * student)], 0, st[rows, :])

    lax.fori_loop(0, 4, teacher_stats, 0)
    stats = jnp.transpose(st[...])[0:8, :]
    sub = lax.broadcasted_iota(jnp.int32, (8, TOKENS), 0)

    def merge(buf, count):
        t_top, s_top = buf[0, 0:1, :], buf[0, 4:5, :]
        for i in range(1, count):
            t_top = jnp.maximum(t_top, buf[i, 0:1, :])
            s_top = jnp.maximum(s_top, buf[i, 4:5, :])
        total = jnp.zeros((8, TOKENS), F32)
        for i in range(count):
            weight = jnp.where(sub < 4, jnp.exp(buf[i, 0:1, :] - t_top), jnp.exp(buf[i, 4:5, :] - s_top))
            total = total + buf[i] * jnp.where(sub == 7, 1.0, weight)
        return jnp.where(sub == 0, t_top, jnp.where(sub == 4, s_top, total))

    ex_tp1[tp] = stats
    late_tp[0]()
    late_tp[1]()
    ex_ph1[ph] = merge(ex_tp1, 16)
    late_ph[0]()
    late_ph[1]()
    late = merge(ex_ph1, 8)
    teacher_top, teacher_total, student_top, student_total = late[0:1], late[1:2], late[4:5], late[5:6]
    picked_all = late[7:8]
    teacher_lse = teacher_top + jnp.log(teacher_total)
    student_lse = student_top + jnp.log(student_total)
    loss = (
        late[2:3] / teacher_total - teacher_lse + student_lse + LABEL_WEIGHT * (student_lse - picked_all)
    )
    inner = (
        (1.0 + LABEL_WEIGHT) * late[6:7] / student_total - late[3:4] / teacher_total - LABEL_WEIGHT * picked_all
    )
    t_factor = jnp.exp(stats[0:1] - teacher_top) / teacher_total
    s_factor = (1.0 + LABEL_WEIGHT) * jnp.exp(stats[4:5] - student_top) / student_total
    col[...] = to_columns([t_factor, s_factor, inner])

    def logit_grad(n, which):
        q = 2 * n + (c if which == 0 else 1 - c)
        rows = slab(q)
        g = (
            es[rows, :] * col[rows, 1:2]
            - acc_t[rows, :] * col[rows, 0:1]
            - LABEL_WEIGHT * label_hit(rows).astype(F32)
        ).astype(BF16)
        g_ref[rows, :] = g
        gp[which, slab(n), :] = g

    for which in (1, 0):

        def grad_step(n, _, which=which):
            logit_grad(2 * n, which)
            logit_grad(2 * n + 1, which)
            return 0

        lax.fori_loop(0, 2, grad_step, 0)
        if which == 1:
            gp_push = remote(gp.at[1], gp_in, misc_s.at[1], misc_r.at[1], sib)
            gp_push.start()

    def own_first(z, _):
        for y in range(4):
            r = nt_dot(gp[0], ws[4 * z + y])
            for xt in range(4):
                own[xt, z, y, 0:64] = r[xt * 64 : xt * 64 + 64, 0:128]
                own[xt, z, y, 64:128] = r[xt * 64 : xt * 64 + 64, 128:256]
        return 0

    def own_second(z):
        for y in range(4):
            r = nt_dot(gp_in[...], ws_sib[4 * z + y])
            for xt in range(4):
                total = own[xt, z, y, 0:64] + r[xt * 64 : xt * 64 + 64, 0:128]
                own[xt, z, y, 0:64] = total
                wt[xt, 0, z, y, 0:64, 0:128] = total.astype(BF16)
                total = own[xt, z, y, 64:128] + r[xt * 64 : xt * 64 + 64, 128:256]
                own[xt, z, y, 64:128] = total
                wt[xt, 0, z, y, 64:96, 0:128] = total[0:32].astype(BF16)
                wt[xt, 0, z, y, 0:32, 128:256] = total[32:64].astype(BF16)

    lax.fori_loop(0, 4, own_first, 0)
    ws_push.wait_recv()
    gp_push.wait_recv()

    def at3(p, one, two, three):
        a, b, d = RS_ORDER[p]
        at = {a: one, b: two, d: three}
        return at["x"], at["z"], at["y"]

    def rest(p, two, three):
        at = {RS_ORDER[p][1]: two, RS_ORDER[p][2]: three}
        return tuple(at[axis] for axis in ("x", "z", "y") if axis in at)

    def stage_ref(p, one, two, three):
        ix, iz, iy = at3(p, one, two, three)
        row, size = ((0, 48), (48, 48), (0, 48))[p]
        return wt.at[ix, 0, iz, iy, pl.ds(row, size), pl.ds(128 if p == 2 else 0, 128)]

    def own_ref(p, one, two, three):
        ix, iz, iy = at3(p, one, two, three)
        return own.at[ix, iz, iy, pl.ds(*RS_PART[p]), :]

    HOP = (2, 1, -1)
    SUBSET = (2, 1, -1, 0)

    def rs1(p, k, i):
        a, b, d = RS_ORDER[p]
        two = rel(b, SUBSET[k])
        src = stage_ref(p, rel(a, HOP[i]), two, ALL)
        dst = rs_b.at[(i, *rest(p, two, ALL), pl.ds(*RS_PART[p]), ALL)]
        return remote(src, dst, send.at[p, 6], rs_r.at[p, 3 * k + i], near(a, HOP[i]))

    def rs1_wait(p, k, i):
        dst = rs_b.at[(i, *rest(p, rel(RS_ORDER[p][1], SUBSET[k]), ALL), pl.ds(*RS_PART[p]), ALL)]
        arrive(dst, rs_r.at[p, 3 * k + i])

    def rs2(p, i):
        a, b, d = RS_ORDER[p]
        src = stage_ref(p, me[a], rel(b, HOP[i]), ALL)
        dst = rs_c.at[i, :, pl.ds(*RS_PART[p]), :]
        return remote(src, dst, send.at[p, 7], rs_r.at[p, 12 + i], near(b, HOP[i]))

    def rs3(p, i):
        a, b, d = RS_ORDER[p]
        src = stage_ref(p, me[a], me[b], rel(d, HOP[i]))
        dst = rs_d.at[i, pl.ds(*RS_PART[p]), :]
        return remote(src, dst, send.at[p, 8], rs_r.at[p, 15 + i], near(d, HOP[i]))

    for k in range(4):
        own_second(rel("z", SUBSET[k]))
        for i in range(3):
            rs1(0, k, i).start()
            rs1(1, k, i).start()
        head_layer(rel("z", SUBSET[k]), k == 0)
        if k < 3:
            for m in range(4):
                rs1(2, m, k).start()

    def first_sum(p, k):
        rows = pl.ds(*RS_PART[p])
        for i in range(3):
            rs1_wait(p, k, i)

        def add_first(n, _):
            two = rel(RS_ORDER[p][1], SUBSET[k])
            ref = own_ref(p, me[RS_ORDER[p][0]], two, n)
            total = ref[...]
            for i in range(3):
                total = total + rs_b[(i, *rest(p, two, n), rows, ALL)].astype(F32)
            if k == 3:
                ref[...] = total
            else:
                stage_ref(p, me[RS_ORDER[p][0]], two, n)[...] = total.astype(BF16)
            return 0

        lax.fori_loop(0, 4, add_first, 0)
        if k < 3:
            rs2(p, k).start()

    for k in range(3):
        first_sum(0, k)
        first_sum(1, k)
    for k in range(4):
        first_sum(2, k)
    first_sum(0, 3)
    first_sum(1, 3)
    for p in PARTS:
        rows = pl.ds(*RS_PART[p])
        for i in range(3):
            arrive(rs_c.at[i, :, rows, :], rs_r.at[p, 12 + i])

        def add_second(n, _, p=p, rows=rows):
            ref = own_ref(p, me[RS_ORDER[p][0]], me[RS_ORDER[p][1]], n)
            total = ref[...]
            for i in range(3):
                total = total + rs_c[i, n, rows, :].astype(F32)
            ref[...] = total
            stage_ref(p, me[RS_ORDER[p][0]], me[RS_ORDER[p][1]], n)[...] = total.astype(BF16)
            return 0

        lax.fori_loop(0, 4, add_second, 0)
        for i in range(3):
            rs3(p, i).start()
    for p in PARTS:
        rows = pl.ds(*RS_PART[p])
        for i in range(3):
            arrive(rs_d.at[i, rows, :], rs_r.at[p, 15 + i])
        total = own_ref(p, *(me[axis] for axis in RS_ORDER[p]))[...]
        for i in range(3):
            total = total + rs_d[i, rows, :].astype(F32)
        fin[rows, :] = total

    gain_push = remote(fin.at[pl.ds(128, 8)], gain_in, misc_s.at[2], misc_r.at[2], sib)
    gain_push.start()
    rows = slab(ph)
    scale = scale_s[...]
    coefficient = scale * scale * col[rows, 2:3] / DS
    for h in range(2):
        cols = pl.ds(h * 128, 128)
        grad = fin[h * 64 : h * 64 + 64, :]
        rows_out[:, cols] = (scale * gain[h : h + 1] * grad - raw[:, h * 128 : h * 128 + 128] * coefficient).astype(BF16)
    sl[0:8, :] = jnp.broadcast_to(loss, (8, TOKENS))
    window = sl[0:1, pl.ds(pl.multiple_of(me["x"] * 128, 128), 128)]
    loss_out[...] = jnp.where(c == 1, window[:, 64:128], window[:, 0:64])

    for p in PARTS:
        rows = pl.ds(*PART_T[p])
        arrive(G.at[0, 0, 0, 0:3, rows, :], send.at[p, 0])
        arrive(G.at[0, 0:3, 0, :, rows, :], send.at[p, 1])
        arrive(G.at[0, 0:3, :, :, rows, :], send.at[p, 3])
        arrive(G.at[0, :, :, :, rows, :], send.at[p, 4])
        rows = pl.ds(*PART_S[p])
        arrive(G.at[0, 0:3, :, :, rows, :], send.at[p, 2])
        arrive(G.at[0, 0:3, 0:1, :, rows, :], send.at[p, 2])
        arrive(G.at[0, 0, 0, 0:3, rows, :], send.at[p, 2])
        arrive(G.at[0, :, :, :, rows, :], send.at[p, 5])
        rows = pl.ds(*RS_PART[p])
        arrive(rs_b.at[:, :, :, rows, :], send.at[p, 6])
        arrive(rs_c.at[:, :, rows, :], send.at[p, 7])
        arrive(rs_d.at[:, rows, :], send.at[p, 8])
    for ex in (early_y, early_z, early_ph, late_tp, late_ph):
        ex[2]()
    ws_push.wait_send()
    gp_push.wait_send()
    head_copy(14, 0).wait()
    head_copy(15, 1).wait()
    gain_push.wait_recv()
    total = (fin[128:136, :] + gain_in[...])[0:2] / gain
    gain_out[...] = jnp.concatenate([total[0:1], total[1:2]], axis=1)
    gain_push.wait_send()


def out_kernel(
    head_in, loss_in, rows_in, gain_in, head_out, loss_out, rows_out, gain_out,
    head, loss, rows, gain, in_sem, out_sem,
):
    def part(ref, i):
        return ref.at[pl.ds(1024 * i, 1024)]

    ways = [(part(head_in, i), part(head, i), part(head_out, i)) for i in range(4)]
    ways += [(loss_in, loss, loss_out), (rows_in, rows, rows_out), (gain_in, gain, gain_out)]
    loads = [pltpu.make_async_copy(src, held, in_sem.at[i]) for i, (src, held, _) in enumerate(ways)]
    stores = [pltpu.make_async_copy(held, dst, out_sem.at[i]) for i, (_, held, dst) in enumerate(ways)]
    for load in loads:
        load.start()
    for load, store in zip(loads, stores):
        load.wait()
        store.start()
    for store in stores:
        store.wait()


def local(teacher_rows, teacher_gain, teacher_head, student_rows, student_gain, student_head, labels):
    vmem = pl.BlockSpec(memory_space=pltpu.VMEM)
    hbm = pl.BlockSpec(memory_space=pl.ANY)
    dma = pltpu.SemaphoreType.DMA
    loss, rows_grad, gain_grad, head_grad = pl.pallas_call(
        comm_kernel,
        out_shape=(
            jax.ShapeDtypeStruct((1, SLAB), F32),
            jax.ShapeDtypeStruct((SLAB, 256), BF16),
            jax.ShapeDtypeStruct((1, 256), F32),
            jax.ShapeDtypeStruct((16, 256, LOCAL_V), BF16),
        ),
        in_specs=[vmem, vmem, hbm, vmem, vmem, hbm, vmem],
        out_specs=(vmem, vmem, vmem, hbm),
        scratch_shapes=[
            pltpu.VMEM((2, 4, 4, 4, 640, 128), BF16),
            pltpu.VMEM((4, 2, 4, 4, 128, LOCAL_V), BF16),
            pltpu.VMEM((16, 256, LOCAL_V), BF16),
            pltpu.VMEM((16, 256, LOCAL_V), BF16),
            pltpu.VMEM((2, 256, LOCAL_V), BF16),
            pltpu.VMEM((TOKENS, LOCAL_V), F32),
            pltpu.VMEM((TOKENS, LOCAL_V), F32),
            pltpu.VMEM((TOKENS, LOCAL_V), F32),
            pltpu.VMEM((TOKENS, 128), F32),
            pltpu.VMEM((TOKENS, 128), F32),
            pltpu.VMEM((TOKENS, 128), F32),
            pltpu.VMEM((SLAB, 1), F32),
            pltpu.VMEM((TOKENS, LOCAL_V), BF16),
            pltpu.VMEM((2, 256, LOCAL_V), BF16),
            pltpu.VMEM((256, LOCAL_V), BF16),
            pltpu.VMEM((4, 4, 4, 144, 128), F32),
            pltpu.VMEM((3, 4, 4, 144, 128), BF16),
            pltpu.VMEM((3, 4, 144, 128), BF16),
            pltpu.VMEM((3, 144, 128), BF16),
            pltpu.VMEM((144, 128), F32),
            pltpu.VMEM((4, 8, 128), F32),
            pltpu.VMEM((4, 8, 128), F32),
            pltpu.VMEM((8, 8, 128), F32),
            pltpu.VMEM((16, 8, TOKENS), F32),
            pltpu.VMEM((8, 8, TOKENS), F32),
            pltpu.VMEM((8, 128), F32),
            dma((5,)), dma((2,)), dma((3, 9)),
            dma((3, 3)), dma((3, 2)), dma((3, 2)), dma((3, 3)), dma((3, 3)), dma((3, 4)), dma((3, 16)),
            dma((3,)), dma((3, 16)), dma((6,)), dma((6, 16)), dma((3,)), dma((3,)), dma((3, 18)),
        ],
        compiler_params=pltpu.CompilerParams(
            collective_id=0, has_side_effects=True, vmem_limit_bytes=63 << 20
        ),
        name="distill",
    )(
        teacher_rows,
        teacher_gain.reshape(1, 128),
        teacher_head.reshape(4, 2, 4, 4, 128, LOCAL_V),
        student_rows,
        student_gain.reshape(2, 128),
        student_head.reshape(16, 256, LOCAL_V),
        labels.reshape(1, TOKENS),
    )
    head_grad, loss, rows_grad, gain_grad = pl.pallas_call(
        out_kernel,
        out_shape=(
            jax.ShapeDtypeStruct((DS, LOCAL_V), BF16),
            jax.ShapeDtypeStruct((1, SLAB), F32),
            jax.ShapeDtypeStruct((SLAB, 256), BF16),
            jax.ShapeDtypeStruct((1, 256), F32),
        ),
        in_specs=[hbm, hbm, hbm, hbm],
        out_specs=(hbm, hbm, hbm, hbm),
        scratch_shapes=[
            pltpu.VMEM((DS, LOCAL_V), BF16),
            pltpu.VMEM((1, SLAB), F32),
            pltpu.VMEM((SLAB, 256), BF16),
            pltpu.VMEM((1, 256), F32),
            dma((7,)),
            dma((7,)),
        ],
        compiler_params=pltpu.CompilerParams(vmem_limit_bytes=63 << 20),
        name="outputs",
    )(head_grad.reshape(DS, LOCAL_V), loss, rows_grad, gain_grad)
    return loss.reshape(SLAB), head_grad, rows_grad, gain_grad.reshape(256)


def solution(mesh):
    placed = (
        P(None, ("phase", "tp")),
        P(("phase", "tp")),
        P(None, ("phase", "tp")),
        P("phase", "tp"),
        P("tp"),
        P(None, ("phase", "tp")),
        P(),
    )
    return jax.shard_map(
        local,
        mesh=mesh,
        in_specs=placed,
        out_specs=(P("phase"), P(None, ("phase", "tp")), P("phase", "tp"), P("tp")),
        check_vma=False,
    )
```

```python
import jax
import jax.numpy as jnp
from jax import lax
from jax.experimental import pallas as pl
from jax.experimental.pallas import tpu as pltpu
from jax.sharding import PartitionSpec as P

NORM_EPSILON = 1e-05
LABEL_WEIGHT = 0.5
F32 = jnp.float32
BF16 = jnp.bfloat16
MESH = pl.DeviceIdType.MESH

DT, DS, TOKENS, LOCAL_V = 16384, 4096, 512, 512
SLAB = 64
PART = ((0, 208), (208, 208), (416, 224))
PART_S = ((0, 48), (208, 48), (416, 32))
PART_T = ((48, 160), (256, 160), (448, 192))
TOKEN_T = (0, 160, 320)
ORDER = (("x", "y", "z"), ("y", "z", "x"), ("z", "x", "y"))
RS_ORDER = (("x", "z", "y"), ("y", "z", "x"), ("z", "x", "y"))
RS_PART = ((0, 48), (48, 48), (96, 32))
ALL = slice(None)
LOW, HIGH = pl.ds(0, 2), pl.ds(2, 2)


def comm_kernel(
    t_rows, t_gain, wt_hbm, s_rows, s_gain, ws_hbm, labels,
    loss_out, rows_out, gain_out, head_out,
    G, wt, ws, ws_sib, head_part, acc_t, sl, es, st, col, lab, scale_s, g_ref, gp, gp_in, own,
    rs_b, rs_c, rs_d, fin, ex_y0, ex_z0, ex_ph0, ex_tp1, ex_ph1, gain_col, gain_own, ex_gain, ex_gain_ph,
    w_sem, out_sem, send, r1, r2, r2f, r1s, r2s, r3s, r3t, sibs_r, sibt_r, ex_s, ex_r, misc_s, misc_r, rs_r,
):
    ph = lax.axis_index("phase")
    tp = lax.axis_index("tp")
    c = ph % 2
    me = {"x": ph // 2, "y": tp % 4, "z": tp // 4}
    sib = (ph + 1 - 2 * c, tp)
    PARTS = range(3)
    STEP = (0, -1, 1, 2)

    def rel(axis, step):
        return (me[axis] + step + 4) % 4

    def near(axis, step):
        at = dict(me)
        at[axis] = rel(axis, step)
        return (at["x"] * 2 + c, at["z"] * 4 + at["y"])

    def remote(src, dst, ssem, rsem, to):
        return pltpu.make_async_remote_copy(
            src_ref=src, dst_ref=dst, send_sem=ssem, recv_sem=rsem, device_id=to, device_id_type=MESH
        )

    wt_loads = [pltpu.make_async_copy(wt_hbm.at[i], wt.at[i], w_sem.at[i]) for i in range(4)]
    ws_load = pltpu.make_async_copy(ws_hbm, ws, w_sem.at[4])
    ws_load.start()
    for load in wt_loads:
        load.start()

    barrier = pltpu.get_barrier_semaphore()
    partners = [sib] + [near(axis, step) for axis in "xyz" for step in (1, -1, 2)]
    for to in partners:
        pl.semaphore_signal(barrier, inc=1, device_id=to, device_id_type=MESH)

    mine = G.at[c, me["x"], me["z"], me["y"]]
    wide = t_rows[...].astype(F32)
    scaled = (wide * t_gain[...].astype(F32)).astype(BF16)
    for (row, size), token in zip(PART_T, TOKEN_T):
        mine[pl.ds(row, size), :] = scaled[token : token + size]
    pl.semaphore_wait(barrier, len(partners))

    def block(p, one, two, three, rows, core=None):
        a, b, d = ORDER[p]
        at = {a: one, b: two, d: three}
        return G.at[c if core is None else core, at["x"], at["z"], at["y"], pl.ds(*rows), :]

    def own_at(p):
        return tuple(me[axis] for axis in ORDER[p])

    def p1(p, i):
        ref = block(p, *own_at(p), PART_T[p])
        return remote(ref, ref, send.at[p, 0], r1.at[p, i], near(ORDER[p][0], (-1, 1, 2)[i]))

    def p2(p, n, i):
        a, b, d = ORDER[p]
        ref = block(p, rel(a, STEP[n]), me[b], me[d], PART_T[p])
        return remote(ref, ref, send.at[p, 1], r2.at[p, i], near(b, (1, -1)[i]))

    def p2f(p, i):
        a, b, d = ORDER[p]
        ref = block(p, (LOW, HIGH)[i], rel(b, (-1, 1)[i]), me[d], PART_T[p])
        return remote(ref, ref, send.at[p, 1], r2f.at[p, i], near(b, (1, -1)[i]))

    def p1s(p, i):
        ref = block(p, *own_at(p), PART_S[p])
        return remote(ref, ref, send.at[p, 2], r1s.at[p, i], near(ORDER[p][0], (-1, 1, 2)[i]))

    def p2s(p, i):
        a, b, d = ORDER[p]
        ref = block(p, ALL, me[b], me[d], PART_S[p])
        return remote(ref, ref, send.at[p, 2], r2s.at[p, i], near(b, (-1, 1, 2)[i]))

    def p3s(p, i):
        d = ORDER[p][2]
        ref = block(p, (ALL, ALL, LOW, HIGH)[i], ALL, rel(d, (0, 0, -1, 1)[i]), PART_S[p])
        return remote(ref, ref, send.at[p, 2], r3s.at[p, i], near(d, (1, -1, 1, -1)[i]))

    def p3t(p, j, i):
        a, b, d = ORDER[p]
        ref = block(p, (ALL, ALL, LOW, HIGH)[i], rel(b, STEP[j]), rel(d, (0, 0, -1, 1)[i]), PART_T[p])
        return remote(ref, ref, send.at[p, 3], r3t.at[p, 4 * j + i], near(d, (1, -1, 1, -1)[i]))

    def arrive(ref, sem):
        pltpu.make_async_copy(ref, ref, sem).wait()

    def p2_wait(p, i):
        a, b, d = ORDER[p]
        arrive(block(p, ALL, rel(b, (-1, 1)[i]), me[d], PART_T[p]), r2.at[p, i])

    def p2f_wait(p, i):
        a, b, d = ORDER[p]
        arrive(block(p, (LOW, HIGH)[i], rel(b, 2), me[d], PART_T[p]), r2f.at[p, i])

    def p1s_wait(p, i):
        a, b, d = ORDER[p]
        arrive(block(p, rel(a, (1, -1, 2)[i]), me[b], me[d], PART_S[p]), r1s.at[p, i])

    def p2s_wait(p, i):
        a, b, d = ORDER[p]
        arrive(block(p, ALL, rel(b, (1, -1, 2)[i]), me[d], PART_S[p]), r2s.at[p, i])

    def p3s_wait(p, i):
        d = ORDER[p][2]
        arrive(block(p, (ALL, ALL, LOW, HIGH)[i], ALL, rel(d, (-1, 1, 2, 2)[i]), PART_S[p]), r3s.at[p, i])

    def p3t_wait(p, j, i):
        a, b, d = ORDER[p]
        ref = block(p, (ALL, ALL, LOW, HIGH)[i], rel(b, STEP[j]), rel(d, (-1, 1, 2, 2)[i]), PART_T[p])
        arrive(ref, r3t.at[p, 4 * j + i])

    def sib_t(p, j, k, core=None):
        a, b, d = ORDER[p]
        ref = block(p, ALL, rel(b, STEP[j]), rel(d, STEP[k]), PART_T[p], core)
        return remote(ref, ref, send.at[p, 4], sibt_r.at[p, 4 * j + k], sib)

    def sib_s(p, core):
        ref = G.at[core, :, :, :, pl.ds(*PART_S[p]), :]
        return remote(ref, ref, send.at[p, 5], sibs_r.at[p], sib)

    def p3t_send(j):
        for p in PARTS:
            p3t(p, j, 0).start()
            p3t(p, j, 1).start()

    def products(j, k, core):
        for p in PARTS:
            a, b, d = ORDER[p]
            at = {a: ALL, b: rel(b, STEP[j]), d: rel(d, STEP[k])}
            rows = G[core, at["x"], at["z"], at["y"], pl.ds(*PART_T[p]), :]
            lhs = jnp.concatenate([rows[i] for i in range(4)], axis=1)
            rhs = wt[at["x"], core, at["z"], at["y"]].reshape(512, LOCAL_V)
            acc_t[pl.ds(TOKEN_T[p], PART_T[p][1]), :] += jnp.dot(lhs, rhs, preferred_element_type=F32)

    def sib_wait(j, k):
        for p in PARTS:
            a, b, d = ORDER[p]
            arrive(block(p, ALL, rel(b, STEP[j]), rel(d, STEP[k]), PART_T[p], 1 - c), sibt_r.at[p, 4 * j + k])

    def consume(j, k):
        sib_wait(j, k)

        def one_core(core, _):
            products(j, k, core)
            return 0

        lax.fori_loop(0, 2, one_core, 0)

    def rowsum(value):
        return jnp.sum(value, axis=1, keepdims=True)

    def to_tp(d):
        return (ph, (tp + d) % 16)

    def to_ph(d):
        return ((ph + d) % 8, tp)

    def exchange(buf, slot, count, number, to):
        def copy(d):
            return remote(buf.at[slot], buf.at[slot], ex_s.at[number], ex_r.at[number, d], to(d))

        def start():
            for d in range(1, count):
                copy(d).start()

        def wait():
            for d in range(1, count):
                copy(d).wait_recv()

        def sent():
            arrive(buf.at[pl.ds(0, count - 1)], ex_s.at[number])

        return start, wait, sent

    early_y = exchange(ex_y0, me["y"], 4, 0, lambda d: near("y", d))
    early_z = exchange(ex_z0, me["z"], 4, 5, lambda d: near("z", d))
    early_ph = exchange(ex_ph0, ph, 8, 1, to_ph)
    late_tp = exchange(ex_tp1, tp, 16, 2, to_tp)
    late_ph = exchange(ex_ph1, ph, 8, 3, to_ph)
    gain_ph = exchange(ex_gain_ph, ph, 8, 4, to_ph)

    def to_columns(rows):
        filled = jnp.concatenate(rows + [jnp.zeros((128 - len(rows), TOKENS), F32)], axis=0)
        return jnp.transpose(filled)

    for i in range(3):
        for p in PARTS:
            p1(p, i).start()
    for p in PARTS:
        p2(p, 0, 0).start()
        p2(p, 0, 1).start()
    raw = s_rows[...].astype(F32)
    raw_squares = rowsum(raw * raw)
    lane_t = lax.broadcasted_iota(jnp.int32, (TOKENS, 128), 1)
    st[...] = jnp.where(lane_t == 0, rowsum(wide * wide), 0.0)
    st[0:SLAB, :] = jnp.where(lane_t[0:SLAB] == 1, raw_squares, st[0:SLAB, :])
    squares = jnp.transpose(st[...])
    ex_y0[me["y"]] = jnp.concatenate(
        [squares[0:1, 128 * i : 128 * i + 128] for i in range(4)]
        + [squares[1:2, 0:128], jnp.zeros((3, 128), F32)],
        axis=0,
    )
    early_y[0]()
    lab[...] = to_columns([labels[...].astype(F32)])
    acc_t[...] = jnp.zeros_like(acc_t)
    for n in (1, 2, 3):
        for p in PARTS:
            a, b, d = ORDER[p]
            arrive(block(p, rel(a, STEP[n]), me[b], me[d], PART_T[p]), r1.at[p, (1, 0, 2)[n - 1]])
            p2(p, n, 0).start()
            p2(p, n, 1).start()
    p3t_send(0)
    early_y[1]()
    ex_z0[me["z"]] = ex_y0[0] + ex_y0[1] + ex_y0[2] + ex_y0[3]
    early_z[0]()
    for p in PARTS:
        sib_t(p, 0, 0).start()
    for i in (0, 1):
        for p in PARTS:
            p2_wait(p, i)
            p2f(p, i).start()
            sib_t(p, i + 1, 0).start()
    early_z[1]()
    early = ex_z0[0] + ex_z0[1] + ex_z0[2] + ex_z0[3]
    ex_ph0[ph] = early
    turned = jnp.transpose(jnp.concatenate([early, jnp.zeros((120, 128), F32)], axis=0))
    own_scale = lax.rsqrt(turned[0:SLAB, 4:5] / DS + NORM_EPSILON)
    scale_s[...] = own_scale
    gain = s_gain[...].astype(F32)
    left = (raw[:, 0:128] * own_scale * gain[0:1]).astype(BF16)
    right = (raw[:, 128:256] * own_scale * gain[1:2]).astype(BF16)
    mine[0:48, :] = left[0:48]
    mine[208:224, :] = left[48:64]
    mine[224:256, :] = right[0:32]
    mine[416:448, :] = right[32:64]
    for i in range(3):
        for p in PARTS:
            p1s(p, i).start()
    for p in PARTS:
        p2f_wait(p, 0)
        p2f_wait(p, 1)
        sib_t(p, 3, 0).start()
    p3t_send(1)
    ws_load.wait()
    ws_push = remote(ws, ws_sib, misc_s.at[0], misc_r.at[0], sib)
    ws_push.start()
    for load in wt_loads:
        load.wait()
    for p in PARTS:
        for i in range(3):
            p1s_wait(p, i)
        for i in range(3):
            p2s(p, i).start()
    consume(0, 0)

    def forward(j):
        for i in (0, 1):
            for p in PARTS:
                p3t_wait(p, j, i)
                p3t(p, j, i + 2).start()
                sib_t(p, j, i + 1).start()

    def opposite(j):
        for p in PARTS:
            p3t_wait(p, j, 2)
            p3t_wait(p, j, 3)
            sib_t(p, j, 3).start()

    forward(0)
    consume(1, 0)
    for p in PARTS:
        for i in range(3):
            p2s_wait(p, i)
        p3s(p, 0).start()
        p3s(p, 1).start()
    p3t_send(2)
    early_ph[0]()
    consume(2, 0)
    consume(3, 0)
    forward(1)
    for i in (0, 1):
        for p in PARTS:
            p3s_wait(p, i)
            p3s(p, i + 2).start()
    p3t_send(3)
    consume(0, 1)
    consume(0, 2)
    opposite(0)
    consume(1, 1)
    early_ph[1]()
    early = ex_ph0[0]
    for i in range(1, 8):
        early = early + ex_ph0[i]
    teacher_scale = lax.rsqrt(jnp.concatenate([early[i : i + 1] for i in range(4)], axis=1) / DT + NORM_EPSILON)
    col[...] = to_columns([teacher_scale])
    for p in PARTS:
        p3s_wait(p, 2)
        p3s_wait(p, 3)
        sib_s(p, c).start()
    consume(1, 2)
    consume(0, 3)
    for p in PARTS:
        arrive(G.at[1 - c, :, :, :, pl.ds(*PART_S[p]), :], sibs_r.at[p])

    def slab(q):
        return pl.ds(pl.multiple_of(q * SLAB, SLAB), SLAB)

    def normed(z, y):
        slabs = []
        for q in range(8):
            ref = G.at[q % 2, q // 2, z, y]
            first = jnp.concatenate([ref[0:48, :], ref[208:224, :]], axis=0)
            second = jnp.concatenate([ref[224:256, :], ref[416:448, :]], axis=0)
            slabs.append(jnp.concatenate([first, second], axis=1))
        return jnp.concatenate(slabs, axis=0)

    def student_dot(z, half):
        t = 4 * z + 2 * half
        lhs = jnp.concatenate([normed(z, 2 * half), normed(z, 2 * half + 1)], axis=1)
        rhs = jnp.concatenate([ws[t], ws[t + 1]], axis=0)
        return jnp.dot(lhs, rhs, preferred_element_type=F32)

    def student_dots(z, _):
        sl[...] += student_dot(z, 0)
        sl[...] += student_dot(z, 1)
        return 0

    def nt_dot(lhs, rhs):
        return lax.dot_general(lhs, rhs, (((1,), (1,)), ((), ())), preferred_element_type=F32)

    eye = (
        lax.broadcasted_iota(jnp.int32, (256, 256), 0) == lax.broadcasted_iota(jnp.int32, (256, 256), 1)
    ).astype(F32).astype(BF16)

    def head_copy(t):
        return pltpu.make_async_copy(head_part.at[t % 2], head_out.at[t], out_sem.at[t % 2])

    lane_c = lax.broadcasted_iota(jnp.int32, (256, 128), 1)

    def turn(z, _):
        for y in range(4):
            turned = nt_dot(eye, normed(z, y)).astype(BF16)
            wt[0, 1, z, y] = turned[0:128]
            wt[1, 1, z, y] = turned[128:256]
        return 0

    def head_layer(z, _):
        for y in range(4):
            t = 4 * z + y
            if y >= 2:
                head_copy(t - 2).wait()
            else:

                @pl.when(z >= 1)
                def _(t=t):
                    head_copy(t - 2).wait()

            turned = jnp.concatenate([wt[0, 1, z, y], wt[1, 1, z, y]], axis=0)
            grad = jnp.dot(turned, g_ref[...], preferred_element_type=F32)
            head_part[t % 2] = grad.astype(BF16)
            head_copy(t).start()
            gain_col[...] = jnp.where(lane_c == t, rowsum(grad * ws[t].astype(F32)), gain_col[...])
        return 0

    sl[...] = student_dot(0, 0)
    sl[...] += student_dot(0, 1)
    forward(2)
    lax.fori_loop(1, 4, student_dots, 0)
    opposite(1)
    lane = lax.broadcasted_iota(jnp.int32, (SLAB, 128), 1)
    vocab_first = ((ph * 16 + tp) * LOCAL_V).astype(F32)

    def label_hit(rows):
        ids = lax.broadcasted_iota(jnp.int32, (SLAB, LOCAL_V), 1).astype(F32) + vocab_first
        return lab[rows, 0:1] == ids

    def pack(columns, first, out):
        for i, column in enumerate(columns):
            out = jnp.where(lane == first + i, column, out)
        return out

    def student_stats(n, _):
        student_slab(2 * n)
        student_slab(2 * n + 1)
        return 0

    def student_slab(q):
        rows = slab(q)
        logits = sl[rows, :]
        top = jnp.max(logits, axis=1, keepdims=True)
        e = jnp.exp(logits - top)
        es[rows, :] = e
        picked = jnp.where(label_hit(rows), logits, 0.0)
        st[rows, :] = pack(
            [top, rowsum(e), rowsum(e * logits), rowsum(picked)], 4, jnp.zeros((SLAB, 128), F32)
        )

    lax.fori_loop(0, 4, student_stats, 0)
    consume(2, 1)
    consume(2, 2)
    forward(3)
    consume(1, 3)
    opposite(2)
    consume(3, 1)
    consume(3, 2)
    consume(2, 3)
    opposite(3)
    products(3, 3, c)
    sib_wait(3, 3)
    products(3, 3, 1 - c)

    def teacher_stats(n, _):
        teacher_slab(2 * n)
        teacher_slab(2 * n + 1)
        return 0

    def teacher_slab(q):
        rows = slab(q)
        logits = acc_t[rows, :] * col[rows, 0:1]
        student = sl[rows, :]
        top = jnp.max(logits, axis=1, keepdims=True)
        e = jnp.exp(logits - top)
        acc_t[rows, :] = e
        st[rows, :] = pack([top, rowsum(e), rowsum(e * (logits - student)), rowsum(e * student)], 0, st[rows, :])

    lax.fori_loop(0, 4, teacher_stats, 0)
    stats = jnp.transpose(st[...])[0:8, :]
    sub = lax.broadcasted_iota(jnp.int32, (8, TOKENS), 0)

    def merge(buf, count):
        t_top, s_top = buf[0, 0:1, :], buf[0, 4:5, :]
        for i in range(1, count):
            t_top = jnp.maximum(t_top, buf[i, 0:1, :])
            s_top = jnp.maximum(s_top, buf[i, 4:5, :])
        total = jnp.zeros((8, TOKENS), F32)
        for i in range(count):
            weight = jnp.where(sub < 4, jnp.exp(buf[i, 0:1, :] - t_top), jnp.exp(buf[i, 4:5, :] - s_top))
            total = total + buf[i] * jnp.where(sub == 7, 1.0, weight)
        return jnp.where(sub == 0, t_top, jnp.where(sub == 4, s_top, total))

    ex_tp1[tp] = stats
    late_tp[0]()
    lax.fori_loop(0, 2, turn, 0)
    late_tp[1]()
    ex_ph1[ph] = merge(ex_tp1, 16)
    late_ph[0]()
    lax.fori_loop(2, 4, turn, 0)
    late_ph[1]()
    late = merge(ex_ph1, 8)
    teacher_top, teacher_total, student_top, student_total = late[0:1], late[1:2], late[4:5], late[5:6]
    picked_all = late[7:8]
    teacher_lse = teacher_top + jnp.log(teacher_total)
    student_lse = student_top + jnp.log(student_total)
    loss = (
        late[2:3] / teacher_total - teacher_lse + student_lse + LABEL_WEIGHT * (student_lse - picked_all)
    )
    inner = (
        (1.0 + LABEL_WEIGHT) * late[6:7] / student_total - late[3:4] / teacher_total - LABEL_WEIGHT * picked_all
    )
    t_factor = jnp.exp(stats[0:1] - teacher_top) / teacher_total
    s_factor = (1.0 + LABEL_WEIGHT) * jnp.exp(stats[4:5] - student_top) / student_total
    col[...] = to_columns([t_factor, s_factor, inner])

    def logit_grad(n, which):
        q = 2 * n + (c if which == 0 else 1 - c)
        rows = slab(q)
        g = (
            es[rows, :] * col[rows, 1:2]
            - acc_t[rows, :] * col[rows, 0:1]
            - LABEL_WEIGHT * label_hit(rows).astype(F32)
        ).astype(BF16)
        g_ref[rows, :] = g
        gp[which, slab(n), :] = g

    for which in (1, 0):

        def grad_step(n, _, which=which):
            logit_grad(2 * n, which)
            logit_grad(2 * n + 1, which)
            return 0

        lax.fori_loop(0, 2, grad_step, 0)
        if which == 1:
            gp_push = remote(gp.at[1], gp_in, misc_s.at[1], misc_r.at[1], sib)
            gp_push.start()
    gain_col[...] = jnp.zeros_like(gain_col)

    def own_first(z, _):
        for y in range(4):
            r = nt_dot(gp[0], ws[4 * z + y])
            for xt in range(4):
                own[xt, z, y, 0:64] = r[xt * 64 : xt * 64 + 64, 0:128]
                own[xt, z, y, 64:128] = r[xt * 64 : xt * 64 + 64, 128:256]
        return 0

    def own_second(z):
        for y in range(4):
            r = nt_dot(gp_in[...], ws_sib[4 * z + y])
            for xt in range(4):
                for h in range(2):
                    at = pl.ds(64 * h, 64)
                    total = own[xt, z, y, at, :] + r[xt * 64 : xt * 64 + 64, 128 * h : 128 * h + 128]
                    own[xt, z, y, at, :] = total
                    wt[xt, 0, z, y, at, 0:128] = total.astype(BF16)

    lax.fori_loop(0, 4, own_first, 0)
    ws_push.wait_recv()
    gp_push.wait_recv()

    def at3(p, one, two, three):
        a, b, d = RS_ORDER[p]
        at = {a: one, b: two, d: three}
        return at["x"], at["z"], at["y"]

    def rest(p, two, three):
        at = {RS_ORDER[p][1]: two, RS_ORDER[p][2]: three}
        return tuple(at[axis] for axis in ("x", "z", "y") if axis in at)

    def stage_ref(p, one, two, three):
        ix, iz, iy = at3(p, one, two, three)
        return wt.at[ix, 0, iz, iy, pl.ds(*RS_PART[p]), pl.ds(0, 128)]

    def own_ref(p, one, two, three):
        ix, iz, iy = at3(p, one, two, three)
        return own.at[ix, iz, iy, pl.ds(*RS_PART[p]), :]

    HOP = (2, 1, -1)
    SUBSET = (2, 1, -1, 0)

    def rs1(p, k, i):
        a, b, d = RS_ORDER[p]
        two = rel(b, SUBSET[k])
        src = stage_ref(p, rel(a, HOP[i]), two, ALL)
        dst = rs_b.at[(i, *rest(p, two, ALL), pl.ds(*RS_PART[p]), ALL)]
        return remote(src, dst, send.at[p, 6], rs_r.at[p, 3 * k + i], near(a, HOP[i]))

    def rs1_wait(p, k, i):
        dst = rs_b.at[(i, *rest(p, rel(RS_ORDER[p][1], SUBSET[k]), ALL), pl.ds(*RS_PART[p]), ALL)]
        arrive(dst, rs_r.at[p, 3 * k + i])

    def rs2(p, i):
        a, b, d = RS_ORDER[p]
        src = stage_ref(p, me[a], rel(b, HOP[i]), ALL)
        dst = rs_c.at[i, :, pl.ds(*RS_PART[p]), :]
        return remote(src, dst, send.at[p, 7], rs_r.at[p, 12 + i], near(b, HOP[i]))

    def rs3(p, i):
        a, b, d = RS_ORDER[p]
        src = stage_ref(p, me[a], me[b], rel(d, HOP[i]))
        dst = rs_d.at[i, pl.ds(*RS_PART[p]), :]
        return remote(src, dst, send.at[p, 8], rs_r.at[p, 15 + i], near(d, HOP[i]))

    for k in range(4):
        own_second(rel("z", SUBSET[k]))
        for i in range(3):
            rs1(0, k, i).start()
            rs1(1, k, i).start()
        if k < 3:
            for m in range(4):
                rs1(2, m, k).start()
    def gain_copy(d):
        to = (tp + d) % 16
        return remote(gain_own.at[to], ex_gain.at[tp], misc_s.at[2], ex_r.at[6, d], (ph, to))

    for k in range(4):
        if k < 3:
            lax.fori_loop((0, 2, 3)[k], (2, 3, 4)[k], head_layer, 0)
        if k == 2:
            turned = jnp.transpose(gain_col[...])
            for t in range(16):
                gain_own[t] = jnp.broadcast_to(turned[t : t + 1], (8, 256))
            ex_gain[tp] = gain_own[tp]
            for d in range(1, 16):
                gain_copy(d).start()
        for p in PARTS:
            rows = pl.ds(*RS_PART[p])
            for i in range(3):
                rs1_wait(p, k, i)

            def add_first(n, _, p=p, k=k, rows=rows):
                two = rel(RS_ORDER[p][1], SUBSET[k])
                ref = own_ref(p, me[RS_ORDER[p][0]], two, n)
                total = ref[...]
                for i in range(3):
                    total = total + rs_b[(i, *rest(p, two, n), rows, ALL)].astype(F32)
                if k == 3:
                    ref[...] = total
                else:
                    stage_ref(p, me[RS_ORDER[p][0]], two, n)[...] = total.astype(BF16)
                return 0

            lax.fori_loop(0, 4, add_first, 0)
            if k < 3:
                rs2(p, k).start()
    for p in PARTS:
        rows = pl.ds(*RS_PART[p])
        for i in range(3):
            arrive(rs_c.at[i, :, rows, :], rs_r.at[p, 12 + i])

        def add_second(n, _, p=p, rows=rows):
            ref = own_ref(p, me[RS_ORDER[p][0]], me[RS_ORDER[p][1]], n)
            total = ref[...]
            for i in range(3):
                total = total + rs_c[i, n, rows, :].astype(F32)
            ref[...] = total
            stage_ref(p, me[RS_ORDER[p][0]], me[RS_ORDER[p][1]], n)[...] = total.astype(BF16)
            return 0

        lax.fori_loop(0, 4, add_second, 0)
        for i in range(3):
            rs3(p, i).start()
    for d in range(1, 16):
        gain_copy(d).wait_recv()
    total = ex_gain[0]
    for i in range(1, 16):
        total = total + ex_gain[i]
    ex_gain_ph[ph] = total
    gain_ph[0]()
    for p in PARTS:
        rows = pl.ds(*RS_PART[p])
        for i in range(3):
            arrive(rs_d.at[i, rows, :], rs_r.at[p, 15 + i])
        total = own_ref(p, *(me[axis] for axis in RS_ORDER[p]))[...]
        for i in range(3):
            total = total + rs_d[i, rows, :].astype(F32)
        fin[rows, :] = total

    rows = slab(ph)
    scale = scale_s[...]
    coefficient = scale * scale * col[rows, 2:3] / DS
    for h in range(2):
        cols = pl.ds(h * 128, 128)
        grad = fin[h * 64 : h * 64 + 64, :]
        rows_out[:, cols] = (scale * gain[h : h + 1] * grad - raw[:, h * 128 : h * 128 + 128] * coefficient).astype(BF16)
    sl[0:8, :] = jnp.broadcast_to(loss, (8, TOKENS))
    window = sl[0:1, pl.ds(pl.multiple_of(me["x"] * 128, 128), 128)]
    loss_out[...] = jnp.where(c == 1, window[:, 64:128], window[:, 0:64])

    for p in PARTS:
        rows = pl.ds(*PART_T[p])
        arrive(G.at[0, 0, 0, 0:3, rows, :], send.at[p, 0])
        arrive(G.at[0, 0:3, 0, :, rows, :], send.at[p, 1])
        arrive(G.at[0, 0:3, :, :, rows, :], send.at[p, 3])
        arrive(G.at[0, :, :, :, rows, :], send.at[p, 4])
        rows = pl.ds(*PART_S[p])
        arrive(G.at[0, 0:3, :, :, rows, :], send.at[p, 2])
        arrive(G.at[0, 0:3, 0:1, :, rows, :], send.at[p, 2])
        arrive(G.at[0, 0, 0, 0:3, rows, :], send.at[p, 2])
        arrive(G.at[0, :, :, :, rows, :], send.at[p, 5])
        rows = pl.ds(*RS_PART[p])
        arrive(rs_b.at[:, :, :, rows, :], send.at[p, 6])
        arrive(rs_c.at[:, :, rows, :], send.at[p, 7])
        arrive(rs_d.at[:, rows, :], send.at[p, 8])
    for ex in (early_y, early_z, early_ph, late_tp, late_ph):
        ex[2]()
    ws_push.wait_send()
    gp_push.wait_send()
    head_copy(14).wait()
    head_copy(15).wait()
    arrive(ex_gain.at[pl.ds(0, 15)], misc_s.at[2])
    gain_ph[1]()
    total = ex_gain_ph[0]
    for i in range(1, 8):
        total = total + ex_gain_ph[i]
    gain_out[...] = total[0:1] / jnp.concatenate([gain[0:1], gain[1:2]], axis=1)
    gain_ph[2]()


def out_kernel(
    head_in, loss_in, rows_in, gain_in, head_out, loss_out, rows_out, gain_out,
    head, loss, rows, gain, in_sem, out_sem,
):
    def part(ref, i):
        return ref.at[pl.ds(1024 * i, 1024)]

    ways = [(part(head_in, i), part(head, i), part(head_out, i)) for i in range(4)]
    ways += [(loss_in, loss, loss_out), (rows_in, rows, rows_out), (gain_in, gain, gain_out)]
    loads = [pltpu.make_async_copy(src, held, in_sem.at[i]) for i, (src, held, _) in enumerate(ways)]
    stores = [pltpu.make_async_copy(held, dst, out_sem.at[i]) for i, (_, held, dst) in enumerate(ways)]
    for load in loads:
        load.start()
    for load, store in zip(loads, stores):
        load.wait()
        store.start()
    for store in stores:
        store.wait()


def local(teacher_rows, teacher_gain, teacher_head, student_rows, student_gain, student_head, labels):
    vmem = pl.BlockSpec(memory_space=pltpu.VMEM)
    hbm = pl.BlockSpec(memory_space=pl.ANY)
    dma = pltpu.SemaphoreType.DMA
    loss, rows_grad, gain_grad, head_grad = pl.pallas_call(
        comm_kernel,
        out_shape=(
            jax.ShapeDtypeStruct((1, SLAB), F32),
            jax.ShapeDtypeStruct((SLAB, 256), BF16),
            jax.ShapeDtypeStruct((1, 256), F32),
            jax.ShapeDtypeStruct((16, 256, LOCAL_V), BF16),
        ),
        in_specs=[vmem, vmem, hbm, vmem, vmem, hbm, vmem],
        out_specs=(vmem, vmem, vmem, hbm),
        scratch_shapes=[
            pltpu.VMEM((2, 4, 4, 4, 640, 128), BF16),
            pltpu.VMEM((4, 2, 4, 4, 128, LOCAL_V), BF16),
            pltpu.VMEM((16, 256, LOCAL_V), BF16),
            pltpu.VMEM((16, 256, LOCAL_V), BF16),
            pltpu.VMEM((2, 256, LOCAL_V), BF16),
            pltpu.VMEM((TOKENS, LOCAL_V), F32),
            pltpu.VMEM((TOKENS, LOCAL_V), F32),
            pltpu.VMEM((TOKENS, LOCAL_V), F32),
            pltpu.VMEM((TOKENS, 128), F32),
            pltpu.VMEM((TOKENS, 128), F32),
            pltpu.VMEM((TOKENS, 128), F32),
            pltpu.VMEM((SLAB, 1), F32),
            pltpu.VMEM((TOKENS, LOCAL_V), BF16),
            pltpu.VMEM((2, 256, LOCAL_V), BF16),
            pltpu.VMEM((256, LOCAL_V), BF16),
            pltpu.VMEM((4, 4, 4, 128, 128), F32),
            pltpu.VMEM((3, 4, 4, 128, 128), BF16),
            pltpu.VMEM((3, 4, 128, 128), BF16),
            pltpu.VMEM((3, 128, 128), BF16),
            pltpu.VMEM((128, 128), F32),
            pltpu.VMEM((4, 8, 128), F32),
            pltpu.VMEM((4, 8, 128), F32),
            pltpu.VMEM((8, 8, 128), F32),
            pltpu.VMEM((16, 8, TOKENS), F32),
            pltpu.VMEM((8, 8, TOKENS), F32),
            pltpu.VMEM((256, 128), F32),
            pltpu.VMEM((16, 8, 256), F32),
            pltpu.VMEM((16, 8, 256), F32),
            pltpu.VMEM((8, 8, 256), F32),
            dma((5,)), dma((2,)), dma((3, 9)),
            dma((3, 3)), dma((3, 2)), dma((3, 2)), dma((3, 3)), dma((3, 3)), dma((3, 4)), dma((3, 16)),
            dma((3,)), dma((3, 16)), dma((6,)), dma((7, 16)), dma((3,)), dma((2,)), dma((3, 18)),
        ],
        compiler_params=pltpu.CompilerParams(
            collective_id=0, has_side_effects=True, vmem_limit_bytes=63 << 20
        ),
        name="distill",
    )(
        teacher_rows,
        teacher_gain.reshape(1, 128),
        teacher_head.reshape(4, 2, 4, 4, 128, LOCAL_V),
        student_rows,
        student_gain.reshape(2, 128),
        student_head.reshape(16, 256, LOCAL_V),
        labels.reshape(1, TOKENS),
    )
    head_grad, loss, rows_grad, gain_grad = pl.pallas_call(
        out_kernel,
        out_shape=(
            jax.ShapeDtypeStruct((DS, LOCAL_V), BF16),
            jax.ShapeDtypeStruct((1, SLAB), F32),
            jax.ShapeDtypeStruct((SLAB, 256), BF16),
            jax.ShapeDtypeStruct((1, 256), F32),
        ),
        in_specs=[hbm, hbm, hbm, hbm],
        out_specs=(hbm, hbm, hbm, hbm),
        scratch_shapes=[
            pltpu.VMEM((DS, LOCAL_V), BF16),
            pltpu.VMEM((1, SLAB), F32),
            pltpu.VMEM((SLAB, 256), BF16),
            pltpu.VMEM((1, 256), F32),
            dma((7,)),
            dma((7,)),
        ],
        compiler_params=pltpu.CompilerParams(vmem_limit_bytes=63 << 20),
        name="outputs",
    )(head_grad.reshape(DS, LOCAL_V), loss, rows_grad, gain_grad)
    return loss.reshape(SLAB), head_grad, rows_grad, gain_grad.reshape(256)


def solution(mesh):
    placed = (
        P(None, ("phase", "tp")),
        P(("phase", "tp")),
        P(None, ("phase", "tp")),
        P("phase", "tp"),
        P("tp"),
        P(None, ("phase", "tp")),
        P(),
    )
    return jax.shard_map(
        local,
        mesh=mesh,
        in_specs=placed,
        out_specs=(P("phase"), P(None, ("phase", "tp")), P("phase", "tp"), P("tp")),
        check_vma=False,
    )
```

```python
import jax
import jax.numpy as jnp
from jax import lax
from jax.experimental import pallas as pl
from jax.experimental.pallas import tpu as pltpu
from jax.sharding import PartitionSpec as P

NORM_EPSILON = 1e-05
LABEL_WEIGHT = 0.5
F32 = jnp.float32
BF16 = jnp.bfloat16
MESH = pl.DeviceIdType.MESH

DT, DS, TOKENS, LOCAL_V = 16384, 4096, 512, 512
SLAB = 64
PART = ((0, 208), (208, 208), (416, 224))
PART_S = ((0, 48), (208, 48), (416, 32))
PART_T = ((48, 160), (256, 160), (448, 192))
TOKEN_T = (0, 160, 320)
ORDER = (("x", "y", "z"), ("y", "z", "x"), ("z", "x", "y"))
RS_ORDER = (("x", "z", "y"), ("y", "z", "x"), ("z", "x", "y"))
RS_PART = ((0, 48), (48, 48), (96, 32))
ALL = slice(None)
LOW, HIGH = pl.ds(0, 2), pl.ds(2, 2)


def comm_kernel(
    t_rows, t_gain, wt_hbm, s_rows, s_gain, ws_hbm, labels,
    loss_out, rows_out, gain_out, head_out,
    G, wt, ws, ws_sib, head_part, acc_t, sl, es, st, col, lab, scale_s, g_ref, gp, gp_in, own,
    rs_b, rs_c, rs_d, fin, ex_y0, ex_z0, ex_ph0, ex_tp1, ex_ph1, gain_col, gain_own, ex_gain, ex_gain_ph,
    w_sem, out_sem, send, r1, r2, r2f, r1s, r2s, r3s, r3t, sibs_r, sibt_r, ex_s, ex_r, misc_s, misc_r, rs_r,
):
    ph = lax.axis_index("phase")
    tp = lax.axis_index("tp")
    c = ph % 2
    me = {"x": ph // 2, "y": tp % 4, "z": tp // 4}
    sib = (ph + 1 - 2 * c, tp)
    PARTS = range(3)
    STEP = (0, -1, 1, 2)

    def rel(axis, step):
        return (me[axis] + step + 4) % 4

    def near(axis, step):
        at = dict(me)
        at[axis] = rel(axis, step)
        return (at["x"] * 2 + c, at["z"] * 4 + at["y"])

    def remote(src, dst, ssem, rsem, to):
        return pltpu.make_async_remote_copy(
            src_ref=src, dst_ref=dst, send_sem=ssem, recv_sem=rsem, device_id=to, device_id_type=MESH
        )

    wt_loads = [pltpu.make_async_copy(wt_hbm.at[i], wt.at[i], w_sem.at[i]) for i in range(4)]
    ws_load = pltpu.make_async_copy(ws_hbm, ws, w_sem.at[4])
    ws_load.start()
    for load in wt_loads:
        load.start()

    barrier = pltpu.get_barrier_semaphore()
    partners = [sib] + [near(axis, step) for axis in "xyz" for step in (1, -1, 2)]
    for to in partners:
        pl.semaphore_signal(barrier, inc=1, device_id=to, device_id_type=MESH)

    mine = G.at[c, me["x"], me["z"], me["y"]]
    wide = t_rows[...].astype(F32)
    scaled = (wide * t_gain[...].astype(F32)).astype(BF16)
    for (row, size), token in zip(PART_T, TOKEN_T):
        mine[pl.ds(row, size), :] = scaled[token : token + size]
    pl.semaphore_wait(barrier, len(partners))

    def block(p, one, two, three, rows, core=None):
        a, b, d = ORDER[p]
        at = {a: one, b: two, d: three}
        return G.at[c if core is None else core, at["x"], at["z"], at["y"], pl.ds(*rows), :]

    def own_at(p):
        return tuple(me[axis] for axis in ORDER[p])

    def p1(p, i):
        ref = block(p, *own_at(p), PART_T[p])
        return remote(ref, ref, send.at[p, 0], r1.at[p, i], near(ORDER[p][0], (-1, 1, 2)[i]))

    def p2(p, n, i):
        a, b, d = ORDER[p]
        ref = block(p, rel(a, STEP[n]), me[b], me[d], PART_T[p])
        return remote(ref, ref, send.at[p, 1], r2.at[p, i], near(b, (1, -1)[i]))

    def p2f(p, i):
        a, b, d = ORDER[p]
        ref = block(p, (LOW, HIGH)[i], rel(b, (-1, 1)[i]), me[d], PART_T[p])
        return remote(ref, ref, send.at[p, 1], r2f.at[p, i], near(b, (1, -1)[i]))

    def p1s(p, i):
        ref = block(p, *own_at(p), PART_S[p])
        return remote(ref, ref, send.at[p, 2], r1s.at[p, i], near(ORDER[p][0], (-1, 1, 2)[i]))

    def p2s(p, i):
        a, b, d = ORDER[p]
        ref = block(p, ALL, me[b], me[d], PART_S[p])
        return remote(ref, ref, send.at[p, 2], r2s.at[p, i], near(b, (-1, 1, 2)[i]))

    def p3s(p, i):
        d = ORDER[p][2]
        ref = block(p, (ALL, ALL, LOW, HIGH)[i], ALL, rel(d, (0, 0, -1, 1)[i]), PART_S[p])
        return remote(ref, ref, send.at[p, 2], r3s.at[p, i], near(d, (1, -1, 1, -1)[i]))

    def p3t(p, j, i):
        a, b, d = ORDER[p]
        ref = block(p, (ALL, ALL, LOW, HIGH)[i], rel(b, STEP[j]), rel(d, (0, 0, -1, 1)[i]), PART_T[p])
        return remote(ref, ref, send.at[p, 3], r3t.at[p, 4 * j + i], near(d, (1, -1, 1, -1)[i]))

    def arrive(ref, sem):
        pltpu.make_async_copy(ref, ref, sem).wait()

    def p2_wait(p, i):
        a, b, d = ORDER[p]
        arrive(block(p, ALL, rel(b, (-1, 1)[i]), me[d], PART_T[p]), r2.at[p, i])

    def p2f_wait(p, i):
        a, b, d = ORDER[p]
        arrive(block(p, (LOW, HIGH)[i], rel(b, 2), me[d], PART_T[p]), r2f.at[p, i])

    def p1s_wait(p, i):
        a, b, d = ORDER[p]
        arrive(block(p, rel(a, (1, -1, 2)[i]), me[b], me[d], PART_S[p]), r1s.at[p, i])

    def p2s_wait(p, i):
        a, b, d = ORDER[p]
        arrive(block(p, ALL, rel(b, (1, -1, 2)[i]), me[d], PART_S[p]), r2s.at[p, i])

    def p3s_wait(p, i):
        d = ORDER[p][2]
        arrive(block(p, (ALL, ALL, LOW, HIGH)[i], ALL, rel(d, (-1, 1, 2, 2)[i]), PART_S[p]), r3s.at[p, i])

    def p3t_wait(p, j, i):
        a, b, d = ORDER[p]
        ref = block(p, (ALL, ALL, LOW, HIGH)[i], rel(b, STEP[j]), rel(d, (-1, 1, 2, 2)[i]), PART_T[p])
        arrive(ref, r3t.at[p, 4 * j + i])

    def sib_t(p, j, k, core=None):
        a, b, d = ORDER[p]
        ref = block(p, ALL, rel(b, STEP[j]), rel(d, STEP[k]), PART_T[p], core)
        return remote(ref, ref, send.at[p, 4], sibt_r.at[p, 4 * j + k], sib)

    def sib_s(p, core):
        ref = G.at[core, :, :, :, pl.ds(*PART_S[p]), :]
        return remote(ref, ref, send.at[p, 5], sibs_r.at[p], sib)

    def p3t_send(j):
        for p in PARTS:
            p3t(p, j, 0).start()
            p3t(p, j, 1).start()

    def products(j, k, core):
        for p in PARTS:
            a, b, d = ORDER[p]
            at = {a: ALL, b: rel(b, STEP[j]), d: rel(d, STEP[k])}
            rows = G[core, at["x"], at["z"], at["y"], pl.ds(*PART_T[p]), :]
            lhs = jnp.concatenate([rows[i] for i in range(4)], axis=1)
            rhs = wt[at["x"], core, at["z"], at["y"]].reshape(512, LOCAL_V)
            acc_t[pl.ds(TOKEN_T[p], PART_T[p][1]), :] += jnp.dot(lhs, rhs, preferred_element_type=F32)

    def sib_wait(j, k):
        for p in PARTS:
            a, b, d = ORDER[p]
            arrive(block(p, ALL, rel(b, STEP[j]), rel(d, STEP[k]), PART_T[p], 1 - c), sibt_r.at[p, 4 * j + k])

    def consume(j, k):
        sib_wait(j, k)

        def one_core(core, _):
            products(j, k, core)
            return 0

        lax.fori_loop(0, 2, one_core, 0)

    def rowsum(value):
        return jnp.sum(value, axis=1, keepdims=True)

    def to_tp(d):
        return (ph, (tp + d) % 16)

    def to_ph(d):
        return ((ph + d) % 8, tp)

    def exchange(buf, slot, count, number, to):
        def copy(d):
            return remote(buf.at[slot], buf.at[slot], ex_s.at[number], ex_r.at[number, d], to(d))

        def start():
            for d in range(1, count):
                copy(d).start()

        def wait():
            for d in range(1, count):
                copy(d).wait_recv()

        def sent():
            arrive(buf.at[pl.ds(0, count - 1)], ex_s.at[number])

        return start, wait, sent

    early_y = exchange(ex_y0, me["y"], 4, 0, lambda d: near("y", d))
    early_z = exchange(ex_z0, me["z"], 4, 5, lambda d: near("z", d))
    early_ph = exchange(ex_ph0, ph, 8, 1, to_ph)
    late_tp = exchange(ex_tp1, tp, 16, 2, to_tp)
    late_ph = exchange(ex_ph1, ph, 8, 3, to_ph)
    gain_ph = exchange(ex_gain_ph, ph, 8, 4, to_ph)

    def to_columns(rows):
        filled = jnp.concatenate(rows + [jnp.zeros((128 - len(rows), TOKENS), F32)], axis=0)
        return jnp.transpose(filled)

    for i in range(3):
        for p in PARTS:
            p1(p, i).start()
    for p in PARTS:
        p2(p, 0, 0).start()
        p2(p, 0, 1).start()
    raw = s_rows[...].astype(F32)
    raw_squares = rowsum(raw * raw)
    lane_t = lax.broadcasted_iota(jnp.int32, (TOKENS, 128), 1)
    st[...] = jnp.where(lane_t == 0, rowsum(wide * wide), 0.0)
    st[0:SLAB, :] = jnp.where(lane_t[0:SLAB] == 1, raw_squares, st[0:SLAB, :])
    squares = jnp.transpose(st[...])
    ex_y0[me["y"]] = jnp.concatenate(
        [squares[0:1, 128 * i : 128 * i + 128] for i in range(4)]
        + [squares[1:2, 0:128], jnp.zeros((3, 128), F32)],
        axis=0,
    )
    early_y[0]()
    lab[...] = to_columns([labels[...].astype(F32)])
    acc_t[...] = jnp.zeros_like(acc_t)
    for n in (1, 2, 3):
        for p in PARTS:
            a, b, d = ORDER[p]
            arrive(block(p, rel(a, STEP[n]), me[b], me[d], PART_T[p]), r1.at[p, (1, 0, 2)[n - 1]])
            p2(p, n, 0).start()
            p2(p, n, 1).start()
    p3t_send(0)
    early_y[1]()
    ex_z0[me["z"]] = ex_y0[0] + ex_y0[1] + ex_y0[2] + ex_y0[3]
    early_z[0]()
    for p in PARTS:
        sib_t(p, 0, 0).start()
    for i in (0, 1):
        for p in PARTS:
            p2_wait(p, i)
            p2f(p, i).start()
            sib_t(p, i + 1, 0).start()
    early_z[1]()
    early = ex_z0[0] + ex_z0[1] + ex_z0[2] + ex_z0[3]
    ex_ph0[ph] = early
    turned = jnp.transpose(jnp.concatenate([early, jnp.zeros((120, 128), F32)], axis=0))
    own_scale = lax.rsqrt(turned[0:SLAB, 4:5] / DS + NORM_EPSILON)
    scale_s[...] = own_scale
    gain = s_gain[...].astype(F32)
    left = (raw[:, 0:128] * own_scale * gain[0:1]).astype(BF16)
    right = (raw[:, 128:256] * own_scale * gain[1:2]).astype(BF16)
    mine[0:48, :] = left[0:48]
    mine[208:224, :] = left[48:64]
    mine[224:256, :] = right[0:32]
    mine[416:448, :] = right[32:64]
    for i in range(3):
        for p in PARTS:
            p1s(p, i).start()
    for p in PARTS:
        p2f_wait(p, 0)
        p2f_wait(p, 1)
        sib_t(p, 3, 0).start()
    p3t_send(1)
    ws_load.wait()
    ws_push = remote(ws, ws_sib, misc_s.at[0], misc_r.at[0], sib)
    ws_push.start()
    for load in wt_loads:
        load.wait()
    for p in PARTS:
        for i in range(3):
            p1s_wait(p, i)
        for i in range(3):
            p2s(p, i).start()
    consume(0, 0)

    def forward(j):
        for i in (0, 1):
            for p in PARTS:
                p3t_wait(p, j, i)
                p3t(p, j, i + 2).start()
                sib_t(p, j, i + 1).start()

    def opposite(j):
        for p in PARTS:
            p3t_wait(p, j, 2)
            p3t_wait(p, j, 3)
            sib_t(p, j, 3).start()

    forward(0)
    consume(1, 0)
    for p in PARTS:
        for i in range(3):
            p2s_wait(p, i)
        p3s(p, 0).start()
        p3s(p, 1).start()
    p3t_send(2)
    early_ph[0]()
    consume(2, 0)
    consume(3, 0)
    forward(1)
    for i in (0, 1):
        for p in PARTS:
            p3s_wait(p, i)
            p3s(p, i + 2).start()
    p3t_send(3)
    consume(0, 1)
    consume(0, 2)
    opposite(0)
    consume(1, 1)
    early_ph[1]()
    early = ex_ph0[0]
    for i in range(1, 8):
        early = early + ex_ph0[i]
    teacher_scale = lax.rsqrt(jnp.concatenate([early[i : i + 1] for i in range(4)], axis=1) / DT + NORM_EPSILON)
    col[...] = to_columns([teacher_scale])
    for p in PARTS:
        p3s_wait(p, 2)
        p3s_wait(p, 3)
        sib_s(p, c).start()
    consume(1, 2)
    consume(0, 3)
    for p in PARTS:
        arrive(G.at[1 - c, :, :, :, pl.ds(*PART_S[p]), :], sibs_r.at[p])

    def slab(q):
        return pl.ds(pl.multiple_of(q * SLAB, SLAB), SLAB)

    def normed(z, y):
        slabs = []
        for q in range(8):
            ref = G.at[q % 2, q // 2, z, y]
            first = jnp.concatenate([ref[0:48, :], ref[208:224, :]], axis=0)
            second = jnp.concatenate([ref[224:256, :], ref[416:448, :]], axis=0)
            slabs.append(jnp.concatenate([first, second], axis=1))
        return jnp.concatenate(slabs, axis=0)

    def student_dot(z, half):
        t = 4 * z + 2 * half
        lhs = jnp.concatenate([normed(z, 2 * half), normed(z, 2 * half + 1)], axis=1)
        rhs = jnp.concatenate([ws[t], ws[t + 1]], axis=0)
        return jnp.dot(lhs, rhs, preferred_element_type=F32)

    def student_dots(z, _):
        sl[...] += student_dot(z, 0)
        sl[...] += student_dot(z, 1)
        return 0

    def nt_dot(lhs, rhs):
        return lax.dot_general(lhs, rhs, (((1,), (1,)), ((), ())), preferred_element_type=F32)

    eye = (
        lax.broadcasted_iota(jnp.int32, (256, 256), 0) == lax.broadcasted_iota(jnp.int32, (256, 256), 1)
    ).astype(F32).astype(BF16)

    def head_copy(t):
        return pltpu.make_async_copy(head_part.at[t % 2], head_out.at[t], out_sem.at[t % 2])

    lane_c = lax.broadcasted_iota(jnp.int32, (256, 128), 1)

    def turn(z, _):
        for y in range(4):
            turned = nt_dot(eye, normed(z, y)).astype(BF16)
            wt[0, 1, z, y] = turned[0:128]
            wt[1, 1, z, y] = turned[128:256]
        return 0

    def head_layer(z, _):
        for y in range(4):
            t = 4 * z + y
            if y >= 2:
                head_copy(t - 2).wait()
            else:

                @pl.when(z >= 1)
                def _(t=t):
                    head_copy(t - 2).wait()

            turned = jnp.concatenate([wt[0, 1, z, y], wt[1, 1, z, y]], axis=0)
            grad = jnp.dot(turned, g_ref[...], preferred_element_type=F32)
            head_part[t % 2] = grad.astype(BF16)
            head_copy(t).start()
            gain_col[...] = jnp.where(lane_c == t, rowsum(grad * ws[t].astype(F32)), gain_col[...])
        return 0

    sl[...] = student_dot(0, 0)
    sl[...] += student_dot(0, 1)
    forward(2)
    lax.fori_loop(1, 4, student_dots, 0)
    opposite(1)
    lane = lax.broadcasted_iota(jnp.int32, (SLAB, 128), 1)
    vocab_first = ((ph * 16 + tp) * LOCAL_V).astype(F32)

    def label_hit(rows):
        ids = lax.broadcasted_iota(jnp.int32, (SLAB, LOCAL_V), 1).astype(F32) + vocab_first
        return lab[rows, 0:1] == ids

    def pack(columns, first, out):
        for i, column in enumerate(columns):
            out = jnp.where(lane == first + i, column, out)
        return out

    def student_stats(n, _):
        student_slab(2 * n)
        student_slab(2 * n + 1)
        return 0

    def student_slab(q):
        rows = slab(q)
        logits = sl[rows, :]
        top = jnp.max(logits, axis=1, keepdims=True)
        e = jnp.exp(logits - top)
        es[rows, :] = e
        picked = jnp.where(label_hit(rows), logits, 0.0)
        st[rows, :] = pack(
            [top, rowsum(e), rowsum(e * logits), rowsum(picked)], 4, jnp.zeros((SLAB, 128), F32)
        )

    lax.fori_loop(0, 4, student_stats, 0)
    consume(2, 1)
    consume(2, 2)
    forward(3)
    consume(1, 3)
    opposite(2)
    consume(3, 1)
    consume(3, 2)
    opposite(3)
    consume(2, 3)
    products(3, 3, c)
    sib_wait(3, 3)
    products(3, 3, 1 - c)

    def teacher_stats(n, _):
        teacher_slab(2 * n)
        teacher_slab(2 * n + 1)
        return 0

    def teacher_slab(q):
        rows = slab(q)
        logits = acc_t[rows, :] * col[rows, 0:1]
        student = sl[rows, :]
        top = jnp.max(logits, axis=1, keepdims=True)
        e = jnp.exp(logits - top)
        acc_t[rows, :] = e
        st[rows, :] = pack([top, rowsum(e), rowsum(e * (logits - student)), rowsum(e * student)], 0, st[rows, :])

    lax.fori_loop(0, 4, teacher_stats, 0)
    stats = jnp.transpose(st[...])[0:8, :]
    sub = lax.broadcasted_iota(jnp.int32, (8, TOKENS), 0)

    def merge(buf, count):
        t_top, s_top = buf[0, 0:1, :], buf[0, 4:5, :]
        for i in range(1, count):
            t_top = jnp.maximum(t_top, buf[i, 0:1, :])
            s_top = jnp.maximum(s_top, buf[i, 4:5, :])
        total = jnp.zeros((8, TOKENS), F32)
        for i in range(count):
            weight = jnp.where(sub < 4, jnp.exp(buf[i, 0:1, :] - t_top), jnp.exp(buf[i, 4:5, :] - s_top))
            total = total + buf[i] * jnp.where(sub == 7, 1.0, weight)
        return jnp.where(sub == 0, t_top, jnp.where(sub == 4, s_top, total))

    ex_tp1[tp] = stats
    late_tp[0]()
    lax.fori_loop(0, 2, turn, 0)
    late_tp[1]()
    ex_ph1[ph] = merge(ex_tp1, 16)
    late_ph[0]()
    lax.fori_loop(2, 4, turn, 0)
    late_ph[1]()
    late = merge(ex_ph1, 8)
    teacher_top, teacher_total, student_top, student_total = late[0:1], late[1:2], late[4:5], late[5:6]
    picked_all = late[7:8]
    teacher_lse = teacher_top + jnp.log(teacher_total)
    student_lse = student_top + jnp.log(student_total)
    loss = (
        late[2:3] / teacher_total - teacher_lse + student_lse + LABEL_WEIGHT * (student_lse - picked_all)
    )
    inner = (
        (1.0 + LABEL_WEIGHT) * late[6:7] / student_total - late[3:4] / teacher_total - LABEL_WEIGHT * picked_all
    )
    t_factor = jnp.exp(stats[0:1] - teacher_top) / teacher_total
    s_factor = (1.0 + LABEL_WEIGHT) * jnp.exp(stats[4:5] - student_top) / student_total
    col[...] = to_columns([t_factor, s_factor, inner])

    def logit_grad(n, which):
        q = 2 * n + (c if which == 0 else 1 - c)
        rows = slab(q)
        g = (
            es[rows, :] * col[rows, 1:2]
            - acc_t[rows, :] * col[rows, 0:1]
            - LABEL_WEIGHT * label_hit(rows).astype(F32)
        ).astype(BF16)
        g_ref[rows, :] = g
        gp[which, slab(n), :] = g

    for which in (1, 0):

        def grad_step(n, _, which=which):
            logit_grad(2 * n, which)
            logit_grad(2 * n + 1, which)
            return 0

        lax.fori_loop(0, 2, grad_step, 0)
        if which == 1:
            gp_push = remote(gp.at[1], gp_in, misc_s.at[1], misc_r.at[1], sib)
            gp_push.start()
    gain_col[...] = jnp.zeros_like(gain_col)

    def own_first(z, _):
        for y in range(4):
            r = nt_dot(gp[0], ws[4 * z + y])
            for xt in range(4):
                own[xt, z, y, 0:64] = r[xt * 64 : xt * 64 + 64, 0:128]
                own[xt, z, y, 64:128] = r[xt * 64 : xt * 64 + 64, 128:256]
        return 0

    def own_second(z):
        for y in range(4):
            r = nt_dot(gp_in[...], ws_sib[4 * z + y])
            for xt in range(4):
                for h in range(2):
                    at = pl.ds(64 * h, 64)
                    total = own[xt, z, y, at, :] + r[xt * 64 : xt * 64 + 64, 128 * h : 128 * h + 128]
                    own[xt, z, y, at, :] = total
                    wt[xt, 0, z, y, at, 0:128] = total.astype(BF16)

    lax.fori_loop(0, 4, own_first, 0)
    ws_push.wait_recv()
    gp_push.wait_recv()

    def at3(p, one, two, three):
        a, b, d = RS_ORDER[p]
        at = {a: one, b: two, d: three}
        return at["x"], at["z"], at["y"]

    def rest(p, two, three):
        at = {RS_ORDER[p][1]: two, RS_ORDER[p][2]: three}
        return tuple(at[axis] for axis in ("x", "z", "y") if axis in at)

    def stage_ref(p, one, two, three):
        ix, iz, iy = at3(p, one, two, three)
        return wt.at[ix, 0, iz, iy, pl.ds(*RS_PART[p]), pl.ds(0, 128)]

    def own_ref(p, one, two, three):
        ix, iz, iy = at3(p, one, two, three)
        return own.at[ix, iz, iy, pl.ds(*RS_PART[p]), :]

    HOP = (2, 1, -1)
    SUBSET = (2, 1, -1, 0)

    def rs1(p, k, i):
        a, b, d = RS_ORDER[p]
        two = rel(b, SUBSET[k])
        src = stage_ref(p, rel(a, HOP[i]), two, ALL)
        dst = rs_b.at[(i, *rest(p, two, ALL), pl.ds(*RS_PART[p]), ALL)]
        return remote(src, dst, send.at[p, 6], rs_r.at[p, 3 * k + i], near(a, HOP[i]))

    def rs1_wait(p, k, i):
        dst = rs_b.at[(i, *rest(p, rel(RS_ORDER[p][1], SUBSET[k]), ALL), pl.ds(*RS_PART[p]), ALL)]
        arrive(dst, rs_r.at[p, 3 * k + i])

    def rs2(p, i):
        a, b, d = RS_ORDER[p]
        src = stage_ref(p, me[a], rel(b, HOP[i]), ALL)
        dst = rs_c.at[i, :, pl.ds(*RS_PART[p]), :]
        return remote(src, dst, send.at[p, 7], rs_r.at[p, 12 + i], near(b, HOP[i]))

    def rs3(p, i):
        a, b, d = RS_ORDER[p]
        src = stage_ref(p, me[a], me[b], rel(d, HOP[i]))
        dst = rs_d.at[i, pl.ds(*RS_PART[p]), :]
        return remote(src, dst, send.at[p, 8], rs_r.at[p, 15 + i], near(d, HOP[i]))

    for k in range(4):
        own_second(rel("z", SUBSET[k]))
        for i in range(3):
            rs1(0, k, i).start()
            rs1(1, k, i).start()
        if k < 3:
            for m in range(4):
                rs1(2, m, k).start()
    def gain_copy(d):
        to = (tp + d) % 16
        return remote(gain_own.at[to], ex_gain.at[tp], misc_s.at[2], ex_r.at[6, d], (ph, to))

    for k in range(4):
        if k < 3:
            lax.fori_loop((0, 2, 3)[k], (2, 3, 4)[k], head_layer, 0)
        if k == 2:
            turned = jnp.transpose(gain_col[...])
            for t in range(16):
                gain_own[t] = jnp.broadcast_to(turned[t : t + 1], (8, 256))
            ex_gain[tp] = gain_own[tp]
            for d in range(1, 16):
                gain_copy(d).start()
        for p in PARTS:
            rows = pl.ds(*RS_PART[p])
            for i in range(3):
                rs1_wait(p, k, i)

            def add_first(n, _, p=p, k=k, rows=rows):
                two = rel(RS_ORDER[p][1], SUBSET[k])
                ref = own_ref(p, me[RS_ORDER[p][0]], two, n)
                total = ref[...]
                for i in range(3):
                    total = total + rs_b[(i, *rest(p, two, n), rows, ALL)].astype(F32)
                if k == 3:
                    ref[...] = total
                else:
                    stage_ref(p, me[RS_ORDER[p][0]], two, n)[...] = total.astype(BF16)
                return 0

            lax.fori_loop(0, 4, add_first, 0)
            if k < 3:
                rs2(p, k).start()
    for p in PARTS:
        rows = pl.ds(*RS_PART[p])
        for i in range(3):
            arrive(rs_c.at[i, :, rows, :], rs_r.at[p, 12 + i])

        def add_second(n, _, p=p, rows=rows):
            ref = own_ref(p, me[RS_ORDER[p][0]], me[RS_ORDER[p][1]], n)
            total = ref[...]
            for i in range(3):
                total = total + rs_c[i, n, rows, :].astype(F32)
            ref[...] = total
            stage_ref(p, me[RS_ORDER[p][0]], me[RS_ORDER[p][1]], n)[...] = total.astype(BF16)
            return 0

        lax.fori_loop(0, 4, add_second, 0)
        for i in range(3):
            rs3(p, i).start()
    for d in range(1, 16):
        gain_copy(d).wait_recv()
    total = ex_gain[0]
    for i in range(1, 16):
        total = total + ex_gain[i]
    ex_gain_ph[ph] = total
    gain_ph[0]()
    for p in PARTS:
        rows = pl.ds(*RS_PART[p])
        for i in range(3):
            arrive(rs_d.at[i, rows, :], rs_r.at[p, 15 + i])
        total = own_ref(p, *(me[axis] for axis in RS_ORDER[p]))[...]
        for i in range(3):
            total = total + rs_d[i, rows, :].astype(F32)
        fin[rows, :] = total

    rows = slab(ph)
    scale = scale_s[...]
    coefficient = scale * scale * col[rows, 2:3] / DS
    for h in range(2):
        cols = pl.ds(h * 128, 128)
        grad = fin[h * 64 : h * 64 + 64, :]
        rows_out[:, cols] = (scale * gain[h : h + 1] * grad - raw[:, h * 128 : h * 128 + 128] * coefficient).astype(BF16)
    sl[0:8, :] = jnp.broadcast_to(loss, (8, TOKENS))
    window = sl[0:1, pl.ds(pl.multiple_of(me["x"] * 128, 128), 128)]
    loss_out[...] = jnp.where(c == 1, window[:, 64:128], window[:, 0:64])

    for p in PARTS:
        rows = pl.ds(*PART_T[p])
        arrive(G.at[0, 0, 0, 0:3, rows, :], send.at[p, 0])
        arrive(G.at[0, 0:3, 0, :, rows, :], send.at[p, 1])
        arrive(G.at[0, 0:3, :, :, rows, :], send.at[p, 3])
        arrive(G.at[0, :, :, :, rows, :], send.at[p, 4])
        rows = pl.ds(*PART_S[p])
        arrive(G.at[0, 0:3, :, :, rows, :], send.at[p, 2])
        arrive(G.at[0, 0:3, 0:1, :, rows, :], send.at[p, 2])
        arrive(G.at[0, 0, 0, 0:3, rows, :], send.at[p, 2])
        arrive(G.at[0, :, :, :, rows, :], send.at[p, 5])
        rows = pl.ds(*RS_PART[p])
        arrive(rs_b.at[:, :, :, rows, :], send.at[p, 6])
        arrive(rs_c.at[:, :, rows, :], send.at[p, 7])
        arrive(rs_d.at[:, rows, :], send.at[p, 8])
    for ex in (early_y, early_z, early_ph, late_tp, late_ph):
        ex[2]()
    ws_push.wait_send()
    gp_push.wait_send()
    head_copy(14).wait()
    head_copy(15).wait()
    arrive(ex_gain.at[pl.ds(0, 15)], misc_s.at[2])
    gain_ph[1]()
    total = ex_gain_ph[0]
    for i in range(1, 8):
        total = total + ex_gain_ph[i]
    gain_out[...] = total[0:1] / jnp.concatenate([gain[0:1], gain[1:2]], axis=1)
    gain_ph[2]()


def out_kernel(
    head_in, loss_in, rows_in, gain_in, head_out, loss_out, rows_out, gain_out,
    head, loss, rows, gain, in_sem, out_sem,
):
    def part(ref, i):
        return ref.at[pl.ds(1024 * i, 1024)]

    ways = [(part(head_in, i), part(head, i), part(head_out, i)) for i in range(4)]
    ways += [(loss_in, loss, loss_out), (rows_in, rows, rows_out), (gain_in, gain, gain_out)]
    loads = [pltpu.make_async_copy(src, held, in_sem.at[i]) for i, (src, held, _) in enumerate(ways)]
    stores = [pltpu.make_async_copy(held, dst, out_sem.at[i]) for i, (_, held, dst) in enumerate(ways)]
    for load in loads:
        load.start()
    for load, store in zip(loads, stores):
        load.wait()
        store.start()
    for store in stores:
        store.wait()


def local(teacher_rows, teacher_gain, teacher_head, student_rows, student_gain, student_head, labels):
    vmem = pl.BlockSpec(memory_space=pltpu.VMEM)
    hbm = pl.BlockSpec(memory_space=pl.ANY)
    dma = pltpu.SemaphoreType.DMA
    loss, rows_grad, gain_grad, head_grad = pl.pallas_call(
        comm_kernel,
        out_shape=(
            jax.ShapeDtypeStruct((1, SLAB), F32),
            jax.ShapeDtypeStruct((SLAB, 256), BF16),
            jax.ShapeDtypeStruct((1, 256), F32),
            jax.ShapeDtypeStruct((16, 256, LOCAL_V), BF16),
        ),
        in_specs=[vmem, vmem, hbm, vmem, vmem, hbm, vmem],
        out_specs=(vmem, vmem, vmem, hbm),
        scratch_shapes=[
            pltpu.VMEM((2, 4, 4, 4, 640, 128), BF16),
            pltpu.VMEM((4, 2, 4, 4, 128, LOCAL_V), BF16),
            pltpu.VMEM((16, 256, LOCAL_V), BF16),
            pltpu.VMEM((16, 256, LOCAL_V), BF16),
            pltpu.VMEM((2, 256, LOCAL_V), BF16),
            pltpu.VMEM((TOKENS, LOCAL_V), F32),
            pltpu.VMEM((TOKENS, LOCAL_V), F32),
            pltpu.VMEM((TOKENS, LOCAL_V), F32),
            pltpu.VMEM((TOKENS, 128), F32),
            pltpu.VMEM((TOKENS, 128), F32),
            pltpu.VMEM((TOKENS, 128), F32),
            pltpu.VMEM((SLAB, 1), F32),
            pltpu.VMEM((TOKENS, LOCAL_V), BF16),
            pltpu.VMEM((2, 256, LOCAL_V), BF16),
            pltpu.VMEM((256, LOCAL_V), BF16),
            pltpu.VMEM((4, 4, 4, 128, 128), F32),
            pltpu.VMEM((3, 4, 4, 128, 128), BF16),
            pltpu.VMEM((3, 4, 128, 128), BF16),
            pltpu.VMEM((3, 128, 128), BF16),
            pltpu.VMEM((128, 128), F32),
            pltpu.VMEM((4, 8, 128), F32),
            pltpu.VMEM((4, 8, 128), F32),
            pltpu.VMEM((8, 8, 128), F32),
            pltpu.VMEM((16, 8, TOKENS), F32),
            pltpu.VMEM((8, 8, TOKENS), F32),
            pltpu.VMEM((256, 128), F32),
            pltpu.VMEM((16, 8, 256), F32),
            pltpu.VMEM((16, 8, 256), F32),
            pltpu.VMEM((8, 8, 256), F32),
            dma((5,)), dma((2,)), dma((3, 9)),
            dma((3, 3)), dma((3, 2)), dma((3, 2)), dma((3, 3)), dma((3, 3)), dma((3, 4)), dma((3, 16)),
            dma((3,)), dma((3, 16)), dma((6,)), dma((7, 16)), dma((3,)), dma((2,)), dma((3, 18)),
        ],
        compiler_params=pltpu.CompilerParams(
            collective_id=0, has_side_effects=True, vmem_limit_bytes=63 << 20
        ),
        name="distill",
    )(
        teacher_rows,
        teacher_gain.reshape(1, 128),
        teacher_head.reshape(4, 2, 4, 4, 128, LOCAL_V),
        student_rows,
        student_gain.reshape(2, 128),
        student_head.reshape(16, 256, LOCAL_V),
        labels.reshape(1, TOKENS),
    )
    head_grad, loss, rows_grad, gain_grad = pl.pallas_call(
        out_kernel,
        out_shape=(
            jax.ShapeDtypeStruct((DS, LOCAL_V), BF16),
            jax.ShapeDtypeStruct((1, SLAB), F32),
            jax.ShapeDtypeStruct((SLAB, 256), BF16),
            jax.ShapeDtypeStruct((1, 256), F32),
        ),
        in_specs=[hbm, hbm, hbm, hbm],
        out_specs=(hbm, hbm, hbm, hbm),
        scratch_shapes=[
            pltpu.VMEM((DS, LOCAL_V), BF16),
            pltpu.VMEM((1, SLAB), F32),
            pltpu.VMEM((SLAB, 256), BF16),
            pltpu.VMEM((1, 256), F32),
            dma((7,)),
            dma((7,)),
        ],
        compiler_params=pltpu.CompilerParams(vmem_limit_bytes=63 << 20),
        name="outputs",
    )(head_grad.reshape(DS, LOCAL_V), loss, rows_grad, gain_grad)
    return loss.reshape(SLAB), head_grad, rows_grad, gain_grad.reshape(256)


def solution(mesh):
    placed = (
        P(None, ("phase", "tp")),
        P(("phase", "tp")),
        P(None, ("phase", "tp")),
        P("phase", "tp"),
        P("tp"),
        P(None, ("phase", "tp")),
        P(),
    )
    return jax.shard_map(
        local,
        mesh=mesh,
        in_specs=placed,
        out_specs=(P("phase"), P(None, ("phase", "tp")), P("phase", "tp"), P("tp")),
        check_vma=False,
    )
```
